32 devices in a mesh: prompt: 8 (over z, core), comp: 4 (over y, x).
Axes of the slice: x: 2, y: 2, z: 4, core: 2. Of those that a mesh axis runs over, the one named last changes fastest.
Arguments:
- prompt_inner: bfloat16 [2048, 16384], P('prompt', 'comp'), may hold values from -0.59765625 to 0.59765625
- prompt_proj: bfloat16 [2048, 4096], P('prompt'), may hold values from -0.8984375 to 0.8984375
- prompt_step: float32 [256, 2048], P('comp', 'prompt')
- completion_inner: bfloat16 [8, 256, 16384], P('comp', None, 'prompt'), may hold values from -0.59765625 to 0.59765625
- completion_gate: bfloat16 [8, 256, 16384], P('comp', None, 'prompt'), may hold values from -12 to 12
- completion_projections: bfloat16 [8, 256, 4096], P('comp'), may hold values from -0.8984375 to 0.8984375
- sample_step: float32 [256, 8, 256], P('prompt', 'comp')
- sample_length: int32 [8], P('comp'), may hold values from 1 to 256, as said below
- decay_log: float32 [256], replicated
- conv_inner: bfloat16 [4, 16384], replicated, may hold values from -3 to 3
- conv_proj: bfloat16 [4, 4096], replicated, may hold values from -3 to 3
- norm_gain: float32 [16384], P('prompt'), may hold values from 0.5 to 1.5
Outputs:
- sample_out: bfloat16 [8, 256, 16384], P('comp', None, 'prompt')
The draws below stay inside these ranges and needn't reach their ends.
Inputs may be any that keep to these rules, and one draw needn't show every extreme that they name: `sample_length`: some completion slot is full.
All inputs are finite; a program needn't handle non-finite values.
Results may differ from the reference program's by a relative error of at most 0.014.
Values may be sent and summed in bfloat16 or wider, within the bound.
No kernel may reach another device: no remote copies, remote signals or barrier semaphores. Data moves between devices by JAX's collectives and lax.ppermute only.
A program may use at most 128 MiB of HBM per device.

```python
import jax
import jax.numpy as jnp
from jax import lax

STATE_HEADS = 256
HEAD_WIDTH = 64
STATE_WIDTH = 256
STATE_GROUPS = 8
CONV = 4
BLOCK = 128
SAMPLE_POSITIONS = 256
PTOK = 2048
SLOT_TOTAL = 8


def head_rates(key):
    base_key = jax.random.fold_in(key, 11)
    slow_share = 0.5
    slow_pick = jax.random.uniform(jax.random.fold_in(base_key, 1), (STATE_HEADS,), jnp.float32) < slow_share
    slow_rate = jnp.exp(jax.random.uniform(jax.random.fold_in(base_key, 3), (STATE_HEADS,), jnp.float32, jnp.log(0.3), jnp.log(1.2))) / (PTOK + SAMPLE_POSITIONS)
    fast_rate = jnp.exp(jax.random.uniform(jax.random.fold_in(base_key, 4), (STATE_HEADS,), jnp.float32, jnp.log(0.002), jnp.log(0.035)))
    rate_vals = jnp.where(slow_pick, slow_rate, fast_rate)
    step_factor = jnp.exp(jax.random.uniform(jax.random.fold_in(base_key, 2), (STATE_HEADS,), jnp.float32, jnp.log(0.7), jnp.log(1.4)))
    step_mean = 3.0 * jnp.sqrt(rate_vals) * step_factor
    return (jnp.log(rate_vals / step_mean), step_mean)


def unscaled_steps(key, salt, shape):
    _, step_mean = head_rates(key)
    noise_vals = jax.random.truncated_normal(jax.random.fold_in(key, salt), -3.0, 3.0, shape, jnp.float32)
    step_vals = step_mean.reshape((STATE_HEADS,) + (1,) * (len(shape) - 1)) * jnp.exp(0.5 * noise_vals)
    return jnp.log(jnp.expm1(step_vals))


def draw_decay_log(key, part):
    return head_rates(key)[0]


def draw_prompt_step(key, part):
    return unscaled_steps(key, 21, (STATE_HEADS, PTOK))


def draw_sample_step(key, part):
    return unscaled_steps(key, 22, (STATE_HEADS, SLOT_TOTAL, SAMPLE_POSITIONS))


def draw_sample_length(key, part):
    sample_lengths = jax.random.randint(jax.random.fold_in(key, 31), (SLOT_TOTAL,), 1, SAMPLE_POSITIONS + 1)
    whole_slot = jax.random.randint(jax.random.fold_in(key, 32), (), 0, SLOT_TOTAL)
    return jnp.where(jnp.arange(SLOT_TOTAL) == whole_slot, SAMPLE_POSITIONS, sample_lengths).astype(jnp.int32)


def level_of(rng, dims, pieces, low, high):
    level, own = 1.0, jax.random.fold_in(rng, 6)
    for position, shards_of in pieces:
        draws = jnp.exp(jax.random.uniform(jax.random.fold_in(own, position), (shards_of,), jnp.float32, low / len(pieces), high / len(pieces)))
        level = level * jnp.repeat(draws, dims[position] // shards_of).reshape([-1 if axis == position else 1 for axis in range(len(dims))])
    return level


def gaussian(rng, dims, deviation, limit, split=(), held_as=jnp.bfloat16):
    entries = deviation * jax.random.normal(rng, dims, jnp.float32)
    if split:
        entries = entries * level_of(rng, dims, split, -0.22, 0.18)
    return jnp.clip(entries, -limit, limit).astype(held_as)


def setup_inputs(seed: int = 0) -> dict:
    keys = jax.random.split(jax.random.key(seed), 13)
    return {
        "prompt_inner": gaussian(keys[0], (PTOK, STATE_HEADS * HEAD_WIDTH), 0.1, 0.59765625, ((0, 8), (1, 4))),
        "prompt_proj": gaussian(keys[1], (PTOK, 2 * STATE_GROUPS * STATE_WIDTH), 0.15, 0.8984375, ((0, 8),)),
        "prompt_step": draw_prompt_step(jax.random.fold_in(keys[12], 71), 0),
        "completion_inner": gaussian(keys[3], (SLOT_TOTAL, SAMPLE_POSITIONS, STATE_HEADS * HEAD_WIDTH), 0.1, 0.59765625, ((0, 4), (2, 8))),
        "completion_gate": gaussian(keys[4], (SLOT_TOTAL, SAMPLE_POSITIONS, STATE_HEADS * HEAD_WIDTH), 2.0, 12.0, ((0, 4), (2, 8))),
        "completion_projections": gaussian(keys[5], (SLOT_TOTAL, SAMPLE_POSITIONS, 2 * STATE_GROUPS * STATE_WIDTH), 0.15, 0.8984375, ((0, 4),)),
        "sample_step": draw_sample_step(jax.random.fold_in(keys[12], 71), 0),
        "sample_length": draw_sample_length(jax.random.fold_in(keys[12], 71), 0),
        "decay_log": draw_decay_log(jax.random.fold_in(keys[12], 71), 0),
        "conv_inner": gaussian(keys[9], (CONV, STATE_HEADS * HEAD_WIDTH), CONV ** -0.5, 3.0),
        "conv_proj": gaussian(keys[10], (CONV, 2 * STATE_GROUPS * STATE_WIDTH), CONV ** -0.5, 3.0),
        "norm_gain": jnp.clip(1.0 + 0.1 * jax.random.normal(keys[11], (STATE_HEADS * HEAD_WIDTH,), jnp.float32), 0.5, 1.5),
    }


EPS = 1e-05
HIGHEST = lax.Precision.HIGHEST

def causal_conv(source, kernel, leading):
    padded = jnp.concatenate([leading, source], axis=0).astype(jnp.float32)
    kernel_wide = kernel.astype(jnp.float32)
    row_count = source.shape[0]
    summed = jnp.zeros(source.shape, jnp.float32)
    for offset in range(kernel.shape[0]):
        summed = summed + kernel_wide[offset] * padded[offset:offset + row_count]
    return jax.nn.silu(summed).astype(jnp.bfloat16)

def block_exact(state_in, inner_blk, b_blk, c_blk, step_blk, rate_vals):
    cumul = jnp.cumsum(-rate_vals[:, :, None] * step_blk, axis=2)
    scores = jnp.einsum('ign,jgn->gij', c_blk.astype(jnp.float32), b_blk.astype(jnp.float32), precision=HIGHEST)
    spread_log = cumul[:, :, :, None] - cumul[:, :, None, :]
    length_q = step_blk.shape[2]
    causal = jnp.arange(length_q)[:, None] >= jnp.arange(length_q)[None, :]
    decay_mat = jnp.exp(jnp.where(causal, spread_log, -jnp.inf))
    mixer_w = (scores[:, None] * decay_mat * step_blk[:, :, None, :]).astype(jnp.bfloat16)
    intra_part = jnp.einsum('gkij,jgkd->igkd', mixer_w.astype(jnp.float32), inner_blk.astype(jnp.float32), precision=HIGHEST)
    readout = jnp.einsum('ign,gkdn->igkd', c_blk.astype(jnp.float32), state_in, precision=HIGHEST)
    inter_part = jnp.transpose(jnp.exp(cumul), (2, 0, 1))[..., None] * readout
    weights = jnp.exp(cumul[:, :, -1:] - cumul) * step_blk
    packed = (inner_blk.astype(jnp.float32) * jnp.transpose(weights, (2, 0, 1))[..., None]).astype(jnp.bfloat16)
    fresh_part = jnp.einsum('jgn,jgkd->gkdn', b_blk.astype(jnp.float32), packed.astype(jnp.float32), precision=HIGHEST)
    return (intra_part + inter_part, jnp.exp(cumul[:, :, -1])[..., None, None] * state_in + fresh_part)

def reference(prompt_inner, prompt_proj, prompt_step, completion_inner, completion_gate, completion_projections, sample_step, sample_length, decay_log, conv_inner, conv_proj, norm_gain):
    heads_group = STATE_HEADS // STATE_GROUPS
    state_feats = STATE_GROUPS * STATE_WIDTH
    lag_rows = CONV - 1
    rate_all = jnp.exp(decay_log)
    lead_inner = jnp.zeros((lag_rows, STATE_HEADS * HEAD_WIDTH), jnp.bfloat16)
    lead_proj = jnp.zeros((lag_rows, state_feats), jnp.bfloat16)
    prompt_conv = causal_conv(prompt_inner, conv_inner, lead_inner)
    prompt_b = causal_conv(prompt_proj[:, :state_feats], conv_proj[:, :state_feats], lead_proj)
    prompt_dt = jax.nn.softplus(prompt_step)
    prompt_cum = jnp.cumsum(-rate_all[:, None] * prompt_dt, axis=1)
    weight_p = jnp.exp(prompt_cum[:, -1:] - prompt_cum) * prompt_dt
    scaled = prompt_conv.astype(jnp.float32).reshape(PTOK, STATE_HEADS, HEAD_WIDTH) * jnp.transpose(weight_p)[:, :, None]
    scaled = scaled.reshape(PTOK, STATE_GROUPS, heads_group, HEAD_WIDTH)
    b_groups = prompt_b.astype(jnp.float32).reshape(PTOK, STATE_GROUPS, STATE_WIDTH)
    prompt_state = jnp.einsum('tgn,tghd->ghdn', b_groups, scaled, precision=HIGHEST)
    tail_inner = prompt_inner[PTOK - lag_rows:]
    tail_proj = prompt_proj[PTOK - lag_rows:]
    block_count = SAMPLE_POSITIONS // BLOCK
    rate_grid = rate_all.reshape(STATE_GROUPS, heads_group)

    def one_sample(slot_args):
        inner_in, gate_in, proj_in, step_raw, live_len = slot_args
        inner_conv = causal_conv(inner_in, conv_inner, tail_inner)
        proj_conv = causal_conv(proj_in, conv_proj, tail_proj)
        b_blocks = proj_conv[:, :state_feats].reshape(block_count, BLOCK, STATE_GROUPS, STATE_WIDTH)
        c_blocks = proj_conv[:, state_feats:].reshape(block_count, BLOCK, STATE_GROUPS, STATE_WIDTH)
        inner_blocks = inner_conv.reshape(block_count, BLOCK, STATE_GROUPS, heads_group, HEAD_WIDTH)
        step_blocks = jnp.transpose(jax.nn.softplus(step_raw).reshape(STATE_GROUPS, heads_group, block_count, BLOCK), (2, 0, 1, 3))

        def advance(carry, block_in):
            block_out, carry_next = block_exact(carry, block_in[0], block_in[1], block_in[2], block_in[3], rate_grid)
            return (carry_next, block_out)
        _, block_outs = lax.scan(advance, prompt_state, (inner_blocks, b_blocks, c_blocks, step_blocks))
        ssm_out = block_outs.reshape(SAMPLE_POSITIONS, STATE_HEADS * HEAD_WIDTH)
        gated = ssm_out * jax.nn.silu(gate_in.astype(jnp.float32))
        grouped = gated.reshape(SAMPLE_POSITIONS, STATE_GROUPS, heads_group * HEAD_WIDTH)
        mean_square = lax.optimization_barrier(jnp.mean(grouped * grouped, axis=2, keepdims=True))
        result = (grouped * lax.rsqrt(mean_square + EPS)).reshape(SAMPLE_POSITIONS, STATE_HEADS * HEAD_WIDTH) * norm_gain[None, :]
        live_rows = jnp.arange(SAMPLE_POSITIONS) < live_len
        return jnp.where(live_rows[:, None], result, 0.0).astype(jnp.bfloat16)
    return lax.map(one_sample, (completion_inner, completion_gate, completion_projections, jnp.transpose(sample_step, (1, 0, 2)), sample_length))
```

```python
import jax
import jax.numpy as jnp
from jax import lax
from jax.experimental import pallas as pl
from jax.experimental.pallas import tpu as pltpu
from jax.sharding import PartitionSpec as P

STATE_HEADS = 256
HEAD_WIDTH = 64
STATE_WIDTH = 256
STATE_GROUPS = 8
CONV = 4
BLOCK = 128


EPS = 1e-05
HIGHEST = lax.Precision.HIGHEST


def from_behind(block, axis, distance):
    devices = range(lax.axis_size(axis))
    route = [(i - distance, i) for i in devices if i - distance in devices]
    return lax.ppermute(block, axis, route)


def carried_in(array, axis, combine, identity):
    peers, position = (lax.axis_size(axis), lax.axis_index(axis))
    everything = jax.tree.map(
        lambda part, kind: lax.all_gather(part.astype(kind), axis),
        array,
        (jnp.bfloat16, jnp.bfloat16),
    )
    start = jax.tree.map(
        lambda part, zero: jnp.broadcast_to(jnp.asarray(zero, part.dtype), part.shape),
        array,
        identity,
    )

    def hop(k, before):
        reached = k < position
        new = combine(
            before, jax.tree.map(lambda part, own: part[k].astype(own.dtype), everything, array)
        )
        return jax.tree.map(lambda a, b: jnp.where(reached, a, b), new, before)

    return lax.fori_loop(0, peers, hop, start)


def from_root(array, axis, root):
    mine = lax.axis_index(axis) == root
    return lax.psum(jnp.where(mine, array, jnp.zeros_like(array)), axis)


def from_partner(block, axis, stride):
    count = lax.axis_size(axis)
    route = []
    for low in range(count):
        high = low | 1 << stride
        if high != low and high < count:
            route += [(low, high), (high, low)]
    return lax.ppermute(block, axis, route)


def causal_conv(source, kernel, leading):
    padded = jnp.concatenate([leading, source], axis=0).astype(jnp.float32)
    kernel_wide = kernel.astype(jnp.float32)
    row_count = source.shape[0]
    summed = jnp.zeros(source.shape, jnp.float32)
    for offset in range(kernel.shape[0]):
        summed = summed + kernel_wide[offset] * padded[offset : offset + row_count]
    return jax.nn.silu(summed).astype(jnp.bfloat16)


def block_scan(state_in, inner_blk, b_blk, c_blk, step_blk, rate_vals):
    cumul = jnp.cumsum(-rate_vals[:, :, None] * step_blk, axis=2)
    scores = jnp.einsum("ign,jgn->gij", c_blk, b_blk, preferred_element_type=jnp.float32)
    spread_log = cumul[:, :, :, None] - cumul[:, :, None, :]
    length_q = step_blk.shape[2]
    causal = jnp.arange(length_q)[:, None] >= jnp.arange(length_q)[None, :]
    decay_mat = jnp.exp(jnp.where(causal, spread_log, -jnp.inf))
    mixer_w = (scores[:, None] * decay_mat * step_blk[:, :, None, :]).astype(jnp.bfloat16)
    intra_part = jnp.einsum(
        "gkij,jgkd->igkd", mixer_w, inner_blk, preferred_element_type=jnp.float32
    )
    readout = jnp.einsum("ign,gkdn->igkd", c_blk.astype(jnp.float32), state_in, precision=HIGHEST)
    inter_part = jnp.transpose(jnp.exp(cumul), (2, 0, 1))[..., None] * readout
    weights = jnp.exp(cumul[:, :, -1:] - cumul) * step_blk
    packed = (inner_blk.astype(jnp.float32) * jnp.transpose(weights, (2, 0, 1))[..., None]).astype(
        jnp.bfloat16
    )
    fresh_part = jnp.einsum("jgn,jgkd->gkdn", b_blk, packed, preferred_element_type=jnp.float32)
    return (
        intra_part + inter_part,
        jnp.exp(cumul[:, :, -1])[..., None, None] * state_in + fresh_part,
    )


def any_shape(
    prompt_inner,
    prompt_proj,
    prompt_step,
    completion_inner,
    completion_gate,
    completion_projections,
    sample_step,
    sample_length,
    decay_log,
    conv_inner,
    conv_proj,
    norm_gain,
):
    prompt_count = lax.axis_size("prompt")
    prompt_idx = lax.axis_index("prompt")
    column_idx = lax.axis_index("comp")
    heads_group = STATE_HEADS // STATE_GROUPS
    heads_col = prompt_step.shape[0]
    heads_row = sample_step.shape[0]
    state_feats = STATE_GROUPS * STATE_WIDTH
    lag_rows = CONV - 1
    rows_prompt = prompt_inner.shape[0]
    prev_inner, prev_proj = from_behind(
        (
            prompt_inner[rows_prompt - lag_rows :],
            prompt_proj[rows_prompt - lag_rows :, :state_feats],
        ),
        "prompt",
        1,
    )
    col_start = column_idx * heads_col
    conv_col = lax.dynamic_slice_in_dim(
        conv_inner, col_start * HEAD_WIDTH, heads_col * HEAD_WIDTH, 1
    )
    inner_conv = causal_conv(prompt_inner, conv_col, prev_inner)
    b_conv = causal_conv(prompt_proj[:, :state_feats], conv_proj[:, :state_feats], prev_proj)
    rate_col = jnp.exp(lax.dynamic_slice_in_dim(decay_log, col_start, heads_col, 0))
    step_col = jax.nn.softplus(prompt_step)
    cumul = jnp.cumsum(-rate_col[:, None] * step_col, axis=1)
    local_log = cumul[:, -1]
    weight_col = jnp.exp(local_log[:, None] - cumul) * step_col
    group_span = max(1, heads_col // heads_group)
    per_group = heads_col // group_span
    group_start = col_start // heads_group
    b_select = lax.dynamic_slice_in_dim(
        b_conv.reshape(rows_prompt, STATE_GROUPS, STATE_WIDTH), group_start, group_span, 1
    ).astype(jnp.float32)
    scaled = (
        inner_conv.astype(jnp.float32).reshape(rows_prompt, heads_col, HEAD_WIDTH)
        * jnp.transpose(weight_col)[:, :, None]
    )
    scaled = scaled.reshape(rows_prompt, group_span, per_group, HEAD_WIDTH)
    local_state = jnp.einsum("tgn,tghd->ghdn", b_select, scaled, precision=HIGHEST).reshape(
        heads_col, HEAD_WIDTH, STATE_WIDTH
    )
    own_inner = prompt_inner[rows_prompt - lag_rows :].astype(jnp.float32)
    own_proj = prompt_proj[rows_prompt - lag_rows :].astype(jnp.float32)
    last_index = prompt_count - 1
    head_start = prompt_idx * heads_row
    owner = head_start // heads_col
    head_offset = head_start - owner * heads_col

    def combine(earlier, later):
        return (earlier[0] + later[0], earlier[1] * jnp.exp(later[0])[:, None, None] + later[1])

    before = carried_in(
        (local_log, local_state),
        "prompt",
        combine,
        (jnp.zeros_like(local_log), jnp.zeros_like(local_state)),
    )
    through = combine(before, (local_log, local_state))[1]
    final_state, tail_inner, tail_proj = (
        from_root(through.astype(jnp.bfloat16), "prompt", last_index).astype(through.dtype),
        from_root(own_inner.astype(jnp.bfloat16), "prompt", last_index).astype(own_inner.dtype),
        from_root(own_proj.astype(jnp.bfloat16), "prompt", last_index).astype(own_proj.dtype),
    )
    moved_state, moved_inner = (
        from_root(final_state.astype(jnp.bfloat16), "comp", owner).astype(final_state.dtype),
        from_root(tail_inner.astype(jnp.bfloat16), "comp", owner).astype(tail_inner.dtype),
    )
    start_state = lax.dynamic_slice_in_dim(moved_state, head_offset, heads_row, 0)
    lead_inner = lax.dynamic_slice_in_dim(
        moved_inner, head_offset * HEAD_WIDTH, heads_row * HEAD_WIDTH, 1
    ).astype(jnp.bfloat16)
    group_row = head_start // heads_group
    b_start = group_row * STATE_WIDTH
    c_start = state_feats + group_row * STATE_WIDTH
    proj_select = jnp.concatenate(
        [
            lax.dynamic_slice_in_dim(completion_projections, b_start, STATE_WIDTH, 2),
            lax.dynamic_slice_in_dim(completion_projections, c_start, STATE_WIDTH, 2),
        ],
        axis=2,
    )
    kernel_select = jnp.concatenate(
        [
            lax.dynamic_slice_in_dim(conv_proj, b_start, STATE_WIDTH, 1),
            lax.dynamic_slice_in_dim(conv_proj, c_start, STATE_WIDTH, 1),
        ],
        axis=1,
    )
    lead_wide = tail_proj.astype(jnp.bfloat16)
    lead_select = jnp.concatenate(
        [
            lax.dynamic_slice_in_dim(lead_wide, b_start, STATE_WIDTH, 1),
            lax.dynamic_slice_in_dim(lead_wide, c_start, STATE_WIDTH, 1),
        ],
        axis=1,
    )
    conv_row = lax.dynamic_slice_in_dim(
        conv_inner, head_start * HEAD_WIDTH, heads_row * HEAD_WIDTH, 1
    )
    rate_row = jnp.exp(lax.dynamic_slice_in_dim(decay_log, head_start, heads_row, 0))
    step_row = jax.nn.softplus(sample_step)
    slot_count = completion_inner.shape[0]
    sample_len = completion_inner.shape[1]
    block_count = sample_len // BLOCK

    def advance(carry, block_in):
        block_out, carry_next = block_scan(
            carry, block_in[0], block_in[1], block_in[2], block_in[3], rate_row[None]
        )
        return (carry_next, block_out)

    gated_list = []
    square_list = []
    for slot in range(slot_count):
        slot_conv = causal_conv(completion_inner[slot], conv_row, lead_inner)
        proj_conv = causal_conv(proj_select[slot], kernel_select, lead_select)
        inner_blocks = slot_conv.reshape(block_count, BLOCK, 1, heads_row, HEAD_WIDTH)
        b_blocks = proj_conv[:, :STATE_WIDTH].reshape(block_count, BLOCK, 1, STATE_WIDTH)
        c_blocks = proj_conv[:, STATE_WIDTH:].reshape(block_count, BLOCK, 1, STATE_WIDTH)
        step_blocks = jnp.transpose(
            step_row[:, slot].reshape(heads_row, block_count, BLOCK), (1, 0, 2)
        )[:, None]
        block_inputs = (inner_blocks, b_blocks, c_blocks, step_blocks)
        _, block_outs = lax.scan(advance, start_state[None], block_inputs)
        ssm_out = block_outs.reshape(sample_len, heads_row * HEAD_WIDTH)
        gated = ssm_out * jax.nn.silu(completion_gate[slot].astype(jnp.float32))
        gated_list.append(gated)
        square_list.append(jnp.sum(gated * gated, axis=1))
    square_all = jnp.stack(square_list)
    partner_bits = (prompt_count // STATE_GROUPS).bit_length() - 1
    for bit_number in range(partner_bits):
        square_all = square_all + from_partner(square_all, "prompt", bit_number)
    scale_all = lax.rsqrt(square_all / (heads_group * HEAD_WIDTH) + EPS)
    gated_all = jnp.stack(gated_list)
    result = gated_all * scale_all[:, :, None] * norm_gain[None, None, :]
    live_rows = jnp.arange(sample_len)[None, :] < sample_length[:, None]
    return jnp.where(live_rows[:, :, None], result, 0.0).astype(jnp.bfloat16)


LOG2E = 1.4426950408889634
AXES = ("prompt", "comp")
CHUNKS = 2
TAIL = 16
VMEM_BYTES = 48 * 1024 * 1024


def routed(block, route):
    columns = lax.axis_size("comp")
    pairs = []
    for row in range(lax.axis_size("prompt")):
        for column in range(columns):
            target = route(row // 2, row % 2, column)
            if target is not None:
                plane, core, to = target
                pairs.append((row * columns + column, (2 * plane + core) * columns + to))
    return lax.ppermute(block, AXES, pairs)


def half_silu(value):
    return 0.5 * value * (1.0 + jnp.tanh(0.5 * value))


def conv_rows(padded, taps, lead, block):
    rows = block.shape[0]
    width = block.shape[1]
    padded[0:8, 0:width] = lead.astype(jnp.float32)[TAIL - 8 :]
    padded[8 : 8 + rows, 0:width] = block.astype(jnp.float32)
    wide = taps.astype(jnp.float32)
    total = wide[0:1] * padded[5 : 5 + rows, 0:width]
    for tap in range(1, CONV):
        total = total + wide[tap : tap + 1] * padded[5 + tap : 5 + tap + rows, 0:width]
    return half_silu(total)


def spread_heads(first, heads, width):
    row = lax.broadcasted_iota(jnp.int32, (heads, width), 0)
    col = lax.broadcasted_iota(jnp.int32, (heads, width), 1)
    return row == first + col // HEAD_WIDTH


def contract(lhs, rhs, dims, precision=None):
    return lax.dot_general(
        lhs, rhs, (dims, ((), ())), preferred_element_type=jnp.float32, precision=precision
    )


def softplus(value):
    return jnp.maximum(value, 0.0) + jnp.log1p(jnp.exp(-jnp.abs(value)))


def prompt_weights_kernel(
    place, own_b, other_b, halo_b, taps, own_step, other_step, decay, w_out, b_out, log_out, padded
):
    core = place[2]
    rows, heads = own_b.shape[0], own_step.shape[0]
    first_own = core == 0
    rate = jnp.exp(decay[...])
    dt_own, dt_other = softplus(own_step[...]), softplus(other_step[...])
    row = lax.broadcasted_iota(jnp.int32, (rows, rows), 0)
    col = lax.broadcasted_iota(jnp.int32, (rows, rows), 1)
    later = (col > row).astype(jnp.float32)
    same = (col == row).astype(jnp.float32)
    ones = jnp.ones((8, rows), jnp.float32)
    last = ((1,), (1,))
    sum_own = contract(ones, dt_own, last, HIGHEST)[0:1]
    sum_other = contract(ones, dt_other, last, HIGHEST)[0:1]
    after_own = contract(later, dt_own, last, HIGHEST) + jnp.where(first_own, sum_other, 0.0)
    after_other = contract(later, dt_other, last, HIGHEST) + jnp.where(first_own, 0.0, sum_own)
    w_out[0:rows] = jnp.exp(-rate * after_own) * contract(same, dt_own, last, HIGHEST)
    w_out[rows:] = jnp.exp(-rate * after_other) * contract(same, dt_other, last, HIGHEST)
    total = jnp.broadcast_to(-rate * (sum_own + sum_other), (8, heads))
    spread = spread_heads(0, heads, heads * HEAD_WIDTH).astype(jnp.float32)
    wide = contract(total, spread, ((1,), (0,)), HIGHEST)
    high = wide.astype(jnp.bfloat16)
    rest = wide - high.astype(jnp.float32)
    mid = rest.astype(jnp.bfloat16)
    low = (rest - mid.astype(jnp.float32)).astype(jnp.bfloat16)
    which = lax.broadcasted_iota(jnp.int32, wide.shape, 0)
    parts = jnp.where(
        which == 0,
        high.astype(jnp.float32),
        jnp.where(which == 1, mid.astype(jnp.float32), jnp.where(which == 2, low.astype(jnp.float32), 0.0)),
    )
    log_out[...] = jnp.concatenate([parts, jnp.zeros_like(parts)], axis=0).astype(jnp.bfloat16)
    own_last, other_last, halo = own_b[rows - TAIL :], other_b[rows - TAIL :], halo_b[...]
    lead_own = jnp.where(first_own, halo.astype(jnp.float32), other_last.astype(jnp.float32))
    lead_other = jnp.where(first_own, own_last.astype(jnp.float32), halo.astype(jnp.float32))
    conv_own = conv_rows(padded, taps[...], lead_own, own_b[...])
    b_out[:, 0:rows] = jnp.transpose(conv_own).astype(jnp.bfloat16)
    conv_other = conv_rows(padded, taps[...], lead_other, other_b[...])
    b_out[:, rows:] = jnp.transpose(conv_other).astype(jnp.bfloat16)


def prompt_state_kernel(
    chunk, parts, place, own, other, halo, taps, weights, b_turned, logs, *rest
):
    outs, padded = rest[:parts], rest[parts]
    column, core = place[1], place[2]
    first_own = core == 0
    rows = own.shape[0]
    width = outs[0].shape[1]
    part_width = own.shape[1] // parts
    heads = weights.shape[1]
    state = b_turned.shape[0]
    w = weights[...].astype(jnp.bfloat16)
    for step in range(parts):
        part = column ^ step
        start = part * part_width + chunk * width
        cols = pl.ds(pl.multiple_of(start, width), width)
        spread = spread_heads(start // HEAD_WIDTH, heads, width).astype(jnp.bfloat16)
        w_wide = contract(w, spread, ((1,), (0,)))
        own_x, other_x, halo_x = own[:, cols], other[:, cols], halo[:, cols]
        own_last, other_last = own_x[rows - TAIL :], other_x[rows - TAIL :]
        lead_own = jnp.where(first_own, halo_x.astype(jnp.float32), other_last.astype(jnp.float32))
        lead_other = jnp.where(first_own, own_last.astype(jnp.float32), halo_x.astype(jnp.float32))
        x_own = conv_rows(padded, taps[:, cols], lead_own, own_x) * w_wide[0:rows]
        x_other = conv_rows(padded, taps[:, cols], lead_other, other_x) * w_wide[rows:]
        mine = contract(b_turned[:, 0:rows], x_own.astype(jnp.bfloat16), ((1,), (0,)))
        theirs = contract(b_turned[:, rows:], x_other.astype(jnp.bfloat16), ((1,), (0,)))
        outs[step][0:state] = (mine + theirs).astype(jnp.bfloat16)
        outs[step][state:] = logs[:, cols]


def join_state_kernel(place, *refs):
    arrived, out = refs[:-1], refs[-1]
    plane = place[0]
    state = out.shape[0]
    totals = []
    for ref in arrived:
        rows = ref[state:].astype(jnp.float32)
        totals.append(rows[0:1] + rows[1:2] + rows[2:3])
    joined = None
    for step, ref in enumerate(arrived):
        after = jnp.zeros_like(totals[0])
        for other in range(len(arrived)):
            if other != step:
                after = after + jnp.where((plane ^ other) > (plane ^ step), totals[other], 0.0)
        term = jnp.exp(after) * ref[0:state].astype(jnp.float32)
        joined = term if joined is None else joined + term
    out[...] = joined.astype(jnp.bfloat16)


def completion_kernel(
    place, inner, gate, b_in, c_in, lead, lead_b, lead_c, taps, taps_b, taps_c, step,
    decay_row, decay_col, fixed_out, factor_out, c_out, padded, diag_low, rows_high,
):
    rows = inner.shape[1]
    width = inner.shape[2]
    heads = step.shape[1]
    half = rows // 2

    @pl.when(pl.program_id(1) == 0)
    def _():
        b = conv_rows(padded, taps_b[...], lead_b[...], b_in[0]).astype(jnp.bfloat16)
        c = conv_rows(padded, taps_c[...], lead_c[...], c_in[0]).astype(jnp.bfloat16)
        c_out[0] = c
        scores = contract(c, b, ((1,), (1,)))
        row = lax.broadcasted_iota(jnp.int32, (rows, rows), 0)
        col = lax.broadcasted_iota(jnp.int32, (rows, rows), 1)
        scores = jnp.where(row >= col, scores, 0.0)
        diag_low[...] = scores[0:half, 0:half]
        rows_high[...] = scores[half:]

    x = conv_rows(padded, taps[...], lead[...], inner[0])
    x = x.astype(jnp.bfloat16)
    dt = softplus(step[0])
    row = lax.broadcasted_iota(jnp.int32, (rows, rows), 0)
    col = lax.broadcasted_iota(jnp.int32, (rows, rows), 1)
    upto = (col <= row).astype(jnp.float32)
    before = (row <= col).astype(jnp.float32)
    cum_col = contract(upto, dt, ((1,), (1,)), HIGHEST) * (-LOG2E * jnp.exp(decay_row[0]))
    cum_row = contract(dt, before, ((1,), (0,)), HIGHEST) * (-LOG2E * jnp.exp(decay_col[...]))
    log_dt = jnp.log(dt) * LOG2E
    base_row = cum_row - log_dt
    silu_gate = half_silu(gate[0].astype(jnp.float32))
    spread = spread_heads(0, heads, width).astype(jnp.bfloat16)
    decay_wide = contract(jnp.exp2(cum_col).astype(jnp.bfloat16), spread, ((1,), (0,)))
    factor_out[0] = (decay_wide * silu_gate).astype(jnp.bfloat16)
    low, high = diag_low[...], rows_high[...]
    pair = 2 * HEAD_WIDTH
    lane = lax.broadcasted_iota(jnp.int32, (rows, pair), 1)
    for first in range(0, heads, 2):
        at = first * HEAD_WIDTH
        x_pair = x[:, at : at + pair]
        zero = jnp.zeros_like(x_pair)
        left = jnp.where(lane < HEAD_WIDTH, x_pair, zero)
        right = jnp.where(lane < HEAD_WIDTH, zero, x_pair)
        lows, highs = [], []
        for h in (first, first + 1):
            cc = cum_col[:, h : h + 1]
            rr, ll = base_row[h : h + 1], log_dt[h : h + 1]
            grown = jnp.minimum(cc[0:half] - rr[:, 0:half], ll[:, 0:half])
            lows.append((low * jnp.exp2(grown)).astype(jnp.bfloat16))
            grown = jnp.minimum(cc[half:] - rr, ll)
            highs.append((high * jnp.exp2(grown)).astype(jnp.bfloat16))
        y_low = contract(
            jnp.concatenate(lows, axis=1),
            jnp.concatenate([left[0:half], right[0:half]], axis=0),
            ((1,), (0,)),
        )
        y_high = contract(
            jnp.concatenate(highs, axis=1), jnp.concatenate([left, right], axis=0), ((1,), (0,))
        )
        fixed_out[0, 0:half, at : at + pair] = (
            y_low * silu_gate[0:half, at : at + pair]
        ).astype(jnp.bfloat16)
        fixed_out[0, half:, at : at + pair] = (
            y_high * silu_gate[half:, at : at + pair]
        ).astype(jnp.bfloat16)


def finish_kernel(parts, chunks, place, live, c_ref, fixed, factor, gain, *refs):
    states, out, gated = refs[: parts * chunks], refs[-2], refs[-1]
    column = place[1]
    slot = pl.program_id(0)
    rows, features = out.shape[1], out.shape[2]
    width = states[0].shape[1]
    part_width = features // parts
    c = c_ref[0]
    squares = jnp.zeros((rows, 1), jnp.float32)
    for chunk in range(chunks):
        for step in range(parts):
            start = (column ^ step) * part_width + chunk * width
            cols = pl.ds(pl.multiple_of(start, width), width)
            read = contract(c, states[chunk * parts + step][...], ((1,), (0,)))
            value = fixed[0, :, cols].astype(jnp.float32) + read * factor[0, :, cols].astype(
                jnp.float32
            )
            gated[:, cols] = value
            squares = squares + jnp.sum(value * value, axis=1, keepdims=True)
    scale = lax.rsqrt(squares / features + EPS)
    alive = lax.broadcasted_iota(jnp.int32, (rows, 1), 0) < live[slot]
    scale = jnp.where(alive, scale, 0.0)
    out[0] = (gated[...] * scale * gain[...]).astype(jnp.bfloat16)


def run(kernel, name, place, out_shape, in_specs, out_specs, operands, grid=(1,), scratch=(), scalars=1):
    return pl.pallas_call(
        kernel,
        out_shape=out_shape,
        grid_spec=pltpu.PrefetchScalarGridSpec(
            num_scalar_prefetch=scalars,
            grid=grid,
            in_specs=in_specs,
            out_specs=out_specs,
            scratch_shapes=scratch,
        ),
        compiler_params=pltpu.CompilerParams(
            dimension_semantics=("arbitrary",) * len(grid), vmem_limit_bytes=VMEM_BYTES
        ),
        name=name,
    )(*place, *operands)


def matched(
    prompt_inner,
    prompt_proj,
    prompt_step,
    completion_inner,
    completion_gate,
    completion_projections,
    sample_step,
    sample_length,
    decay_log,
    conv_inner,
    conv_proj,
    norm_gain,
):
    parts = lax.axis_size("comp")
    row, column = lax.axis_index("prompt"), lax.axis_index("comp")
    plane, core = row // 2, row % 2
    group = 2 * column + core
    rows = prompt_inner.shape[0]
    heads = sample_step.shape[0]
    features = heads * HEAD_WIDTH
    place = jnp.stack([plane, column, core, row]).astype(jnp.int32)
    bf16, f32 = jnp.bfloat16, jnp.float32

    def take(array, start, size, axis):
        return lax.dynamic_slice_in_dim(array, start, size, axis)

    swap = lambda z, k, c: (z, 1 - k, c)
    other_inner = routed(take(prompt_inner, (1 - core) * features, features, 1), swap)
    other_b = routed(take(prompt_proj, (2 * column + 1 - core) * STATE_WIDTH, STATE_WIDTH, 1), swap)
    other_step = routed(take(prompt_step, (1 - core) * heads, heads, 0), swap)
    own_step = take(prompt_step, core * heads, heads, 0)

    last_inner, last_proj = prompt_inner[rows - TAIL :], prompt_proj[rows - TAIL :]
    planes = lax.axis_size("prompt") // 2
    halo, tail = None, None
    for to in range(2):
        inner_to = last_inner[:, to * features : (to + 1) * features]
        b_to = take(last_proj, (2 * column + to) * STATE_WIDTH, STATE_WIDTH, 1)
        c_to = take(last_proj, (STATE_GROUPS + 2 * column + to) * STATE_WIDTH, STATE_WIDTH, 1)
        near = routed(
            jnp.concatenate([inner_to, b_to], axis=1),
            lambda z, k, c: (z + 1, to, c) if k == 1 and z + 1 < planes else None,
        )
        far = routed(
            jnp.concatenate([inner_to, b_to, c_to], axis=1),
            lambda z, k, c: (c, to, c) if k == 1 and z + 1 == planes else None,
        )
        halo = near if halo is None else halo + near
        tail = far if tail is None else tail + far
    first_tail = tail
    for step in range(1, parts):
        tail = tail + routed(first_tail, lambda z, k, c: (z, k, z ^ step) if c == z else None)

    whole = lambda shape: pl.BlockSpec(shape, lambda *_: (0,) * len(shape))
    decay_group = take(decay_log, group * heads, heads, 0)[None]
    weights, b_turned, logs = run(
        prompt_weights_kernel,
        "prompt_weights",
        (place,),
        (
            jax.ShapeDtypeStruct((2 * rows, heads), f32),
            jax.ShapeDtypeStruct((STATE_WIDTH, 2 * rows), bf16),
            jax.ShapeDtypeStruct((TAIL, features), bf16),
        ),
        [
            pl.BlockSpec((rows, STATE_WIDTH), lambda i, s: (0, 2 * s[1] + s[2])),
            whole((rows, STATE_WIDTH)),
            pl.BlockSpec((TAIL, STATE_WIDTH), lambda i, s: (0, features // STATE_WIDTH)),
            pl.BlockSpec((CONV, STATE_WIDTH), lambda i, s: (0, 2 * s[1] + s[2])),
            whole((heads, rows)),
            whole((heads, rows)),
            whole((1, heads)),
        ],
        (whole((2 * rows, heads)), whole((STATE_WIDTH, 2 * rows)), whole((TAIL, features))),
        (prompt_proj, other_b, halo, conv_proj, own_step, other_step, decay_group),
        scratch=[pltpu.VMEM((rows + 8, STATE_WIDTH), f32)],
    )
    width = features // parts // CHUNKS
    message = jax.ShapeDtypeStruct((STATE_WIDTH + TAIL, width), bf16)
    joined = []
    for chunk in range(CHUNKS):
        sent = run(
            lambda *refs, chunk=chunk: prompt_state_kernel(chunk, parts, *refs),
            "prompt_state",
            (place,),
            (message,) * parts,
            [
                pl.BlockSpec((rows, features), lambda i, s: (0, s[2])),
                whole((rows, features)),
                pl.BlockSpec((TAIL, features), lambda i, s: (0, 0)),
                pl.BlockSpec((CONV, features), lambda i, s: (0, 2 * s[1] + s[2])),
                whole((2 * rows, heads)),
                whole((STATE_WIDTH, 2 * rows)),
                whole((TAIL, features)),
            ],
            (whole(message.shape),) * parts,
            (prompt_inner, other_inner, halo, conv_inner, weights, b_turned, logs),
            scratch=[pltpu.VMEM((rows + 8, width), f32)],
        )
        held = [sent[0]] + [
            routed(sent[step], lambda z, k, c: (z, k, c ^ step)) for step in range(1, parts)
        ]
        ready = [lax.select_n(column ^ plane ^ step, *held) for step in range(parts)]
        arrived = [ready[0]] + [
            routed(ready[step], lambda z, k, c: (z ^ step, k, c)) for step in range(1, parts)
        ]
        state = run(
            join_state_kernel,
            "join_state",
            (place,),
            jax.ShapeDtypeStruct((STATE_WIDTH, width), bf16),
            [whole(message.shape)] * parts,
            whole((STATE_WIDTH, width)),
            arrived,
        )
        joined += [state] + [
            routed(state, lambda z, k, c: (z, k, c ^ step)) for step in range(1, parts)
        ]

    slots, positions = completion_inner.shape[:2]
    block_heads = 8
    block = block_heads * HEAD_WIDTH
    blocks = heads // block_heads
    decay_own = take(decay_log, row * heads, heads, 0)
    cols_at = features // block
    c_at = STATE_GROUPS
    fixed, factor, c_rows = run(
        completion_kernel,
        "completion_blocks",
        (place,),
        (
            jax.ShapeDtypeStruct((slots, positions, features), bf16),
            jax.ShapeDtypeStruct((slots, positions, features), bf16),
            jax.ShapeDtypeStruct((slots, positions, STATE_WIDTH), bf16),
        ),
        [
            pl.BlockSpec((1, positions, block), lambda i, j, s: (i, 0, j)),
            pl.BlockSpec((1, positions, block), lambda i, j, s: (i, 0, j)),
            pl.BlockSpec((1, positions, STATE_WIDTH), lambda i, j, s: (i, 0, s[3])),
            pl.BlockSpec((1, positions, STATE_WIDTH), lambda i, j, s: (i, 0, c_at + s[3])),
            pl.BlockSpec((TAIL, block), lambda i, j, s: (0, j)),
            pl.BlockSpec((TAIL, STATE_WIDTH), lambda i, j, s: (0, features // STATE_WIDTH)),
            pl.BlockSpec((TAIL, STATE_WIDTH), lambda i, j, s: (0, features // STATE_WIDTH + 1)),
            pl.BlockSpec((CONV, block), lambda i, j, s: (0, s[3] * cols_at + j)),
            pl.BlockSpec((CONV, STATE_WIDTH), lambda i, j, s: (0, s[3])),
            pl.BlockSpec((CONV, STATE_WIDTH), lambda i, j, s: (0, c_at + s[3])),
            pl.BlockSpec((1, block_heads, positions), lambda i, j, s: (i, j, 0)),
            pl.BlockSpec((1, 1, block_heads), lambda i, j, s: (j, 0, 0)),
            pl.BlockSpec((block_heads, 1), lambda i, j, s: (j, 0)),
        ],
        (
            pl.BlockSpec((1, positions, block), lambda i, j, s: (i, 0, j)),
            pl.BlockSpec((1, positions, block), lambda i, j, s: (i, 0, j)),
            pl.BlockSpec((1, positions, STATE_WIDTH), lambda i, j, s: (i, 0, 0)),
        ),
        (
            completion_inner,
            completion_gate,
            completion_projections,
            completion_projections,
            tail,
            tail,
            tail,
            conv_inner,
            conv_proj,
            conv_proj,
            jnp.transpose(sample_step, (1, 0, 2)),
            decay_own.reshape(blocks, 1, block_heads),
            decay_own[:, None],
        ),
        grid=(slots, blocks),
        scratch=[
            pltpu.VMEM((positions + 8, block), f32),
            pltpu.VMEM((positions // 2, positions // 2), f32),
            pltpu.VMEM((positions // 2, positions), f32),
        ],
    )
    return run(
        lambda *refs: finish_kernel(parts, CHUNKS, *refs),
        "finish",
        (place, sample_length),
        jax.ShapeDtypeStruct((slots, positions, features), bf16),
        [
            pl.BlockSpec((1, positions, STATE_WIDTH), lambda i, s, n: (i, 0, 0)),
            pl.BlockSpec((1, positions, features), lambda i, s, n: (i, 0, 0)),
            pl.BlockSpec((1, positions, features), lambda i, s, n: (i, 0, 0)),
            whole((1, features)),
        ]
        + [whole((STATE_WIDTH, width))] * (parts * CHUNKS),
        pl.BlockSpec((1, positions, features), lambda i, s, n: (i, 0, 0)),
        [c_rows, fixed, factor, norm_gain[None]] + joined,
        grid=(slots,),
        scratch=[pltpu.VMEM((positions, features), f32)],
        scalars=2,
    )


def local(*arrays):
    columns, prompts = lax.axis_size("comp"), lax.axis_size("prompt")
    heads_col, heads_row = arrays[2].shape[0], arrays[6].shape[0]
    one_group = heads_row == STATE_HEADS // STATE_GROUPS and heads_col == 2 * heads_row
    if one_group and prompts == 2 * columns and columns & (columns - 1) == 0:
        return matched(*arrays)
    return any_shape(*arrays)


def solution(mesh):
    placed = (
        P("prompt", "comp"),
        P("prompt", None),
        P("comp", "prompt"),
        P("comp", None, "prompt"),
        P("comp", None, "prompt"),
        P("comp", None, None),
        P("prompt", "comp", None),
        P("comp"),
        P(),
        P(),
        P(),
        P("prompt"),
    )
    return jax.shard_map(
        local, mesh=mesh, in_specs=placed, out_specs=P("comp", None, "prompt"), check_vma=False
    )
```

```python
import jax
import jax.numpy as jnp
from jax import lax
from jax.experimental import pallas as pl
from jax.experimental.pallas import tpu as pltpu
from jax.sharding import PartitionSpec as P

STATE_HEADS = 256
HEAD_WIDTH = 64
STATE_WIDTH = 256
STATE_GROUPS = 8
CONV = 4
BLOCK = 128


EPS = 1e-05
HIGHEST = lax.Precision.HIGHEST


def from_behind(block, axis, distance):
    devices = range(lax.axis_size(axis))
    route = [(i - distance, i) for i in devices if i - distance in devices]
    return lax.ppermute(block, axis, route)


def carried_in(array, axis, combine, identity):
    peers, position = (lax.axis_size(axis), lax.axis_index(axis))
    everything = jax.tree.map(
        lambda part, kind: lax.all_gather(part.astype(kind), axis),
        array,
        (jnp.bfloat16, jnp.bfloat16),
    )
    start = jax.tree.map(
        lambda part, zero: jnp.broadcast_to(jnp.asarray(zero, part.dtype), part.shape),
        array,
        identity,
    )

    def hop(k, before):
        reached = k < position
        new = combine(
            before, jax.tree.map(lambda part, own: part[k].astype(own.dtype), everything, array)
        )
        return jax.tree.map(lambda a, b: jnp.where(reached, a, b), new, before)

    return lax.fori_loop(0, peers, hop, start)


def from_root(array, axis, root):
    mine = lax.axis_index(axis) == root
    return lax.psum(jnp.where(mine, array, jnp.zeros_like(array)), axis)


def from_partner(block, axis, stride):
    count = lax.axis_size(axis)
    route = []
    for low in range(count):
        high = low | 1 << stride
        if high != low and high < count:
            route += [(low, high), (high, low)]
    return lax.ppermute(block, axis, route)


def causal_conv(source, kernel, leading):
    padded = jnp.concatenate([leading, source], axis=0).astype(jnp.float32)
    kernel_wide = kernel.astype(jnp.float32)
    row_count = source.shape[0]
    summed = jnp.zeros(source.shape, jnp.float32)
    for offset in range(kernel.shape[0]):
        summed = summed + kernel_wide[offset] * padded[offset : offset + row_count]
    return jax.nn.silu(summed).astype(jnp.bfloat16)


def block_scan(state_in, inner_blk, b_blk, c_blk, step_blk, rate_vals):
    cumul = jnp.cumsum(-rate_vals[:, :, None] * step_blk, axis=2)
    scores = jnp.einsum("ign,jgn->gij", c_blk, b_blk, preferred_element_type=jnp.float32)
    spread_log = cumul[:, :, :, None] - cumul[:, :, None, :]
    length_q = step_blk.shape[2]
    causal = jnp.arange(length_q)[:, None] >= jnp.arange(length_q)[None, :]
    decay_mat = jnp.exp(jnp.where(causal, spread_log, -jnp.inf))
    mixer_w = (scores[:, None] * decay_mat * step_blk[:, :, None, :]).astype(jnp.bfloat16)
    intra_part = jnp.einsum(
        "gkij,jgkd->igkd", mixer_w, inner_blk, preferred_element_type=jnp.float32
    )
    readout = jnp.einsum("ign,gkdn->igkd", c_blk.astype(jnp.float32), state_in, precision=HIGHEST)
    inter_part = jnp.transpose(jnp.exp(cumul), (2, 0, 1))[..., None] * readout
    weights = jnp.exp(cumul[:, :, -1:] - cumul) * step_blk
    packed = (inner_blk.astype(jnp.float32) * jnp.transpose(weights, (2, 0, 1))[..., None]).astype(
        jnp.bfloat16
    )
    fresh_part = jnp.einsum("jgn,jgkd->gkdn", b_blk, packed, preferred_element_type=jnp.float32)
    return (
        intra_part + inter_part,
        jnp.exp(cumul[:, :, -1])[..., None, None] * state_in + fresh_part,
    )


def any_shape(
    prompt_inner,
    prompt_proj,
    prompt_step,
    completion_inner,
    completion_gate,
    completion_projections,
    sample_step,
    sample_length,
    decay_log,
    conv_inner,
    conv_proj,
    norm_gain,
):
    prompt_count = lax.axis_size("prompt")
    prompt_idx = lax.axis_index("prompt")
    column_idx = lax.axis_index("comp")
    heads_group = STATE_HEADS // STATE_GROUPS
    heads_col = prompt_step.shape[0]
    heads_row = sample_step.shape[0]
    state_feats = STATE_GROUPS * STATE_WIDTH
    lag_rows = CONV - 1
    rows_prompt = prompt_inner.shape[0]
    prev_inner, prev_proj = from_behind(
        (
            prompt_inner[rows_prompt - lag_rows :],
            prompt_proj[rows_prompt - lag_rows :, :state_feats],
        ),
        "prompt",
        1,
    )
    col_start = column_idx * heads_col
    conv_col = lax.dynamic_slice_in_dim(
        conv_inner, col_start * HEAD_WIDTH, heads_col * HEAD_WIDTH, 1
    )
    inner_conv = causal_conv(prompt_inner, conv_col, prev_inner)
    b_conv = causal_conv(prompt_proj[:, :state_feats], conv_proj[:, :state_feats], prev_proj)
    rate_col = jnp.exp(lax.dynamic_slice_in_dim(decay_log, col_start, heads_col, 0))
    step_col = jax.nn.softplus(prompt_step)
    cumul = jnp.cumsum(-rate_col[:, None] * step_col, axis=1)
    local_log = cumul[:, -1]
    weight_col = jnp.exp(local_log[:, None] - cumul) * step_col
    group_span = max(1, heads_col // heads_group)
    per_group = heads_col // group_span
    group_start = col_start // heads_group
    b_select = lax.dynamic_slice_in_dim(
        b_conv.reshape(rows_prompt, STATE_GROUPS, STATE_WIDTH), group_start, group_span, 1
    ).astype(jnp.float32)
    scaled = (
        inner_conv.astype(jnp.float32).reshape(rows_prompt, heads_col, HEAD_WIDTH)
        * jnp.transpose(weight_col)[:, :, None]
    )
    scaled = scaled.reshape(rows_prompt, group_span, per_group, HEAD_WIDTH)
    local_state = jnp.einsum("tgn,tghd->ghdn", b_select, scaled, precision=HIGHEST).reshape(
        heads_col, HEAD_WIDTH, STATE_WIDTH
    )
    own_inner = prompt_inner[rows_prompt - lag_rows :].astype(jnp.float32)
    own_proj = prompt_proj[rows_prompt - lag_rows :].astype(jnp.float32)
    last_index = prompt_count - 1
    head_start = prompt_idx * heads_row
    owner = head_start // heads_col
    head_offset = head_start - owner * heads_col

    def combine(earlier, later):
        return (earlier[0] + later[0], earlier[1] * jnp.exp(later[0])[:, None, None] + later[1])

    before = carried_in(
        (local_log, local_state),
        "prompt",
        combine,
        (jnp.zeros_like(local_log), jnp.zeros_like(local_state)),
    )
    through = combine(before, (local_log, local_state))[1]
    final_state, tail_inner, tail_proj = (
        from_root(through.astype(jnp.bfloat16), "prompt", last_index).astype(through.dtype),
        from_root(own_inner.astype(jnp.bfloat16), "prompt", last_index).astype(own_inner.dtype),
        from_root(own_proj.astype(jnp.bfloat16), "prompt", last_index).astype(own_proj.dtype),
    )
    moved_state, moved_inner = (
        from_root(final_state.astype(jnp.bfloat16), "comp", owner).astype(final_state.dtype),
        from_root(tail_inner.astype(jnp.bfloat16), "comp", owner).astype(tail_inner.dtype),
    )
    start_state = lax.dynamic_slice_in_dim(moved_state, head_offset, heads_row, 0)
    lead_inner = lax.dynamic_slice_in_dim(
        moved_inner, head_offset * HEAD_WIDTH, heads_row * HEAD_WIDTH, 1
    ).astype(jnp.bfloat16)
    group_row = head_start // heads_group
    b_start = group_row * STATE_WIDTH
    c_start = state_feats + group_row * STATE_WIDTH
    proj_select = jnp.concatenate(
        [
            lax.dynamic_slice_in_dim(completion_projections, b_start, STATE_WIDTH, 2),
            lax.dynamic_slice_in_dim(completion_projections, c_start, STATE_WIDTH, 2),
        ],
        axis=2,
    )
    kernel_select = jnp.concatenate(
        [
            lax.dynamic_slice_in_dim(conv_proj, b_start, STATE_WIDTH, 1),
            lax.dynamic_slice_in_dim(conv_proj, c_start, STATE_WIDTH, 1),
        ],
        axis=1,
    )
    lead_wide = tail_proj.astype(jnp.bfloat16)
    lead_select = jnp.concatenate(
        [
            lax.dynamic_slice_in_dim(lead_wide, b_start, STATE_WIDTH, 1),
            lax.dynamic_slice_in_dim(lead_wide, c_start, STATE_WIDTH, 1),
        ],
        axis=1,
    )
    conv_row = lax.dynamic_slice_in_dim(
        conv_inner, head_start * HEAD_WIDTH, heads_row * HEAD_WIDTH, 1
    )
    rate_row = jnp.exp(lax.dynamic_slice_in_dim(decay_log, head_start, heads_row, 0))
    step_row = jax.nn.softplus(sample_step)
    slot_count = completion_inner.shape[0]
    sample_len = completion_inner.shape[1]
    block_count = sample_len // BLOCK

    def advance(carry, block_in):
        block_out, carry_next = block_scan(
            carry, block_in[0], block_in[1], block_in[2], block_in[3], rate_row[None]
        )
        return (carry_next, block_out)

    gated_list = []
    square_list = []
    for slot in range(slot_count):
        slot_conv = causal_conv(completion_inner[slot], conv_row, lead_inner)
        proj_conv = causal_conv(proj_select[slot], kernel_select, lead_select)
        inner_blocks = slot_conv.reshape(block_count, BLOCK, 1, heads_row, HEAD_WIDTH)
        b_blocks = proj_conv[:, :STATE_WIDTH].reshape(block_count, BLOCK, 1, STATE_WIDTH)
        c_blocks = proj_conv[:, STATE_WIDTH:].reshape(block_count, BLOCK, 1, STATE_WIDTH)
        step_blocks = jnp.transpose(
            step_row[:, slot].reshape(heads_row, block_count, BLOCK), (1, 0, 2)
        )[:, None]
        block_inputs = (inner_blocks, b_blocks, c_blocks, step_blocks)
        _, block_outs = lax.scan(advance, start_state[None], block_inputs)
        ssm_out = block_outs.reshape(sample_len, heads_row * HEAD_WIDTH)
        gated = ssm_out * jax.nn.silu(completion_gate[slot].astype(jnp.float32))
        gated_list.append(gated)
        square_list.append(jnp.sum(gated * gated, axis=1))
    square_all = jnp.stack(square_list)
    partner_bits = (prompt_count // STATE_GROUPS).bit_length() - 1
    for bit_number in range(partner_bits):
        square_all = square_all + from_partner(square_all, "prompt", bit_number)
    scale_all = lax.rsqrt(square_all / (heads_group * HEAD_WIDTH) + EPS)
    gated_all = jnp.stack(gated_list)
    result = gated_all * scale_all[:, :, None] * norm_gain[None, None, :]
    live_rows = jnp.arange(sample_len)[None, :] < sample_length[:, None]
    return jnp.where(live_rows[:, :, None], result, 0.0).astype(jnp.bfloat16)


LOG2E = 1.4426950408889634
AXES = ("prompt", "comp")
CHUNKS = 2
TAIL = 16
VMEM_BYTES = 48 * 1024 * 1024


def routed(block, route):
    columns = lax.axis_size("comp")
    pairs = []
    for row in range(lax.axis_size("prompt")):
        for column in range(columns):
            target = route(row // 2, row % 2, column)
            if target is not None:
                plane, core, to = target
                pairs.append((row * columns + column, (2 * plane + core) * columns + to))
    return lax.ppermute(block, AXES, pairs)


def half_silu(value):
    return 0.5 * value * (1.0 + jnp.tanh(0.5 * value))


def conv_rows(padded, taps, lead, block):
    rows = block.shape[0]
    width = block.shape[1]
    padded[0:8, 0:width] = lead.astype(jnp.float32)[TAIL - 8 :]
    padded[8 : 8 + rows, 0:width] = block.astype(jnp.float32)
    wide = taps.astype(jnp.float32)
    total = wide[0:1] * padded[5 : 5 + rows, 0:width]
    for tap in range(1, CONV):
        total = total + wide[tap : tap + 1] * padded[5 + tap : 5 + tap + rows, 0:width]
    return half_silu(total)


def spread_heads(first, heads, width):
    row = lax.broadcasted_iota(jnp.int32, (heads, width), 0)
    col = lax.broadcasted_iota(jnp.int32, (heads, width), 1)
    return row == first + col // HEAD_WIDTH


def contract(lhs, rhs, dims, precision=None):
    return lax.dot_general(
        lhs, rhs, (dims, ((), ())), preferred_element_type=jnp.float32, precision=precision
    )


def softplus(value):
    return jnp.maximum(value, 0.0) + jnp.log1p(jnp.exp(-jnp.abs(value)))


def group_of(decay, index, size):
    every = jnp.reshape(decay[...], (1, decay.shape[0]))
    return pltpu.roll(every, decay.shape[0] - index * size, 1)[:, 0:size]


def pack_kernel(
    place, inner, proj, step, last_inner, last_b, last_c, swap_out, near_0, near_1, extra, sems
):
    rows, heads = step.shape[1], step.shape[0]
    features = heads * HEAD_WIDTH
    column, core = place[1], place[2]
    theirs = 1 - core
    to_features = pltpu.make_async_copy(
        inner.at[:, pl.ds(pl.multiple_of(theirs * features, features), features)],
        swap_out.at[0:rows, 0:features],
        sems.at[0],
    )
    to_features.start()
    group_at = (2 * column + theirs) * STATE_WIDTH
    to_b = pltpu.make_async_copy(
        proj.at[:, pl.ds(pl.multiple_of(group_at, STATE_WIDTH), STATE_WIDTH)],
        swap_out.at[0:rows, features : features + STATE_WIDTH],
        sems.at[1],
    )
    to_b.start()
    dt = jnp.transpose(softplus(step[...]))
    high = dt.astype(jnp.bfloat16)
    low = (dt - high.astype(jnp.float32)).astype(jnp.bfloat16)
    extra[0:rows, 0 : 4 * heads] = jnp.concatenate([high, low, high, low], axis=1)
    for to, near in enumerate((near_0, near_1)):
        group = slice(to * STATE_WIDTH, (to + 1) * STATE_WIDTH)
        inner_last = last_inner[:, to * features : (to + 1) * features].astype(jnp.float32)
        bc_last = jnp.concatenate([last_b[:, group], last_c[:, group]], axis=1)
        pieces = [
            inner_last[TAIL - 3 :, at : at + 2 * STATE_WIDTH]
            for at in range(0, features, 2 * STATE_WIDTH)
        ]
        pieces.append(bc_last.astype(jnp.float32)[TAIL - 3 :])
        pieces.append(jnp.zeros((TAIL - 3 * len(pieces), 2 * STATE_WIDTH), jnp.float32))
        near[...] = jnp.concatenate(pieces, axis=0).astype(jnp.bfloat16)
    extra[rows:] = jnp.where(core == 0, near_1[...].astype(jnp.float32), near_0[...].astype(jnp.float32)).astype(jnp.bfloat16)
    to_dt = pltpu.make_async_copy(
        extra.at[0:rows, 0 : 4 * heads], swap_out.at[0:rows, features + STATE_WIDTH :], sems.at[2]
    )
    to_dt.start()
    to_tail = pltpu.make_async_copy(
        extra.at[rows:], swap_out.at[rows:, 0 : 2 * STATE_WIDTH], sems.at[3]
    )
    to_tail.start()
    to_features.wait()
    to_b.wait()
    to_dt.wait()
    to_tail.wait()


def prompt_weights_kernel(
    place, own_b, other_b, other_dt, other_tail, halo_0, halo_1, own_tail, taps, own_step, decay,
    w_out, b_out, log_out, halo_out, tail_out, padded,
):
    core = place[2]
    rows, heads = own_b.shape[0], own_step.shape[0]
    first_own = core == 0
    rate = jnp.exp(group_of(decay, 2 * place[1] + core, heads))
    dt_own = jnp.transpose(softplus(own_step[...]))
    parts = other_dt[...].astype(jnp.float32)
    dt_other = parts[:, 0:heads] + parts[:, heads : 2 * heads]
    row = lax.broadcasted_iota(jnp.int32, (rows, rows), 0)
    col = lax.broadcasted_iota(jnp.int32, (rows, rows), 1)
    later = (col > row).astype(jnp.float32)
    after = contract(later, jnp.concatenate([dt_own, dt_other], axis=1), ((1,), (0,)), HIGHEST)
    sum_own = after[0:1, 0:heads] + dt_own[0:1]
    sum_other = after[0:1, heads:] + dt_other[0:1]
    after_own = after[:, 0:heads] + jnp.where(first_own, sum_other, 0.0)
    after_other = after[:, heads:] + jnp.where(first_own, 0.0, sum_own)
    w_out[0:rows] = jnp.exp(-rate * after_own) * dt_own
    w_out[rows:] = jnp.exp(-rate * after_other) * dt_other
    total = jnp.broadcast_to(-rate * (sum_own + sum_other), (8, heads))
    spread = spread_heads(0, heads, heads * HEAD_WIDTH).astype(jnp.bfloat16)
    which = lax.broadcasted_iota(jnp.int32, total.shape, 0)
    high = total.astype(jnp.bfloat16).astype(jnp.float32)
    mid = (total - high).astype(jnp.bfloat16).astype(jnp.float32)
    low = total - high - mid
    parts = jnp.where(which == 0, high, jnp.where(which == 1, mid, jnp.where(which == 2, low, 0.0)))
    wide = contract(parts.astype(jnp.bfloat16), spread, ((1,), (0,)))
    log_out[...] = jnp.concatenate([wide, jnp.zeros_like(wide)], axis=0).astype(jnp.bfloat16)
    near = halo_0[...].astype(jnp.float32) + halo_1[...].astype(jnp.float32)
    features = heads * HEAD_WIDTH
    for index in range(features // near.shape[1]):
        at = index * near.shape[1]
        rows_3 = near[3 * index : 3 * index + 3]
        wide = jnp.concatenate([jnp.zeros((TAIL - 3, near.shape[1]), jnp.float32), rows_3], axis=0)
        halo_out[:, at : at + near.shape[1]] = wide.astype(jnp.bfloat16)
    at = 3 * (features // near.shape[1])
    halo = jnp.concatenate(
        [jnp.zeros((TAIL - 3, STATE_WIDTH), jnp.float32), near[at : at + 3, 0:STATE_WIDTH]], axis=0
    )
    tail_out[...] = jnp.where(
        first_own, other_tail[...].astype(jnp.float32), own_tail[...].astype(jnp.float32)
    ).astype(jnp.bfloat16)
    own_last, other_last = own_b[rows - TAIL :], other_b[rows - TAIL :]
    lead_own = jnp.where(first_own, halo, other_last.astype(jnp.float32))
    lead_other = jnp.where(first_own, own_last.astype(jnp.float32), halo)
    conv_own = conv_rows(padded, taps[...], lead_own, own_b[...])
    b_out[:, 0:rows] = jnp.transpose(conv_own).astype(jnp.bfloat16)
    conv_other = conv_rows(padded, taps[...], lead_other, other_b[...])
    b_out[:, rows:] = jnp.transpose(conv_other).astype(jnp.bfloat16)


def prompt_state_kernel(
    chunk, parts, place, own, other, halo, taps, weights, b_turned, logs, tail, *rest
):
    outs, padded = rest[:parts], rest[parts]
    column, core = place[1], place[2]
    first_own = core == 0
    rows = own.shape[0]
    width = outs[0].shape[1]
    part_width = own.shape[1] // parts
    heads = weights.shape[1]
    state = b_turned.shape[0]
    w = weights[...].astype(jnp.bfloat16)
    for step in range(parts):
        part = column ^ step
        start = part * part_width + chunk * width
        cols = pl.ds(pl.multiple_of(start, width), width)
        spread = spread_heads(start // HEAD_WIDTH, heads, width).astype(jnp.bfloat16)
        w_wide = contract(w, spread, ((1,), (0,)))
        own_x, other_x, halo_x = own[:, cols], other[:, cols], halo[:, cols]
        own_last, other_last = own_x[rows - TAIL :], other_x[rows - TAIL :]
        lead_own = jnp.where(first_own, halo_x.astype(jnp.float32), other_last.astype(jnp.float32))
        lead_other = jnp.where(first_own, own_last.astype(jnp.float32), halo_x.astype(jnp.float32))
        x_own = conv_rows(padded, taps[:, cols], lead_own, own_x) * w_wide[0:rows]
        x_other = conv_rows(padded, taps[:, cols], lead_other, other_x) * w_wide[rows:]
        mine = contract(b_turned[:, 0:rows], x_own.astype(jnp.bfloat16), ((1,), (0,)))
        theirs = contract(b_turned[:, rows:], x_other.astype(jnp.bfloat16), ((1,), (0,)))
        outs[step][0:state] = (mine + theirs).astype(jnp.bfloat16)
        outs[step][state : state + TAIL] = logs[:, cols]
        if outs[step].shape[0] > state + TAIL:
            for index in range(2):
                at = state + TAIL * (index + 1)
                outs[step][at : at + TAIL] = tail[:, index * width : (index + 1) * width]


def pick_kernel(count, place, *refs):
    held, ready = refs[:count], refs[count : 2 * count]
    turn = place[0] ^ place[1]
    rows, width = ready[0].shape
    for index in range(count):

        @pl.when(turn == index)
        def _():
            for step in range(count):
                ready[step][...] = held[index ^ step][0:rows]
            for tail in refs[2 * count :]:
                for half in range(2):
                    at = rows + TAIL * half
                    tail[:, half * width : (half + 1) * width] = held[index][at : at + TAIL]


def join_state_kernel(place, *refs):
    arrived, out = refs[: lax.axis_size("comp")], refs[-1]
    plane = place[0]
    state = out.shape[0]
    totals = []
    for ref in arrived:
        rows = ref[state:].astype(jnp.float32)
        totals.append(rows[0:1] + rows[1:2] + rows[2:3])
    joined = None
    for step, ref in enumerate(arrived):
        after = jnp.zeros_like(totals[0])
        for other in range(len(arrived)):
            if other != step:
                after = after + jnp.where((plane ^ other) > (plane ^ step), totals[other], 0.0)
        term = jnp.exp(after) * ref[0:state].astype(jnp.float32)
        joined = term if joined is None else joined + term
    out[...] = joined.astype(jnp.bfloat16)


def completion_kernel(
    slot, place, inner, gate, b_in, c_in, tail, taps, taps_b, taps_c, step,
    decay, after, fixed_out, factor_out, c_out, padded, diag_low, rows_high,
    cum_cols, base_rows, log_rows, leads,
):
    rows = inner.shape[1]
    width = inner.shape[2]
    heads = width // HEAD_WIDTH
    half = rows // 2

    @pl.when(pl.program_id(0) == 0)
    def _():
        edges = tail[...].astype(jnp.float32)
        blank = jnp.zeros((TAIL - 3, width), jnp.float32)
        for block in range(leads.shape[0]):
            leads[block] = jnp.concatenate([blank, edges[3 * block : 3 * block + 3]], axis=0)
        lead_bc = leads[leads.shape[0] - 1]
        lead_b, lead_c = lead_bc[:, 0:STATE_WIDTH], lead_bc[:, STATE_WIDTH:]
        b = conv_rows(padded, taps_b[...], lead_b, b_in[0]).astype(jnp.bfloat16)
        c = conv_rows(padded, taps_c[...], lead_c, c_in[0]).astype(jnp.bfloat16)
        c_out[...] = c
        scores = contract(c, b, ((1,), (1,)))
        row = lax.broadcasted_iota(jnp.int32, (rows, rows), 0)
        col = lax.broadcasted_iota(jnp.int32, (rows, rows), 1)
        scores = jnp.where(row >= col, scores, 0.0)
        diag_low[...] = scores[0:half, 0:half]
        rows_high[...] = scores[half:]
        dt = softplus(step[:, slot])
        decay_row = jnp.broadcast_to(group_of(decay, place[3], dt.shape[0]), (8, dt.shape[0]))
        decay_col = jnp.transpose(decay_row)[:, 0:1]
        before = (row <= col).astype(jnp.float32)
        cum = contract(dt, before, ((1,), (0,)), HIGHEST) * (-LOG2E * jnp.exp(decay_col))
        log_dt = jnp.log(dt) * LOG2E
        turned = jnp.transpose(cum)
        for block in range(cum_cols.shape[0]):
            those = slice(block * heads, (block + 1) * heads)
            cum_cols[block] = turned[:, those]
            base_rows[block] = cum[those] - log_dt[those]
            log_rows[block] = log_dt[those]

    x = conv_rows(padded, taps[...], leads[pl.program_id(0)], inner[0])
    x = x.astype(jnp.bfloat16)
    here = pl.program_id(0)
    cum_col, base_row, log_dt = cum_cols[here], base_rows[here], log_rows[here]
    silu_gate = half_silu(gate[0].astype(jnp.float32))
    spread = spread_heads(0, heads, width).astype(jnp.bfloat16)
    decay_wide = contract(jnp.exp2(cum_col).astype(jnp.bfloat16), spread, ((1,), (0,)))
    factor_out[...] = (decay_wide * silu_gate).astype(jnp.bfloat16)
    low, high = diag_low[...], rows_high[...]
    pair = 2 * HEAD_WIDTH
    lane = lax.broadcasted_iota(jnp.int32, (rows, pair), 1)
    for first in range(0, heads, 2):
        at = first * HEAD_WIDTH
        x_pair = x[:, at : at + pair]
        zero = jnp.zeros_like(x_pair)
        left = jnp.where(lane < HEAD_WIDTH, x_pair, zero)
        right = jnp.where(lane < HEAD_WIDTH, zero, x_pair)
        lows, highs = [], []
        for h in (first, first + 1):
            cc = cum_col[:, h : h + 1]
            rr, ll = base_row[h : h + 1], log_dt[h : h + 1]
            grown = jnp.minimum(cc[0:half] - rr[:, 0:half], ll[:, 0:half])
            lows.append((low * jnp.exp2(grown)).astype(jnp.bfloat16))
            grown = jnp.minimum(cc[half:] - rr, ll)
            highs.append((high * jnp.exp2(grown)).astype(jnp.bfloat16))
        y_low = contract(
            jnp.concatenate(lows, axis=1),
            jnp.concatenate([left[0:half], right[0:half]], axis=0),
            ((1,), (0,)),
        )
        y_high = contract(
            jnp.concatenate(highs, axis=1), jnp.concatenate([left, right], axis=0), ((1,), (0,))
        )
        fixed_out[0:half, at : at + pair] = (
            y_low * silu_gate[0:half, at : at + pair]
        ).astype(jnp.bfloat16)
        fixed_out[half:, at : at + pair] = (
            y_high * silu_gate[half:, at : at + pair]
        ).astype(jnp.bfloat16)


def finish_kernel(parts, chunks, slots, place, live, gain, *refs):
    states, rest = refs[: parts * chunks], refs[parts * chunks :]
    out, gated = rest[-2], rest[-1]
    column = place[1]
    rows, features = out.shape[1], out.shape[2]
    width = states[0].shape[1]
    part_width = features // parts
    for slot in range(slots):
        c_ref, fixed, factor = rest[3 * slot : 3 * slot + 3]

        @pl.when(pl.program_id(0) == slot)
        def _():
            c = c_ref[...]
            squares = jnp.zeros((rows, 1), jnp.float32)
            for chunk in range(chunks):
                for step in range(parts):
                    start = (column ^ step) * part_width + chunk * width
                    cols = pl.ds(pl.multiple_of(start, width), width)
                    read = contract(c, states[chunk * parts + step][...], ((1,), (0,)))
                    weight = factor[:, cols].astype(jnp.float32)
                    value = fixed[:, cols].astype(jnp.float32) + read * weight
                    gated[:, cols] = value
                    squares = squares + jnp.sum(value * value, axis=1, keepdims=True)
            scale = lax.rsqrt(squares / features + EPS)
            alive = lax.broadcasted_iota(jnp.int32, (rows, 1), 0) < live[slot]
            scale = jnp.where(alive, scale, 0.0)
            out[0] = (gated[...] * scale * jnp.reshape(gain[...], (1, features))).astype(jnp.bfloat16)


LASTS = dict(
    pack=2, prompt_weights=2, prompt_state=3, pick=1, join_state=1, completion=8, finish=4
)


def run(kernel, name, place, out_shape, in_specs, out_specs, operands, grid=(1,), scratch=(), scalars=1):
    return pl.pallas_call(
        kernel,
        out_shape=out_shape,
        grid_spec=pltpu.PrefetchScalarGridSpec(
            num_scalar_prefetch=scalars,
            grid=grid,
            in_specs=in_specs,
            out_specs=out_specs,
            scratch_shapes=scratch,
        ),
        compiler_params=pltpu.CompilerParams(
            dimension_semantics=("arbitrary",) * len(grid), vmem_limit_bytes=VMEM_BYTES
        ),
        cost_estimate=pl.CostEstimate(
            flops=LASTS[name] * 10**9, transcendentals=0, bytes_accessed=LASTS[name] * 3 * 10**6
        ),
        name=name,
    )(*place, *operands)


def matched(
    prompt_inner,
    prompt_proj,
    prompt_step,
    completion_inner,
    completion_gate,
    completion_projections,
    sample_step,
    sample_length,
    decay_log,
    conv_inner,
    conv_proj,
    norm_gain,
):
    parts = lax.axis_size("comp")
    row, column = lax.axis_index("prompt"), lax.axis_index("comp")
    plane, core = row // 2, row % 2
    group = 2 * column + core
    rows = prompt_inner.shape[0]
    heads = sample_step.shape[0]
    features = heads * HEAD_WIDTH
    place = jnp.stack([plane, column, core, row]).astype(jnp.int32)
    bf16, f32 = jnp.bfloat16, jnp.float32

    def take(array, start, size, axis):
        return lax.dynamic_slice_in_dim(array, start, size, axis)

    whole = lambda shape: pl.BlockSpec(shape, lambda *_: (0,) * len(shape))
    unread = pl.BlockSpec(memory_space=pl.ANY)
    planes = lax.axis_size("prompt") // 2
    state_blocks = features // STATE_WIDTH
    swapped_width = features + STATE_WIDTH + 4 * heads
    pair_width = 2 * STATE_WIDTH
    edge = jax.ShapeDtypeStruct((TAIL, pair_width), bf16)
    last_block = rows // TAIL - 1
    c_at = STATE_GROUPS
    in_hbm = pl.BlockSpec(memory_space=pltpu.HBM)
    held_inner = pltpu.with_memory_space_constraint(prompt_inner, pltpu.HBM)
    held_proj = pltpu.with_memory_space_constraint(prompt_proj, pltpu.HBM)

    swap, near_0, near_1 = run(
        pack_kernel,
        "pack",
        (place,),
        (jax.ShapeDtypeStruct((rows + TAIL, swapped_width), bf16), edge, edge),
        [
            in_hbm,
            in_hbm,
            pl.BlockSpec((heads, rows), lambda i, s: (1 - s[2], 0)),
            pl.BlockSpec((TAIL, 2 * features), lambda i, s: (last_block, 0)),
            pl.BlockSpec((TAIL, pair_width), lambda i, s: (last_block, s[1])),
            pl.BlockSpec((TAIL, pair_width), lambda i, s: (last_block, c_at // 2 + s[1])),
        ],
        (pl.BlockSpec(memory_space=pl.ANY),) + (whole(edge.shape),) * 2,
        (held_inner, held_proj, prompt_step, held_inner, held_proj, held_proj),
        scratch=[pltpu.VMEM((rows + TAIL, pair_width), bf16), pltpu.SemaphoreType.DMA((4,))],
    )
    other = routed(swap, lambda z, k, c: (z, 1 - k, c))
    halo_0, halo_1 = [
        routed(near, lambda z, k, c: (z + 1, to, c) if k == 1 and z + 1 < planes else None)
        for to, near in enumerate((near_0, near_1))
    ]
    weights, b_turned, logs, halo, tail = run(
        prompt_weights_kernel,
        "prompt_weights",
        (place,),
        (
            jax.ShapeDtypeStruct((2 * rows, heads), f32),
            jax.ShapeDtypeStruct((STATE_WIDTH, 2 * rows), bf16),
            jax.ShapeDtypeStruct((TAIL, features), bf16),
            jax.ShapeDtypeStruct((TAIL, features), bf16),
            edge,
        ),
        [
            pl.BlockSpec((rows, STATE_WIDTH), lambda i, s: (0, 2 * s[1] + s[2])),
            pl.BlockSpec((rows, STATE_WIDTH), lambda i, s: (0, state_blocks)),
            pl.BlockSpec((rows, 4 * heads), lambda i, s: (0, (features + STATE_WIDTH) // (4 * heads))),
            pl.BlockSpec((TAIL, pair_width), lambda i, s: (rows // TAIL, 0)),
            whole(edge.shape),
            whole(edge.shape),
            whole(edge.shape),
            pl.BlockSpec((CONV, STATE_WIDTH), lambda i, s: (0, 2 * s[1] + s[2])),
            pl.BlockSpec((heads, rows), lambda i, s: (s[2], 0)),
            whole((STATE_HEADS,)),
        ],
        (
            whole((2 * rows, heads)),
            whole((STATE_WIDTH, 2 * rows)),
            whole((TAIL, features)),
            whole((TAIL, features)),
            whole(edge.shape),
        ),
        (
            prompt_proj, other, other, other, halo_0, halo_1, near_1, conv_proj, prompt_step, decay_log,
        ),
        scratch=[pltpu.VMEM((rows + 8, STATE_WIDTH), f32)],
    )
    width = features // parts // CHUNKS
    message = jax.ShapeDtypeStruct((STATE_WIDTH + TAIL, width), bf16)
    far = routed(tail, lambda z, k, c: (c, k, c) if z + 1 == planes else None)
    held = []
    for chunk in range(CHUNKS):
        last = chunk + 1 == CHUNKS
        spread = jax.ShapeDtypeStruct((STATE_WIDTH + (3 if last else 1) * TAIL, width), bf16)
        sent = run(
            lambda *refs, chunk=chunk: prompt_state_kernel(chunk, parts, *refs),
            "prompt_state",
            (place,),
            (spread,) * parts,
            [
                pl.BlockSpec((rows, features), lambda i, s: (0, s[2])),
                pl.BlockSpec((rows, features), lambda i, s: (0, 0)),
                pl.BlockSpec((TAIL, features), lambda i, s: (0, 0)),
                pl.BlockSpec((CONV, features), lambda i, s: (0, 2 * s[1] + s[2])),
                whole((2 * rows, heads)),
                whole((STATE_WIDTH, 2 * rows)),
                whole((TAIL, features)),
                whole(edge.shape) if last else unread,
            ],
            (whole(spread.shape),) * parts,
            (prompt_inner, other, halo, conv_inner, weights, b_turned, logs, far if last else tail),
            scratch=[pltpu.VMEM((rows + 8, width), f32)],
        )
        held.append(
            [sent[0]]
            + [routed(sent[step], lambda z, k, c: (z, k, c ^ step)) for step in range(1, parts)]
        )

    slots, positions = completion_inner.shape[:2]
    block_heads = 8
    block = block_heads * HEAD_WIDTH
    blocks = heads // block_heads
    finished = []

    def completion(slot, after):
        return run(
            lambda *refs: completion_kernel(slot, *refs),
            "completion",
            (place,),
            (
                jax.ShapeDtypeStruct((positions, features), bf16),
                jax.ShapeDtypeStruct((positions, features), bf16),
                jax.ShapeDtypeStruct((positions, STATE_WIDTH), bf16),
            ),
            [
                pl.BlockSpec((1, positions, block), lambda j, s: (slot, 0, j)),
                pl.BlockSpec((1, positions, block), lambda j, s: (slot, 0, j)),
                pl.BlockSpec((1, positions, STATE_WIDTH), lambda j, s: (slot, 0, s[3])),
                pl.BlockSpec((1, positions, STATE_WIDTH), lambda j, s: (slot, 0, c_at + s[3])),
                whole(edge.shape),
                pl.BlockSpec((CONV, block), lambda j, s: (0, s[3] * blocks + j)),
                pl.BlockSpec((CONV, STATE_WIDTH), lambda j, s: (0, s[3])),
                pl.BlockSpec((CONV, STATE_WIDTH), lambda j, s: (0, c_at + s[3])),
                whole((heads, slots, positions)),
                whole((STATE_HEADS,)),
                unread,
            ],
            (
                pl.BlockSpec((positions, block), lambda j, s: (0, j)),
                pl.BlockSpec((positions, block), lambda j, s: (0, j)),
                whole((positions, STATE_WIDTH)),
            ),
            (
                completion_inner,
                completion_gate,
                completion_projections,
                completion_projections,
                tail,
                conv_inner,
                conv_proj,
                conv_proj,
                sample_step,
                decay_log,
                after,
            ),
            grid=(blocks,),
            scratch=[
                pltpu.VMEM((positions + 8, block), f32),
                pltpu.VMEM((positions // 2, positions // 2), f32),
                pltpu.VMEM((positions // 2, positions), f32),
                pltpu.VMEM((blocks, positions, block_heads), f32),
                pltpu.VMEM((blocks, block_heads, positions), f32),
                pltpu.VMEM((blocks, block_heads, positions), f32),
                pltpu.VMEM((blocks + 1, TAIL, block), f32),
            ],
        )

    arrived = []
    for chunk in range(CHUNKS):
        last = chunk + 1 == CHUNKS
        picked = (message,) * parts + (edge,) * last
        ready = run(
            lambda *refs: pick_kernel(parts, *refs),
            "pick",
            (place,),
            picked,
            [whole(array.shape) for array in held[chunk]],
            tuple(whole(each.shape) for each in picked),
            held[chunk],
        )
        arrived.append(
            [ready[0]]
            + [routed(ready[step], lambda z, k, c: (z ^ step, k, c)) for step in range(1, parts)]
        )
    tail = ready[parts]
    joined, after = [], ready[0]
    for chunk in range(CHUNKS):
        for slot in range(chunk * slots // CHUNKS, (chunk + 1) * slots // CHUNKS):
            finished.append(completion(slot, after))
            after = finished[-1][2]
        state = run(
            join_state_kernel,
            "join_state",
            (place,),
            jax.ShapeDtypeStruct((STATE_WIDTH, width), bf16),
            [whole(message.shape)] * parts + [unread],
            whole((STATE_WIDTH, width)),
            arrived[chunk] + [after],
        )
        joined += [state] + [
            routed(state, lambda z, k, c: (z, k, c ^ step)) for step in range(1, parts)
        ]
        after = state
    return run(
        lambda *refs: finish_kernel(parts, CHUNKS, slots, *refs),
        "finish",
        (place, sample_length),
        jax.ShapeDtypeStruct((slots, positions, features), bf16),
        [whole((features,))]
        + [whole((STATE_WIDTH, width))] * (parts * CHUNKS)
        + [
            whole((positions, STATE_WIDTH)),
            whole((positions, features)),
            whole((positions, features)),
        ]
        * slots,
        pl.BlockSpec((1, positions, features), lambda i, s, n: (i, 0, 0)),
        [norm_gain]
        + joined
        + [array for fixed, factor, c in finished for array in (c, fixed, factor)],
        grid=(slots,),
        scratch=[pltpu.VMEM((positions, features), f32)],
        scalars=2,
    )


def local(*arrays):
    columns, prompts = lax.axis_size("comp"), lax.axis_size("prompt")
    heads_col, heads_row = arrays[2].shape[0], arrays[6].shape[0]
    one_group = heads_row == STATE_HEADS // STATE_GROUPS and heads_col == 2 * heads_row
    if one_group and prompts == 2 * columns and columns & (columns - 1) == 0:
        return matched(*arrays)
    return any_shape(*arrays)


def solution(mesh):
    placed = (
        P("prompt", "comp"),
        P("prompt", None),
        P("comp", "prompt"),
        P("comp", None, "prompt"),
        P("comp", None, "prompt"),
        P("comp", None, None),
        P("prompt", "comp", None),
        P("comp"),
        P(),
        P(),
        P(),
        P("prompt"),
    )
    return jax.shard_map(
        local, mesh=mesh, in_specs=placed, out_specs=P("comp", None, "prompt"), check_vma=False
    )
```

```python
import jax
import jax.numpy as jnp
from jax import lax
from jax.experimental import pallas as pl
from jax.experimental.pallas import tpu as pltpu
from jax.sharding import PartitionSpec as P

STATE_HEADS = 256
HEAD_WIDTH = 64
STATE_WIDTH = 256
STATE_GROUPS = 8
CONV = 4
BLOCK = 128


EPS = 1e-05
HIGHEST = lax.Precision.HIGHEST


def from_behind(block, axis, distance):
    devices = range(lax.axis_size(axis))
    route = [(i - distance, i) for i in devices if i - distance in devices]
    return lax.ppermute(block, axis, route)


def carried_in(array, axis, combine, identity):
    peers, position = (lax.axis_size(axis), lax.axis_index(axis))
    everything = jax.tree.map(
        lambda part, kind: lax.all_gather(part.astype(kind), axis),
        array,
        (jnp.bfloat16, jnp.bfloat16),
    )
    start = jax.tree.map(
        lambda part, zero: jnp.broadcast_to(jnp.asarray(zero, part.dtype), part.shape),
        array,
        identity,
    )

    def hop(k, before):
        reached = k < position
        new = combine(
            before, jax.tree.map(lambda part, own: part[k].astype(own.dtype), everything, array)
        )
        return jax.tree.map(lambda a, b: jnp.where(reached, a, b), new, before)

    return lax.fori_loop(0, peers, hop, start)


def from_root(array, axis, root):
    mine = lax.axis_index(axis) == root
    return lax.psum(jnp.where(mine, array, jnp.zeros_like(array)), axis)


def from_partner(block, axis, stride):
    count = lax.axis_size(axis)
    route = []
    for low in range(count):
        high = low | 1 << stride
        if high != low and high < count:
            route += [(low, high), (high, low)]
    return lax.ppermute(block, axis, route)


def causal_conv(source, kernel, leading):
    padded = jnp.concatenate([leading, source], axis=0).astype(jnp.float32)
    kernel_wide = kernel.astype(jnp.float32)
    row_count = source.shape[0]
    summed = jnp.zeros(source.shape, jnp.float32)
    for offset in range(kernel.shape[0]):
        summed = summed + kernel_wide[offset] * padded[offset : offset + row_count]
    return jax.nn.silu(summed).astype(jnp.bfloat16)


def block_scan(state_in, inner_blk, b_blk, c_blk, step_blk, rate_vals):
    cumul = jnp.cumsum(-rate_vals[:, :, None] * step_blk, axis=2)
    scores = jnp.einsum("ign,jgn->gij", c_blk, b_blk, preferred_element_type=jnp.float32)
    spread_log = cumul[:, :, :, None] - cumul[:, :, None, :]
    length_q = step_blk.shape[2]
    causal = jnp.arange(length_q)[:, None] >= jnp.arange(length_q)[None, :]
    decay_mat = jnp.exp(jnp.where(causal, spread_log, -jnp.inf))
    mixer_w = (scores[:, None] * decay_mat * step_blk[:, :, None, :]).astype(jnp.bfloat16)
    intra_part = jnp.einsum(
        "gkij,jgkd->igkd", mixer_w, inner_blk, preferred_element_type=jnp.float32
    )
    readout = jnp.einsum("ign,gkdn->igkd", c_blk.astype(jnp.float32), state_in, precision=HIGHEST)
    inter_part = jnp.transpose(jnp.exp(cumul), (2, 0, 1))[..., None] * readout
    weights = jnp.exp(cumul[:, :, -1:] - cumul) * step_blk
    packed = (inner_blk.astype(jnp.float32) * jnp.transpose(weights, (2, 0, 1))[..., None]).astype(
        jnp.bfloat16
    )
    fresh_part = jnp.einsum("jgn,jgkd->gkdn", b_blk, packed, preferred_element_type=jnp.float32)
    return (
        intra_part + inter_part,
        jnp.exp(cumul[:, :, -1])[..., None, None] * state_in + fresh_part,
    )


def any_shape(
    prompt_inner,
    prompt_proj,
    prompt_step,
    completion_inner,
    completion_gate,
    completion_projections,
    sample_step,
    sample_length,
    decay_log,
    conv_inner,
    conv_proj,
    norm_gain,
):
    prompt_count = lax.axis_size("prompt")
    prompt_idx = lax.axis_index("prompt")
    column_idx = lax.axis_index("comp")
    heads_group = STATE_HEADS // STATE_GROUPS
    heads_col = prompt_step.shape[0]
    heads_row = sample_step.shape[0]
    state_feats = STATE_GROUPS * STATE_WIDTH
    lag_rows = CONV - 1
    rows_prompt = prompt_inner.shape[0]
    prev_inner, prev_proj = from_behind(
        (
            prompt_inner[rows_prompt - lag_rows :],
            prompt_proj[rows_prompt - lag_rows :, :state_feats],
        ),
        "prompt",
        1,
    )
    col_start = column_idx * heads_col
    conv_col = lax.dynamic_slice_in_dim(
        conv_inner, col_start * HEAD_WIDTH, heads_col * HEAD_WIDTH, 1
    )
    inner_conv = causal_conv(prompt_inner, conv_col, prev_inner)
    b_conv = causal_conv(prompt_proj[:, :state_feats], conv_proj[:, :state_feats], prev_proj)
    rate_col = jnp.exp(lax.dynamic_slice_in_dim(decay_log, col_start, heads_col, 0))
    step_col = jax.nn.softplus(prompt_step)
    cumul = jnp.cumsum(-rate_col[:, None] * step_col, axis=1)
    local_log = cumul[:, -1]
    weight_col = jnp.exp(local_log[:, None] - cumul) * step_col
    group_span = max(1, heads_col // heads_group)
    per_group = heads_col // group_span
    group_start = col_start // heads_group
    b_select = lax.dynamic_slice_in_dim(
        b_conv.reshape(rows_prompt, STATE_GROUPS, STATE_WIDTH), group_start, group_span, 1
    ).astype(jnp.float32)
    scaled = (
        inner_conv.astype(jnp.float32).reshape(rows_prompt, heads_col, HEAD_WIDTH)
        * jnp.transpose(weight_col)[:, :, None]
    )
    scaled = scaled.reshape(rows_prompt, group_span, per_group, HEAD_WIDTH)
    local_state = jnp.einsum("tgn,tghd->ghdn", b_select, scaled, precision=HIGHEST).reshape(
        heads_col, HEAD_WIDTH, STATE_WIDTH
    )
    own_inner = prompt_inner[rows_prompt - lag_rows :].astype(jnp.float32)
    own_proj = prompt_proj[rows_prompt - lag_rows :].astype(jnp.float32)
    last_index = prompt_count - 1
    head_start = prompt_idx * heads_row
    owner = head_start // heads_col
    head_offset = head_start - owner * heads_col

    def combine(earlier, later):
        return (earlier[0] + later[0], earlier[1] * jnp.exp(later[0])[:, None, None] + later[1])

    before = carried_in(
        (local_log, local_state),
        "prompt",
        combine,
        (jnp.zeros_like(local_log), jnp.zeros_like(local_state)),
    )
    through = combine(before, (local_log, local_state))[1]
    final_state, tail_inner, tail_proj = (
        from_root(through.astype(jnp.bfloat16), "prompt", last_index).astype(through.dtype),
        from_root(own_inner.astype(jnp.bfloat16), "prompt", last_index).astype(own_inner.dtype),
        from_root(own_proj.astype(jnp.bfloat16), "prompt", last_index).astype(own_proj.dtype),
    )
    moved_state, moved_inner = (
        from_root(final_state.astype(jnp.bfloat16), "comp", owner).astype(final_state.dtype),
        from_root(tail_inner.astype(jnp.bfloat16), "comp", owner).astype(tail_inner.dtype),
    )
    start_state = lax.dynamic_slice_in_dim(moved_state, head_offset, heads_row, 0)
    lead_inner = lax.dynamic_slice_in_dim(
        moved_inner, head_offset * HEAD_WIDTH, heads_row * HEAD_WIDTH, 1
    ).astype(jnp.bfloat16)
    group_row = head_start // heads_group
    b_start = group_row * STATE_WIDTH
    c_start = state_feats + group_row * STATE_WIDTH
    proj_select = jnp.concatenate(
        [
            lax.dynamic_slice_in_dim(completion_projections, b_start, STATE_WIDTH, 2),
            lax.dynamic_slice_in_dim(completion_projections, c_start, STATE_WIDTH, 2),
        ],
        axis=2,
    )
    kernel_select = jnp.concatenate(
        [
            lax.dynamic_slice_in_dim(conv_proj, b_start, STATE_WIDTH, 1),
            lax.dynamic_slice_in_dim(conv_proj, c_start, STATE_WIDTH, 1),
        ],
        axis=1,
    )
    lead_wide = tail_proj.astype(jnp.bfloat16)
    lead_select = jnp.concatenate(
        [
            lax.dynamic_slice_in_dim(lead_wide, b_start, STATE_WIDTH, 1),
            lax.dynamic_slice_in_dim(lead_wide, c_start, STATE_WIDTH, 1),
        ],
        axis=1,
    )
    conv_row = lax.dynamic_slice_in_dim(
        conv_inner, head_start * HEAD_WIDTH, heads_row * HEAD_WIDTH, 1
    )
    rate_row = jnp.exp(lax.dynamic_slice_in_dim(decay_log, head_start, heads_row, 0))
    step_row = jax.nn.softplus(sample_step)
    slot_count = completion_inner.shape[0]
    sample_len = completion_inner.shape[1]
    block_count = sample_len // BLOCK

    def advance(carry, block_in):
        block_out, carry_next = block_scan(
            carry, block_in[0], block_in[1], block_in[2], block_in[3], rate_row[None]
        )
        return (carry_next, block_out)

    gated_list = []
    square_list = []
    for slot in range(slot_count):
        slot_conv = causal_conv(completion_inner[slot], conv_row, lead_inner)
        proj_conv = causal_conv(proj_select[slot], kernel_select, lead_select)
        inner_blocks = slot_conv.reshape(block_count, BLOCK, 1, heads_row, HEAD_WIDTH)
        b_blocks = proj_conv[:, :STATE_WIDTH].reshape(block_count, BLOCK, 1, STATE_WIDTH)
        c_blocks = proj_conv[:, STATE_WIDTH:].reshape(block_count, BLOCK, 1, STATE_WIDTH)
        step_blocks = jnp.transpose(
            step_row[:, slot].reshape(heads_row, block_count, BLOCK), (1, 0, 2)
        )[:, None]
        block_inputs = (inner_blocks, b_blocks, c_blocks, step_blocks)
        _, block_outs = lax.scan(advance, start_state[None], block_inputs)
        ssm_out = block_outs.reshape(sample_len, heads_row * HEAD_WIDTH)
        gated = ssm_out * jax.nn.silu(completion_gate[slot].astype(jnp.float32))
        gated_list.append(gated)
        square_list.append(jnp.sum(gated * gated, axis=1))
    square_all = jnp.stack(square_list)
    partner_bits = (prompt_count // STATE_GROUPS).bit_length() - 1
    for bit_number in range(partner_bits):
        square_all = square_all + from_partner(square_all, "prompt", bit_number)
    scale_all = lax.rsqrt(square_all / (heads_group * HEAD_WIDTH) + EPS)
    gated_all = jnp.stack(gated_list)
    result = gated_all * scale_all[:, :, None] * norm_gain[None, None, :]
    live_rows = jnp.arange(sample_len)[None, :] < sample_length[:, None]
    return jnp.where(live_rows[:, :, None], result, 0.0).astype(jnp.bfloat16)


LOG2E = 1.4426950408889634
AXES = ("prompt", "comp")
CHUNKS = (1, 1)
PIECES = 1
TAIL = 16
VMEM_BYTES = 16 * 1024 * 1024


def routed(block, route):
    columns = lax.axis_size("comp")
    pairs = []
    for row in range(lax.axis_size("prompt")):
        for column in range(columns):
            target = route(row // 2, row % 2, column)
            if target is not None:
                plane, core, to = target
                pairs.append((row * columns + column, (2 * plane + core) * columns + to))
    return lax.ppermute(block, AXES, pairs)


def half_silu(value):
    return 0.5 * value * (1.0 + jnp.tanh(0.5 * value))


def conv_rows(taps, lead, block):
    wide = taps.astype(jnp.float32)
    rows = block.astype(jnp.float32)
    edge = jnp.concatenate([lead.astype(jnp.float32)[TAIL - 8 :], rows[0:8]], axis=0)
    total = wide[CONV - 1 : CONV] * rows
    for back in range(1, CONV):
        shifted = pltpu.roll(rows, back, 0)
        shifted = jnp.concatenate([edge[8 - back : 16 - back], shifted[8:]], axis=0)
        total = total + wide[CONV - 1 - back : CONV - back] * shifted
    return half_silu(total)


def spread_heads(first, heads, width):
    row = lax.broadcasted_iota(jnp.int32, (heads, width), 0)
    col = lax.broadcasted_iota(jnp.int32, (heads, width), 1)
    return row == first + col // HEAD_WIDTH


def contract(lhs, rhs, dims, precision=None):
    return lax.dot_general(
        lhs, rhs, (dims, ((), ())), preferred_element_type=jnp.float32, precision=precision
    )


def softplus(value):
    return jnp.maximum(value, 0.0) + jnp.log1p(jnp.exp(-jnp.abs(value)))


def group_of(decay, index, size):
    every = jnp.reshape(decay[...], (1, decay.shape[0]))
    return pltpu.roll(every, decay.shape[0] - index * size, 1)[:, 0:size]


def pack_kernel(
    place, inner, proj, step, swap_out, edge_out, own_out, step_in, inner_in, b_in, c_in, sems
):
    heads, rows = step_in.shape
    features = heads * HEAD_WIDTH
    column, core = place[1], place[2]
    theirs = 1 - core
    pair = 2 * STATE_WIDTH

    def columns(first, size):
        return pl.ds(pl.multiple_of(first * size, size), size)

    last = slice(rows - TAIL, rows)
    copies = [
        (step.at[columns(theirs, heads)], step_in),
        (inner.at[last], inner_in),
        (proj.at[last, columns(column, pair)], b_in),
        (proj.at[last, columns(STATE_GROUPS // 2 + column, pair)], c_in),
        (proj.at[:, columns(2 * column + theirs, STATE_WIDTH)], swap_out.at[0:rows, 0:STATE_WIDTH]),
        (proj.at[:, columns(2 * column + core, STATE_WIDTH)], own_out),
    ]
    copies = [
        pltpu.make_async_copy(source, target, sems.at[index])
        for index, (source, target) in enumerate(copies)
    ]
    for copy in copies:
        copy.start()
    for copy in copies:
        copy.wait()
    dt = jnp.transpose(softplus(step_in[...]))
    high = dt.astype(jnp.bfloat16)
    low = (dt - high.astype(jnp.float32)).astype(jnp.bfloat16)
    swap_out[0:rows, STATE_WIDTH:pair] = jnp.concatenate([high, low] * (STATE_WIDTH // heads // 2), axis=1)
    edges = []
    for to in range(2):
        group = slice(to * STATE_WIDTH, (to + 1) * STATE_WIDTH)
        inner_last = inner_in[:, to * features : (to + 1) * features].astype(jnp.float32)
        bc_last = jnp.concatenate([b_in[:, group], c_in[:, group]], axis=1)
        pieces = [inner_last[TAIL - 3 :, at : at + pair] for at in range(0, features, pair)]
        pieces.append(bc_last.astype(jnp.float32)[TAIL - 3 :])
        pieces.append(jnp.zeros((TAIL - 3 * len(pieces), pair), jnp.float32))
        edges.append(jnp.concatenate(pieces, axis=0))
    swap_out[rows:] = jnp.where(core == 0, edges[1], edges[0]).astype(jnp.bfloat16)
    edge_out[...] = edges[1].astype(jnp.bfloat16)


def prompt_weights_kernel(
    place, own, other, taps_b, step, decay, w_out, b_out, log_out, first_out
):
    rows = own.shape[0]
    heads = step.shape[0] // 2
    group = 2 * place[1] + place[2]
    own_b = own[...]
    other_b = other[0:rows, 0:STATE_WIDTH]
    other_dt = other[0:rows, STATE_WIDTH : STATE_WIDTH + 2 * heads]
    taps = taps_b[:, pl.ds(pl.multiple_of(group * STATE_WIDTH, STATE_WIDTH), STATE_WIDTH)]
    own_step = step[pl.ds(pl.multiple_of(place[2] * heads, heads), heads)]
    core = place[2]
    first_own = core == 0
    rate = jnp.exp(group_of(decay, 2 * place[1] + core, heads))
    dt_own = jnp.transpose(softplus(own_step))
    parts = other_dt.astype(jnp.float32)
    dt_other = parts[:, 0:heads] + parts[:, heads : 2 * heads]
    row = lax.broadcasted_iota(jnp.int32, (rows, rows), 0)
    col = lax.broadcasted_iota(jnp.int32, (rows, rows), 1)
    later = (col > row).astype(jnp.float32)
    after = contract(later, jnp.concatenate([dt_own, dt_other], axis=1), ((1,), (0,)), HIGHEST)
    sum_own = after[0:1, 0:heads] + dt_own[0:1]
    sum_other = after[0:1, heads:] + dt_other[0:1]
    after_own = after[:, 0:heads] + jnp.where(first_own, sum_other, 0.0)
    after_other = after[:, heads:] + jnp.where(first_own, 0.0, sum_own)
    w_out[0:rows] = jnp.exp(-rate * after_own) * dt_own
    w_out[rows:] = jnp.exp(-rate * after_other) * dt_other
    total = jnp.broadcast_to(-rate * (sum_own + sum_other), (8, heads))
    spread = spread_heads(0, heads, heads * HEAD_WIDTH).astype(jnp.bfloat16)
    which = lax.broadcasted_iota(jnp.int32, total.shape, 0)
    high = total.astype(jnp.bfloat16).astype(jnp.float32)
    mid = (total - high).astype(jnp.bfloat16).astype(jnp.float32)
    low = total - high - mid
    parts = jnp.where(which == 0, high, jnp.where(which == 1, mid, jnp.where(which == 2, low, 0.0)))
    wide = contract(parts.astype(jnp.bfloat16), spread, ((1,), (0,)))
    log_out[...] = jnp.concatenate([wide, jnp.zeros_like(wide)], axis=0).astype(jnp.bfloat16)
    own_last, other_last = own_b[rows - TAIL :], other_b[rows - TAIL :]
    first = jnp.where(first_own, own_b[0:TAIL].astype(jnp.float32), other_b[0:TAIL].astype(jnp.float32))
    first_out[...] = first.astype(jnp.bfloat16)
    blank = jnp.zeros((TAIL, STATE_WIDTH), jnp.float32)
    lead_own = jnp.where(first_own, blank, other_last.astype(jnp.float32))
    lead_other = jnp.where(first_own, own_last.astype(jnp.float32), blank)
    conv_own = conv_rows(taps, lead_own, own_b)
    b_out[:, 0:rows] = jnp.transpose(conv_own).astype(jnp.bfloat16)
    conv_other = conv_rows(taps, lead_other, other_b)
    b_out[:, rows:] = jnp.transpose(conv_other).astype(jnp.bfloat16)


def prompt_state_kernel(
    offset, parts, place, inner, other, near, taps, taps_b, weights, b_turned, b_first, logs, tail,
    *rest,
):
    outs, b_here = rest[:parts], rest[-1]
    column, core = place[1], place[2]
    group = 2 * column + core
    first_own = core == 0
    rows = inner.shape[0]
    width = outs[0].shape[1]
    heads = weights.shape[1]
    features = heads * HEAD_WIDTH
    part_width = features // parts
    state = b_turned.shape[0]
    w = weights[...].astype(jnp.bfloat16)
    before = jnp.where(place[0] == 0, 0.0, near[...].astype(jnp.float32))
    blank = jnp.zeros((TAIL - 3, STATE_WIDTH), jnp.float32)
    lead_b = jnp.concatenate([blank, before[3 * parts : 3 * parts + 3, 0:STATE_WIDTH]], axis=0)
    taps_here = taps_b[:, pl.ds(pl.multiple_of(group * STATE_WIDTH, STATE_WIDTH), STATE_WIDTH)]
    fresh = conv_rows(taps_here, lead_b, b_first[...])
    fresh = jnp.transpose(jnp.concatenate([fresh, jnp.zeros((128 - TAIL, state), jnp.float32)], axis=0))
    lane = lax.broadcasted_iota(jnp.int32, fresh.shape, 1)
    for index, first in enumerate((core == 0, core == 1)):
        at = index * rows
        old = b_turned[:, at : at + 128].astype(jnp.float32)
        patched = jnp.where(lane < jnp.where(first, CONV - 1, 0), fresh, old)
        b_here[:, at : at + 128] = patched.astype(jnp.bfloat16)
        b_here[:, at + 128 : at + rows] = b_turned[:, at + 128 : at + rows]
    blank = jnp.zeros((TAIL - 3, width), jnp.float32)
    for turn in range(parts):
        part = column ^ turn
        start = part * part_width + offset
        cols = pl.ds(pl.multiple_of(start, 128), width)
        tap_cols = pl.ds(pl.multiple_of(group * features + start, 128), width)
        spread = spread_heads(start // HEAD_WIDTH, heads, width).astype(jnp.bfloat16)
        w_wide = contract(w, spread, ((1,), (0,)))
        own_cols = pl.ds(pl.multiple_of(core * features + start, 128), width)
        own_x, other_x = inner[:, own_cols], other[:, own_cols]
        halo = before[0:3, offset : offset + width]
        for index in range(1, parts):
            at = before[3 * index : 3 * index + 3, offset : offset + width]
            halo = jnp.where(part == index, at, halo)
        halo = jnp.concatenate([blank, halo], axis=0)
        own_last, other_last = own_x[rows - TAIL :], other_x[rows - TAIL :]
        lead_own = jnp.where(first_own, halo, other_last.astype(jnp.float32))
        lead_other = jnp.where(first_own, own_last.astype(jnp.float32), halo)
        x_own = conv_rows(taps[:, tap_cols], lead_own, own_x) * w_wide[0:rows]
        x_other = conv_rows(taps[:, tap_cols], lead_other, other_x) * w_wide[rows:]
        mine = contract(b_here[:, 0:rows], x_own.astype(jnp.bfloat16), ((1,), (0,)))
        theirs = contract(b_here[:, rows:], x_other.astype(jnp.bfloat16), ((1,), (0,)))
        outs[turn][0:state] = (mine + theirs).astype(jnp.bfloat16)
        outs[turn][state : state + TAIL] = logs[:, cols]
        if outs[turn].shape[0] > state + TAIL:
            for index in range(tail.shape[1] // width):
                at = state + TAIL * (index + 1)
                outs[turn][at : at + TAIL] = tail[:, index * width : (index + 1) * width]


def pick_kernel(count, place, after, *refs):
    held, (stays, goes), tails = refs[:count], refs[count : count + 2], refs[count + 2 :]
    turn = place[0] ^ place[1]
    rows, width = stays.shape[1:]
    for index in range(count):

        @pl.when(turn == index)
        def _():
            for step in range(0, count, 2):
                stays[step // 2] = held[index ^ step][0:rows]
                goes[step // 2] = held[index ^ (step + 1)][0:rows]
            for tail in tails:
                for piece in range(tail.shape[1] // width):
                    at = rows + TAIL * piece
                    tail[:, piece * width : (piece + 1) * width] = held[index][at : at + TAIL]


def log_of(message, state):
    rows = message[state:].astype(jnp.float32)
    return rows[0:1] + rows[1:2] + rows[2:3]


def merge_kernel(bit, place, own, came, *refs):
    after, *outs = refs
    state = own.shape[1] - TAIL
    first = (place[0] >> bit) & 1 == 0
    count = own.shape[0]
    for index in range(count):
        mine, theirs = own[index], came[index]
        log_mine, log_theirs = log_of(mine, state), log_of(theirs, state)
        mine_by = jnp.exp(jnp.where(first, log_theirs, 0.0))
        theirs_by = jnp.exp(jnp.where(first, 0.0, log_mine))
        joined = mine[0:state].astype(jnp.float32) * mine_by
        joined = joined + theirs[0:state].astype(jnp.float32) * theirs_by
        if len(outs) == 1:
            outs[0][...] = joined.astype(jnp.bfloat16)
            continue
        out = outs[0] if index < count // 2 else outs[1]
        at = index % (count // 2)
        out[at, 0:state] = joined.astype(jnp.bfloat16)
        total = log_mine + log_theirs
        high = total.astype(jnp.bfloat16)
        rest = total - high.astype(jnp.float32)
        mid = rest.astype(jnp.bfloat16)
        low = (rest - mid.astype(jnp.float32)).astype(jnp.bfloat16)
        blank = jnp.zeros((TAIL - 3, total.shape[1]), jnp.float32)
        parts = [part.astype(jnp.float32) for part in (high, mid, low)] + [blank]
        out[at, state:] = jnp.concatenate(parts, axis=0).astype(jnp.bfloat16)


def completion_kernel(
    slot, piece, pieces, place, inner, gate, proj, tail, taps, taps_bc, step, decay, after, *refs
):
    if piece == 0:
        fixed_out, factor_out, c_out, score_out, x_held, gate_held, bc_in, sems = refs
    else:
        _, _, score_in, fixed_out, factor_out, x_held, gate_held = refs
    rows, features = fixed_out.shape
    heads = step.shape[0] // pieces
    first_head = piece * heads
    half = rows // 2
    own = place[3]
    state = STATE_WIDTH
    if piece == 0:
        copies = [
            pltpu.make_async_copy(
                proj.at[slot, :, pl.ds(pl.multiple_of((own + skip) * state, state), state)],
                bc_in.at[index],
                sems.at[index],
            )
            for index, skip in enumerate((0, STATE_GROUPS))
        ]
        for copy in copies:
            copy.start()
    edges = tail[...].astype(jnp.float32)
    pair_width = edges.shape[1]
    blank = jnp.zeros((TAIL - 3, pair_width), jnp.float32)
    row = lax.broadcasted_iota(jnp.int32, (rows, rows), 0)
    col = lax.broadcasted_iota(jnp.int32, (rows, rows), 1)
    dt = softplus(step[first_head : first_head + heads, slot])
    every = heads * pieces
    decay_row = jnp.broadcast_to(group_of(decay, own, every), (8, every))
    decay_col = jnp.transpose(decay_row)[first_head : first_head + heads, 0:1]
    before = (row <= col).astype(jnp.float32)
    cum = contract(dt, before, ((1,), (0,)), HIGHEST) * (-LOG2E * jnp.exp(decay_col))
    log_dt = jnp.log(dt) * LOG2E
    base_rows = cum - log_dt
    cum_cols = jnp.transpose(cum)
    decay_cols = jnp.exp2(cum_cols).astype(jnp.bfloat16)
    blocks = features // pair_width
    for block in range(piece * blocks // pieces, (piece + 1) * blocks // pieces):
        at = block * pair_width
        cols = slice(at, at + pair_width)
        lead = jnp.concatenate([blank, edges[3 * block : 3 * block + 3]], axis=0)
        taps_here = taps[:, pl.ds(pl.multiple_of(own * features + at, pair_width), pair_width)]
        x_held[:, cols] = conv_rows(taps_here, lead, inner[slot, :, cols]).astype(jnp.bfloat16)
        silu_gate = half_silu(gate[slot, :, cols].astype(jnp.float32))
        gate_held[:, cols] = silu_gate
        spread = spread_heads(at // HEAD_WIDTH - first_head, heads, pair_width).astype(jnp.bfloat16)
        decay_wide = contract(decay_cols, spread, ((1,), (0,)))
        factor_out[:, cols] = (decay_wide * silu_gate).astype(jnp.bfloat16)
    if piece == 0:
        for copy in copies:
            copy.wait()
        lead_bc = jnp.concatenate([blank, edges[3 * blocks : 3 * blocks + 3]], axis=0)
        bc = []
        for index, skip in enumerate((0, STATE_GROUPS)):
            taps_here = taps_bc[:, pl.ds(pl.multiple_of((own + skip) * state, state), state)]
            lead = lead_bc[:, index * state : (index + 1) * state]
            bc.append(conv_rows(taps_here, lead, bc_in[index]).astype(jnp.bfloat16))
        c_out[...] = bc[1]
        scores = contract(bc[1], bc[0], ((1,), (1,)))
        scores = jnp.where(row >= col, scores, 0.0)
        score_out[...] = scores
    else:
        scores = score_in[...]
    low, high_left, high_right = scores[0:half, 0:half], scores[half:, 0:half], scores[half:, half:]
    pair = 2 * HEAD_WIDTH
    lane = lax.broadcasted_iota(jnp.int32, (rows, pair), 1)
    for first in range(0, heads, 2):
        at = (first_head + first) * HEAD_WIDTH
        cols = slice(at, at + pair)
        x_pair = x_held[:, cols]
        zero = jnp.zeros_like(x_pair)
        left = jnp.where(lane < HEAD_WIDTH, x_pair, zero)
        right = jnp.where(lane < HEAD_WIDTH, zero, x_pair)
        lows, highs = [], []
        for h in (first, first + 1):
            cc = cum_cols[:, h : h + 1]
            rr, ll = base_rows[h : h + 1], log_dt[h : h + 1]
            grown = jnp.minimum(cc[0:half] - rr[:, 0:half], ll[:, 0:half])
            lows.append((low * jnp.exp2(grown)).astype(jnp.bfloat16))
            grown = jnp.minimum(cc[half:] - rr[:, 0:half], ll[:, 0:half])
            highs.append((high_left * jnp.exp2(grown)).astype(jnp.bfloat16))
            grown = jnp.minimum(cc[half:] - rr[:, half:], ll[:, half:])
            highs.append((high_right * jnp.exp2(grown)).astype(jnp.bfloat16))
        y_low = contract(
            jnp.concatenate(lows, axis=1),
            jnp.concatenate([left[0:half], right[0:half]], axis=0),
            ((1,), (0,)),
        )
        y_high = contract(
            jnp.concatenate(highs, axis=1), jnp.concatenate([left, right], axis=0), ((1,), (0,))
        )
        fixed_out[0:half, cols] = (y_low * gate_held[0:half, cols]).astype(jnp.bfloat16)
        fixed_out[half:, cols] = (y_high * gate_held[half:, cols]).astype(jnp.bfloat16)


def read_slot(parts, offset, column, slot, states, own_work, gated, slot_at):
    c_ref, fixed, factor = own_work[3 * slot : 3 * slot + 3]
    rows, features = fixed.shape
    part_width = features // parts
    width = states[0].shape[1]
    c = c_ref[...]
    total = jnp.zeros((rows, 128), jnp.float32)
    for step in range(parts):
        start = (column ^ step) * part_width + offset
        cols = pl.ds(pl.multiple_of(start, 128), width)
        read = contract(c, states[step][...], ((1,), (0,)))
        weight = factor[:, cols].astype(jnp.float32)
        value = fixed[:, cols].astype(jnp.float32) + read * weight
        gated[slot_at, step] = value
        square = value * value
        for lanes in range(0, width, 128):
            total = total + square[:, lanes : lanes + 128]
    return total


def read_kernel(parts, offset, slots, place, *refs):
    states, own_work, (gated, squares) = refs[:parts], refs[parts:-2], refs[-2:]
    for slot in range(slots):
        squares[slot] = read_slot(parts, offset, place[1], slot, states, own_work, gated, slot)


def finish_kernel(parts, offsets, slots, place, live, gain, *refs):
    chunks = len(offsets)
    inputs, (out, gated, held, sems) = refs[:-4], refs[-4:]
    earlier, inputs = inputs[: 2 * (chunks - 1)], inputs[2 * (chunks - 1) :]
    states, own_work = inputs[:parts], inputs[parts:]
    column = place[1]
    slots, rows, features = held.shape
    part_width = features // parts
    copies = []
    for slot in range(slots):
        total = read_slot(parts, offsets[-1], column, slot, states, own_work, gated, 0)
        for chunk in range(chunks - 1):
            total = total + earlier[2 * chunk + 1][slot]
        scale = lax.rsqrt(jnp.sum(total, axis=1, keepdims=True) / features + EPS)
        alive = lax.broadcasted_iota(jnp.int32, (rows, 1), 0) < live[slot]
        scale = jnp.where(alive, scale, 0.0)
        for step in range(parts):
            for chunk, offset in enumerate(offsets):
                last = chunk + 1 == chunks
                values = gated if last else earlier[2 * chunk]
                width = values.shape[-1]
                start = (column ^ step) * part_width + offset
                cols = pl.ds(pl.multiple_of(start, 128), width)
                gain_here = jnp.reshape(gain[cols], (1, width))
                value = values[0 if last else slot, step]
                held[slot, :, cols] = (value * scale * gain_here).astype(jnp.bfloat16)
            part = pl.ds(pl.multiple_of((column ^ step) * part_width, part_width), part_width)
            copies.append(
                pltpu.make_async_copy(
                    held.at[slot, :, part], out.at[slot, :, part], sems.at[slot * parts + step]
                )
            )
            copies[-1].start()
    for copy in copies:
        copy.wait()


LASTS = dict(
    pack=2, prompt_weights=2, prompt_state=3, pick=1, merge=1, completion=4, read=2, finish=2
)


def matched(
    prompt_inner,
    prompt_proj,
    prompt_step,
    completion_inner,
    completion_gate,
    completion_projections,
    sample_step,
    sample_length,
    decay_log,
    conv_inner,
    conv_proj,
    norm_gain,
):
    parts = lax.axis_size("comp")
    row, column = lax.axis_index("prompt"), lax.axis_index("comp")
    plane, core = row // 2, row % 2
    group = 2 * column + core
    rows = prompt_inner.shape[0]
    heads = sample_step.shape[0]
    features = heads * HEAD_WIDTH
    place = jnp.stack([plane, column, core, row]).astype(jnp.int32)
    bf16, f32 = jnp.bfloat16, jnp.float32

    def take(array, start, size, axis):
        return lax.dynamic_slice_in_dim(array, start, size, axis)

    planes = lax.axis_size("prompt") // 2
    pair_width = 2 * STATE_WIDTH
    edge = jax.ShapeDtypeStruct((TAIL, pair_width), bf16)
    held_inner = pltpu.with_memory_space_constraint(prompt_inner, pltpu.HBM)
    held_proj = pltpu.with_memory_space_constraint(prompt_proj, pltpu.HBM)
    held_step = pltpu.with_memory_space_constraint(prompt_step, pltpu.HBM)

    swap, edge_1, own_b = run_whole(
        pack_kernel,
        "pack",
        (place,),
        (
            jax.ShapeDtypeStruct((rows + TAIL, pair_width), bf16),
            edge,
            jax.ShapeDtypeStruct((rows, STATE_WIDTH), bf16),
        ),
        (held_inner, held_proj, held_step),
        spaces=[pltpu.HBM] * 3,
        scratch=[
            pltpu.VMEM((heads, rows), f32),
            pltpu.VMEM((TAIL, 2 * features), bf16),
            pltpu.VMEM((TAIL, pair_width), bf16),
            pltpu.VMEM((TAIL, pair_width), bf16),
            pltpu.SemaphoreType.DMA((6,)),
        ],
    )
    trade = lambda z, k, c: (z, 1 - k, c)
    other = routed(swap, trade)
    other_inner = routed(prompt_inner, trade)
    edges = jnp.where(core == 0, other[rows:], edge_1)
    near = routed(edges, lambda z, k, c: (z + 1, k, c) if z + 1 < planes else None)
    far = routed(edges, lambda z, k, c: (c, k, c) if z + 1 == planes else None)
    weights, b_turned, logs, b_first = run_whole(
        prompt_weights_kernel,
        "prompt_weights",
        (place,),
        (
            jax.ShapeDtypeStruct((2 * rows, heads), f32),
            jax.ShapeDtypeStruct((STATE_WIDTH, 2 * rows), bf16),
            jax.ShapeDtypeStruct((TAIL, features), bf16),
            jax.ShapeDtypeStruct((TAIL, STATE_WIDTH), bf16),
        ),
        (own_b, other, conv_proj, prompt_step, decay_log),
    )
    unit = features // parts // sum(CHUNKS)
    widths = [unit * size for size in CHUNKS]
    offsets = [sum(widths[:chunk]) for chunk in range(len(widths))]
    picks = []
    for chunk, width in enumerate(widths):
        message = jax.ShapeDtypeStruct((STATE_WIDTH + TAIL, width), bf16)
        with_tail = chunk == 0
        tail_rows = TAIL * (pair_width // width) if with_tail else 0
        spread = jax.ShapeDtypeStruct((STATE_WIDTH + TAIL + tail_rows, width), bf16)
        sent = run_whole(
            lambda *refs, offset=offsets[chunk]: prompt_state_kernel(offset, parts, *refs),
            "prompt_state",
            (place,),
            (spread,) * parts,
            (
                prompt_inner, other_inner, near, conv_inner, conv_proj, weights, b_turned, b_first,
                logs, far,
            ),
            scratch=[pltpu.VMEM((STATE_WIDTH, 2 * rows), bf16)],
        )
        held = [sent[0]] + [
            routed(sent[step], lambda z, k, c: (z, k, c ^ step)) for step in range(1, parts)
        ]
        two = jax.ShapeDtypeStruct((parts // 2,) + message.shape, bf16)
        picks.append(
            lambda after, held=held, two=two, with_tail=with_tail: run_whole(
                lambda *refs: pick_kernel(parts, *refs),
                "pick",
                (place,),
                (two, two) + (edge,) * with_tail,
                [after] + held,
                spaces=[pl.ANY] + [pltpu.VMEM] * parts,
            )
        )

    slots, positions = completion_inner.shape[:2]
    held_projections = pltpu.with_memory_space_constraint(completion_projections, pltpu.HBM)
    wide = jax.ShapeDtypeStruct((positions, features), bf16)
    pieces = PIECES

    def completion(slot, piece, after, begun):
        outs = (wide, wide)
        scratch = [pltpu.VMEM((positions, features), bf16), pltpu.VMEM((positions, features), f32)]
        operands = [
            completion_inner, completion_gate, held_projections, tail, conv_inner, conv_proj,
            sample_step, decay_log, after,
        ]
        if piece == 0:
            outs += (
                jax.ShapeDtypeStruct((positions, STATE_WIDTH), bf16),
                jax.ShapeDtypeStruct((positions, positions), f32),
            )
            scratch += [
                pltpu.VMEM((2, positions, STATE_WIDTH), bf16), pltpu.SemaphoreType.DMA((2,)),
            ]
            aliases = None
        else:
            fixed, factor, c, scores = begun
            aliases = {len(operands) + 1: 0, len(operands) + 2: 1}
            operands += [fixed, factor, scores]
        results = run_whole(
            lambda *refs: completion_kernel(slot, piece, pieces, *refs),
            "completion",
            (place,),
            outs,
            operands,
            spaces=[pltpu.VMEM] * 2
            + [pltpu.HBM]
            + [pltpu.VMEM] * 5
            + [pl.ANY]
            + [pltpu.VMEM] * (len(operands) - 9),
            scratch=scratch,
            aliases=aliases,
        )
        return results if piece == 0 else results + tuple(begun[2:])

    def merge(bit, own, came, shapes, after):
        return run_whole(
            lambda *refs: merge_kernel(bit, *refs),
            "merge",
            (place,),
            shapes,
            (own, came, after),
            spaces=[pltpu.VMEM] * 2 + [pl.ANY],
        )

    def gather(state):
        return [state] + [
            routed(state, lambda z, k, c: (z, k, c ^ step)) for step in range(1, parts)
        ]

    work = [(slot, piece) for slot in range(slots) for piece in range(pieces)]
    begun = {}

    def do_work(after):
        if not work:
            return after
        slot, piece = work.pop(0)
        begun[slot] = completion(slot, piece, after, begun.get(slot))
        return begun[slot][1]

    stays, goes, merged, joined = [], [], [], []
    near_plane = lambda z, k, c: (z ^ 1, k, c)
    far_plane = lambda z, k, c: (z ^ 2, k, c)
    tail, after = None, place
    for chunk in range(len(widths)):
        stay, go, *maybe = picks[chunk](after)
        tail = maybe[0] if maybe else tail
        stays.append(stay)
        goes.append(routed(go, near_plane))
        if chunk + 1 < len(widths):
            after = do_work(go)
    after = go
    for chunk, width in enumerate(widths):
        one = jax.ShapeDtypeStruct((1, STATE_WIDTH + TAIL, width), bf16)
        stay, go = merge(0, stays[chunk], goes[chunk], (one, one), after)
        merged.append((stay, routed(go, far_plane)))
        after = do_work(go) if chunk + 1 < len(widths) else go
    for chunk, width in enumerate(widths):
        state = jax.ShapeDtypeStruct((STATE_WIDTH, width), bf16)
        joined.append(gather(merge(1, *merged[chunk], state, after)))
        after = do_work(joined[-1][0])
    while work:
        after = do_work(after)
    finished = [begun[slot][:3] for slot in range(slots)]
    own_work = [array for fixed, factor, c in finished for array in (c, fixed, factor)]
    earlier = []
    for chunk, width in enumerate(widths[:-1]):
        earlier += run_whole(
            lambda *refs, offset=offsets[chunk]: read_kernel(parts, offset, slots, *refs),
            "read",
            (place,),
            (
                jax.ShapeDtypeStruct((slots, parts, positions, width), f32),
                jax.ShapeDtypeStruct((slots, positions, 128), f32),
            ),
            joined[chunk] + own_work,
        )
    return run_whole(
        lambda *refs: finish_kernel(parts, offsets, slots, *refs),
        "finish",
        (place, sample_length),
        jax.ShapeDtypeStruct((slots, positions, features), bf16),
        [norm_gain] + earlier + joined[-1] + own_work,
        out_spaces=pltpu.HBM,
        scratch=[
            pltpu.VMEM((1, parts, positions, widths[-1]), f32),
            pltpu.VMEM((slots, positions, features), bf16),
            pltpu.SemaphoreType.DMA((slots * parts,)),
        ],
    )


def run_whole(
    kernel, name, place, out_shape, operands, scratch=(), spaces=None, out_spaces=None, aliases=None
):
    vmem = pltpu.VMEM
    spaces = spaces or [vmem] * len(operands)
    out_spaces = out_spaces or jax.tree.map(lambda _: vmem, out_shape)
    return pl.pallas_call(
        kernel,
        out_shape=out_shape,
        in_specs=[pl.BlockSpec(memory_space=pltpu.SMEM)] * len(place)
        + [pl.BlockSpec(memory_space=space) for space in spaces],
        out_specs=jax.tree.map(lambda space: pl.BlockSpec(memory_space=space), out_spaces),
        scratch_shapes=scratch,
        input_output_aliases=aliases or {},
        compiler_params=pltpu.CompilerParams(vmem_limit_bytes=VMEM_BYTES),
        cost_estimate=pl.CostEstimate(
            flops=LASTS[name] * 10**9, transcendentals=0, bytes_accessed=LASTS[name] * 3 * 10**6
        ),
        name=name,
    )(*place, *operands)


def local(*arrays):
    columns, prompts = lax.axis_size("comp"), lax.axis_size("prompt")
    heads_col, heads_row = arrays[2].shape[0], arrays[6].shape[0]
    one_group = heads_row == STATE_HEADS // STATE_GROUPS and heads_col == 2 * heads_row
    if one_group and prompts == 2 * columns and columns & (columns - 1) == 0:
        return matched(*arrays)
    return any_shape(*arrays)


def solution(mesh):
    placed = (
        P("prompt", "comp"),
        P("prompt", None),
        P("comp", "prompt"),
        P("comp", None, "prompt"),
        P("comp", None, "prompt"),
        P("comp", None, None),
        P("prompt", "comp", None),
        P("comp"),
        P(),
        P(),
        P(),
        P("prompt"),
    )
    return jax.shard_map(
        local, mesh=mesh, in_specs=placed, out_specs=P("comp", None, "prompt"), check_vma=False
    )
```

```python
import jax
import jax.numpy as jnp
from jax import lax
from jax.experimental import pallas as pl
from jax.experimental.pallas import tpu as pltpu
from jax.sharding import PartitionSpec as P

STATE_HEADS = 256
HEAD_WIDTH = 64
STATE_WIDTH = 256
STATE_GROUPS = 8
CONV = 4
BLOCK = 128


EPS = 1e-05
HIGHEST = lax.Precision.HIGHEST


def from_behind(block, axis, distance):
    devices = range(lax.axis_size(axis))
    route = [(i - distance, i) for i in devices if i - distance in devices]
    return lax.ppermute(block, axis, route)


def carried_in(array, axis, combine, identity):
    peers, position = (lax.axis_size(axis), lax.axis_index(axis))
    everything = jax.tree.map(
        lambda part, kind: lax.all_gather(part.astype(kind), axis),
        array,
        (jnp.bfloat16, jnp.bfloat16),
    )
    start = jax.tree.map(
        lambda part, zero: jnp.broadcast_to(jnp.asarray(zero, part.dtype), part.shape),
        array,
        identity,
    )

    def hop(k, before):
        reached = k < position
        new = combine(
            before, jax.tree.map(lambda part, own: part[k].astype(own.dtype), everything, array)
        )
        return jax.tree.map(lambda a, b: jnp.where(reached, a, b), new, before)

    return lax.fori_loop(0, peers, hop, start)


def from_root(array, axis, root):
    mine = lax.axis_index(axis) == root
    return lax.psum(jnp.where(mine, array, jnp.zeros_like(array)), axis)


def from_partner(block, axis, stride):
    count = lax.axis_size(axis)
    route = []
    for low in range(count):
        high = low | 1 << stride
        if high != low and high < count:
            route += [(low, high), (high, low)]
    return lax.ppermute(block, axis, route)


def causal_conv(source, kernel, leading):
    padded = jnp.concatenate([leading, source], axis=0).astype(jnp.float32)
    kernel_wide = kernel.astype(jnp.float32)
    row_count = source.shape[0]
    summed = jnp.zeros(source.shape, jnp.float32)
    for offset in range(kernel.shape[0]):
        summed = summed + kernel_wide[offset] * padded[offset : offset + row_count]
    return jax.nn.silu(summed).astype(jnp.bfloat16)


def block_scan(state_in, inner_blk, b_blk, c_blk, step_blk, rate_vals):
    cumul = jnp.cumsum(-rate_vals[:, :, None] * step_blk, axis=2)
    scores = jnp.einsum("ign,jgn->gij", c_blk, b_blk, preferred_element_type=jnp.float32)
    spread_log = cumul[:, :, :, None] - cumul[:, :, None, :]
    length_q = step_blk.shape[2]
    causal = jnp.arange(length_q)[:, None] >= jnp.arange(length_q)[None, :]
    decay_mat = jnp.exp(jnp.where(causal, spread_log, -jnp.inf))
    mixer_w = (scores[:, None] * decay_mat * step_blk[:, :, None, :]).astype(jnp.bfloat16)
    intra_part = jnp.einsum(
        "gkij,jgkd->igkd", mixer_w, inner_blk, preferred_element_type=jnp.float32
    )
    readout = jnp.einsum("ign,gkdn->igkd", c_blk.astype(jnp.float32), state_in, precision=HIGHEST)
    inter_part = jnp.transpose(jnp.exp(cumul), (2, 0, 1))[..., None] * readout
    weights = jnp.exp(cumul[:, :, -1:] - cumul) * step_blk
    packed = (inner_blk.astype(jnp.float32) * jnp.transpose(weights, (2, 0, 1))[..., None]).astype(
        jnp.bfloat16
    )
    fresh_part = jnp.einsum("jgn,jgkd->gkdn", b_blk, packed, preferred_element_type=jnp.float32)
    return (
        intra_part + inter_part,
        jnp.exp(cumul[:, :, -1])[..., None, None] * state_in + fresh_part,
    )


def any_shape(
    prompt_inner,
    prompt_proj,
    prompt_step,
    completion_inner,
    completion_gate,
    completion_projections,
    sample_step,
    sample_length,
    decay_log,
    conv_inner,
    conv_proj,
    norm_gain,
):
    prompt_count = lax.axis_size("prompt")
    prompt_idx = lax.axis_index("prompt")
    column_idx = lax.axis_index("comp")
    heads_group = STATE_HEADS // STATE_GROUPS
    heads_col = prompt_step.shape[0]
    heads_row = sample_step.shape[0]
    state_feats = STATE_GROUPS * STATE_WIDTH
    lag_rows = CONV - 1
    rows_prompt = prompt_inner.shape[0]
    prev_inner, prev_proj = from_behind(
        (
            prompt_inner[rows_prompt - lag_rows :],
            prompt_proj[rows_prompt - lag_rows :, :state_feats],
        ),
        "prompt",
        1,
    )
    col_start = column_idx * heads_col
    conv_col = lax.dynamic_slice_in_dim(
        conv_inner, col_start * HEAD_WIDTH, heads_col * HEAD_WIDTH, 1
    )
    inner_conv = causal_conv(prompt_inner, conv_col, prev_inner)
    b_conv = causal_conv(prompt_proj[:, :state_feats], conv_proj[:, :state_feats], prev_proj)
    rate_col = jnp.exp(lax.dynamic_slice_in_dim(decay_log, col_start, heads_col, 0))
    step_col = jax.nn.softplus(prompt_step)
    cumul = jnp.cumsum(-rate_col[:, None] * step_col, axis=1)
    local_log = cumul[:, -1]
    weight_col = jnp.exp(local_log[:, None] - cumul) * step_col
    group_span = max(1, heads_col // heads_group)
    per_group = heads_col // group_span
    group_start = col_start // heads_group
    b_select = lax.dynamic_slice_in_dim(
        b_conv.reshape(rows_prompt, STATE_GROUPS, STATE_WIDTH), group_start, group_span, 1
    ).astype(jnp.float32)
    scaled = (
        inner_conv.astype(jnp.float32).reshape(rows_prompt, heads_col, HEAD_WIDTH)
        * jnp.transpose(weight_col)[:, :, None]
    )
    scaled = scaled.reshape(rows_prompt, group_span, per_group, HEAD_WIDTH)
    local_state = jnp.einsum("tgn,tghd->ghdn", b_select, scaled, precision=HIGHEST).reshape(
        heads_col, HEAD_WIDTH, STATE_WIDTH
    )
    own_inner = prompt_inner[rows_prompt - lag_rows :].astype(jnp.float32)
    own_proj = prompt_proj[rows_prompt - lag_rows :].astype(jnp.float32)
    last_index = prompt_count - 1
    head_start = prompt_idx * heads_row
    owner = head_start // heads_col
    head_offset = head_start - owner * heads_col

    def combine(earlier, later):
        return (earlier[0] + later[0], earlier[1] * jnp.exp(later[0])[:, None, None] + later[1])

    before = carried_in(
        (local_log, local_state),
        "prompt",
        combine,
        (jnp.zeros_like(local_log), jnp.zeros_like(local_state)),
    )
    through = combine(before, (local_log, local_state))[1]
    final_state, tail_inner, tail_proj = (
        from_root(through.astype(jnp.bfloat16), "prompt", last_index).astype(through.dtype),
        from_root(own_inner.astype(jnp.bfloat16), "prompt", last_index).astype(own_inner.dtype),
        from_root(own_proj.astype(jnp.bfloat16), "prompt", last_index).astype(own_proj.dtype),
    )
    moved_state, moved_inner = (
        from_root(final_state.astype(jnp.bfloat16), "comp", owner).astype(final_state.dtype),
        from_root(tail_inner.astype(jnp.bfloat16), "comp", owner).astype(tail_inner.dtype),
    )
    start_state = lax.dynamic_slice_in_dim(moved_state, head_offset, heads_row, 0)
    lead_inner = lax.dynamic_slice_in_dim(
        moved_inner, head_offset * HEAD_WIDTH, heads_row * HEAD_WIDTH, 1
    ).astype(jnp.bfloat16)
    group_row = head_start // heads_group
    b_start = group_row * STATE_WIDTH
    c_start = state_feats + group_row * STATE_WIDTH
    proj_select = jnp.concatenate(
        [
            lax.dynamic_slice_in_dim(completion_projections, b_start, STATE_WIDTH, 2),
            lax.dynamic_slice_in_dim(completion_projections, c_start, STATE_WIDTH, 2),
        ],
        axis=2,
    )
    kernel_select = jnp.concatenate(
        [
            lax.dynamic_slice_in_dim(conv_proj, b_start, STATE_WIDTH, 1),
            lax.dynamic_slice_in_dim(conv_proj, c_start, STATE_WIDTH, 1),
        ],
        axis=1,
    )
    lead_wide = tail_proj.astype(jnp.bfloat16)
    lead_select = jnp.concatenate(
        [
            lax.dynamic_slice_in_dim(lead_wide, b_start, STATE_WIDTH, 1),
            lax.dynamic_slice_in_dim(lead_wide, c_start, STATE_WIDTH, 1),
        ],
        axis=1,
    )
    conv_row = lax.dynamic_slice_in_dim(
        conv_inner, head_start * HEAD_WIDTH, heads_row * HEAD_WIDTH, 1
    )
    rate_row = jnp.exp(lax.dynamic_slice_in_dim(decay_log, head_start, heads_row, 0))
    step_row = jax.nn.softplus(sample_step)
    slot_count = completion_inner.shape[0]
    sample_len = completion_inner.shape[1]
    block_count = sample_len // BLOCK

    def advance(carry, block_in):
        block_out, carry_next = block_scan(
            carry, block_in[0], block_in[1], block_in[2], block_in[3], rate_row[None]
        )
        return (carry_next, block_out)

    gated_list = []
    square_list = []
    for slot in range(slot_count):
        slot_conv = causal_conv(completion_inner[slot], conv_row, lead_inner)
        proj_conv = causal_conv(proj_select[slot], kernel_select, lead_select)
        inner_blocks = slot_conv.reshape(block_count, BLOCK, 1, heads_row, HEAD_WIDTH)
        b_blocks = proj_conv[:, :STATE_WIDTH].reshape(block_count, BLOCK, 1, STATE_WIDTH)
        c_blocks = proj_conv[:, STATE_WIDTH:].reshape(block_count, BLOCK, 1, STATE_WIDTH)
        step_blocks = jnp.transpose(
            step_row[:, slot].reshape(heads_row, block_count, BLOCK), (1, 0, 2)
        )[:, None]
        block_inputs = (inner_blocks, b_blocks, c_blocks, step_blocks)
        _, block_outs = lax.scan(advance, start_state[None], block_inputs)
        ssm_out = block_outs.reshape(sample_len, heads_row * HEAD_WIDTH)
        gated = ssm_out * jax.nn.silu(completion_gate[slot].astype(jnp.float32))
        gated_list.append(gated)
        square_list.append(jnp.sum(gated * gated, axis=1))
    square_all = jnp.stack(square_list)
    partner_bits = (prompt_count // STATE_GROUPS).bit_length() - 1
    for bit_number in range(partner_bits):
        square_all = square_all + from_partner(square_all, "prompt", bit_number)
    scale_all = lax.rsqrt(square_all / (heads_group * HEAD_WIDTH) + EPS)
    gated_all = jnp.stack(gated_list)
    result = gated_all * scale_all[:, :, None] * norm_gain[None, None, :]
    live_rows = jnp.arange(sample_len)[None, :] < sample_length[:, None]
    return jnp.where(live_rows[:, :, None], result, 0.0).astype(jnp.bfloat16)


LOG2E = 1.4426950408889634
AXES = ("prompt", "comp")
CHUNKS = (1, 1)
LOG_LANES = 32
TAIL = 16
VMEM_BYTES = 16 * 1024 * 1024


def routed(block, route):
    columns = lax.axis_size("comp")
    pairs = []
    for row in range(lax.axis_size("prompt")):
        for column in range(columns):
            target = route(row // 2, row % 2, column)
            if target is not None:
                plane, core, to = target
                pairs.append((row * columns + column, (2 * plane + core) * columns + to))
    return lax.ppermute(block, AXES, pairs)


def half_silu(value):
    return 0.5 * value * (1.0 + jnp.tanh(0.5 * value))


def conv_rows(taps, lead, block):
    wide = taps.astype(jnp.float32)
    rows = block.astype(jnp.float32)
    edge = jnp.concatenate([lead.astype(jnp.float32)[TAIL - 8 :], rows[0:8]], axis=0)
    total = wide[CONV - 1 : CONV] * rows
    for back in range(1, CONV):
        shifted = pltpu.roll(rows, back, 0)
        shifted = jnp.concatenate([edge[8 - back : 16 - back], shifted[8:]], axis=0)
        total = total + wide[CONV - 1 - back : CONV - back] * shifted
    return half_silu(total)


def spread_heads(first, heads, width):
    row = lax.broadcasted_iota(jnp.int32, (heads, width), 0)
    col = lax.broadcasted_iota(jnp.int32, (heads, width), 1)
    return row == first + col // HEAD_WIDTH


def contract(lhs, rhs, dims, precision=None):
    return lax.dot_general(
        lhs, rhs, (dims, ((), ())), preferred_element_type=jnp.float32, precision=precision
    )


def softplus(value):
    return jnp.maximum(value, 0.0) + jnp.log1p(jnp.exp(-jnp.abs(value)))


def group_of(decay, index, size):
    every = jnp.reshape(decay[...], (1, decay.shape[0]))
    return pltpu.roll(every, decay.shape[0] - index * size, 1)[:, 0:size]


def pack_kernel(
    place, inner, proj, step, swap_out, edge_out, own_out, step_in, inner_in, b_in, c_in, sems
):
    heads, rows = step_in.shape
    features = heads * HEAD_WIDTH
    column, core = place[1], place[2]
    theirs = 1 - core
    pair = 2 * STATE_WIDTH

    def columns(first, size):
        return pl.ds(pl.multiple_of(first * size, size), size)

    last = slice(rows - TAIL, rows)
    copies = [
        (step.at[columns(theirs, heads)], step_in),
        (inner.at[last], inner_in),
        (proj.at[last, columns(column, pair)], b_in),
        (proj.at[last, columns(STATE_GROUPS // 2 + column, pair)], c_in),
        (proj.at[:, columns(2 * column + theirs, STATE_WIDTH)], swap_out.at[0:rows, 0:STATE_WIDTH]),
        (proj.at[:, columns(2 * column + core, STATE_WIDTH)], own_out),
    ]
    copies = [
        pltpu.make_async_copy(source, target, sems.at[index])
        for index, (source, target) in enumerate(copies)
    ]
    for copy in copies:
        copy.start()
    for copy in copies:
        copy.wait()
    dt = jnp.transpose(softplus(step_in[...]))
    high = dt.astype(jnp.bfloat16)
    low = (dt - high.astype(jnp.float32)).astype(jnp.bfloat16)
    swap_out[0:rows, STATE_WIDTH:pair] = jnp.concatenate([high, low] * (STATE_WIDTH // heads // 2), axis=1)
    edges = []
    for to in range(2):
        group = slice(to * STATE_WIDTH, (to + 1) * STATE_WIDTH)
        inner_last = inner_in[:, to * features : (to + 1) * features].astype(jnp.float32)
        bc_last = jnp.concatenate([b_in[:, group], c_in[:, group]], axis=1)
        pieces = [inner_last[TAIL - 3 :, at : at + pair] for at in range(0, features, pair)]
        pieces.append(bc_last.astype(jnp.float32)[TAIL - 3 :])
        pieces.append(jnp.zeros((TAIL - 3 * len(pieces), pair), jnp.float32))
        edges.append(jnp.concatenate(pieces, axis=0))
    swap_out[rows:] = jnp.where(core == 0, edges[1], edges[0]).astype(jnp.bfloat16)
    edge_out[...] = edges[1].astype(jnp.bfloat16)


def log_lanes(high, low):
    lane = lax.broadcasted_iota(jnp.int32, high.shape, 1)
    return jnp.where(lane % LOG_LANES < LOG_LANES // 2, high, low)


def logs_of(tiles, width):
    rows = [tile.astype(jnp.float32)[TAIL - 1 : TAIL] for tile in tiles]
    lanes = rows[0].shape[1]
    rows.append(jnp.zeros((8 - len(rows), lanes), jnp.float32))
    source = lax.broadcasted_iota(jnp.int32, (lanes, width + lanes), 0)
    target = lax.broadcasted_iota(jnp.int32, (lanes, width + lanes), 1)
    head = jnp.where(target < width, target >> 6, (target - width) >> 5)
    pick = (source >> 5 == head) & ((source & (LOG_LANES // 2 - 1)) == 0)
    rows = jnp.concatenate(rows, axis=0).astype(jnp.bfloat16)
    found = contract(rows, pick.astype(jnp.bfloat16), ((1,), (0,)))
    return found[:, 0:width], found[:, width:]


def prompt_weights_kernel(
    place, own, other, taps_b, step, decay, w_out, b_out, log_out, first_out
):
    rows = own.shape[0]
    heads = step.shape[0] // 2
    group = 2 * place[1] + place[2]
    own_b = own[...]
    other_b = other[0:rows, 0:STATE_WIDTH]
    other_dt = other[0:rows, STATE_WIDTH : STATE_WIDTH + 2 * heads]
    taps = taps_b[:, pl.ds(pl.multiple_of(group * STATE_WIDTH, STATE_WIDTH), STATE_WIDTH)]
    own_step = step[pl.ds(pl.multiple_of(place[2] * heads, heads), heads)]
    core = place[2]
    first_own = core == 0
    rate = jnp.exp(group_of(decay, 2 * place[1] + core, heads))
    dt_own = jnp.transpose(softplus(own_step))
    parts = other_dt.astype(jnp.float32)
    dt_other = parts[:, 0:heads] + parts[:, heads : 2 * heads]
    row = lax.broadcasted_iota(jnp.int32, (rows, rows), 0)
    col = lax.broadcasted_iota(jnp.int32, (rows, rows), 1)
    later = (col > row).astype(jnp.float32)
    after = contract(later, jnp.concatenate([dt_own, dt_other], axis=1), ((1,), (0,)), HIGHEST)
    sum_own = after[0:1, 0:heads] + dt_own[0:1]
    sum_other = after[0:1, heads:] + dt_other[0:1]
    after_own = after[:, 0:heads] + jnp.where(first_own, sum_other, 0.0)
    after_other = after[:, heads:] + jnp.where(first_own, 0.0, sum_own)
    w_out[0:rows] = jnp.exp(-rate * after_own) * dt_own
    w_out[rows:] = jnp.exp(-rate * after_other) * dt_other
    total = jnp.broadcast_to(-rate * (sum_own + sum_other), (8, heads))
    high = total.astype(jnp.bfloat16)
    low = (total - high.astype(jnp.float32)).astype(jnp.bfloat16)
    row = lax.broadcasted_iota(jnp.int32, (heads, heads * LOG_LANES), 0)
    lane = lax.broadcasted_iota(jnp.int32, (heads, heads * LOG_LANES), 1)
    spread = (row == lane // LOG_LANES).astype(jnp.bfloat16)
    log_out[...] = log_lanes(
        contract(high, spread, ((1,), (0,))), contract(low, spread, ((1,), (0,)))
    )
    own_last, other_last = own_b[rows - TAIL :], other_b[rows - TAIL :]
    first = jnp.where(first_own, own_b[0:TAIL].astype(jnp.float32), other_b[0:TAIL].astype(jnp.float32))
    first_out[...] = first.astype(jnp.bfloat16)
    blank = jnp.zeros((TAIL, STATE_WIDTH), jnp.float32)
    lead_own = jnp.where(first_own, blank, other_last.astype(jnp.float32))
    lead_other = jnp.where(first_own, own_last.astype(jnp.float32), blank)
    conv_own = conv_rows(taps, lead_own, own_b)
    b_out[:, 0:rows] = jnp.transpose(conv_own).astype(jnp.bfloat16)
    conv_other = conv_rows(taps, lead_other, other_b)
    b_out[:, rows:] = jnp.transpose(conv_other).astype(jnp.bfloat16)


def prompt_state_kernel(
    offset, parts, place, inner, other, near, taps, taps_b, weights, b_turned, b_first, logs, tail,
    *rest,
):
    outs, handed, b_here = rest[:parts], rest[parts:-1], rest[-1]
    column, core = place[1], place[2]
    group = 2 * column + core
    first_own = core == 0
    rows = inner.shape[0]
    width = outs[0].shape[1]
    heads = weights.shape[1]
    features = heads * HEAD_WIDTH
    part_width = features // parts
    state = b_turned.shape[0]
    w = weights[...].astype(jnp.bfloat16)
    before = jnp.where(place[0] == 0, 0.0, near[...].astype(jnp.float32))
    blank = jnp.zeros((TAIL - 3, STATE_WIDTH), jnp.float32)
    lead_b = jnp.concatenate([blank, before[3 * parts : 3 * parts + 3, 0:STATE_WIDTH]], axis=0)
    taps_here = taps_b[:, pl.ds(pl.multiple_of(group * STATE_WIDTH, STATE_WIDTH), STATE_WIDTH)]
    fresh = conv_rows(taps_here, lead_b, b_first[...])
    fresh = jnp.transpose(jnp.concatenate([fresh, jnp.zeros((128 - TAIL, state), jnp.float32)], axis=0))
    lane = lax.broadcasted_iota(jnp.int32, fresh.shape, 1)
    for index, first in enumerate((core == 0, core == 1)):
        at = index * rows
        old = b_turned[:, at : at + 128].astype(jnp.float32)
        patched = jnp.where(lane < jnp.where(first, CONV - 1, 0), fresh, old)
        b_here[:, at : at + 128] = patched.astype(jnp.bfloat16)
        b_here[:, at + 128 : at + rows] = b_turned[:, at + 128 : at + rows]
    blank = jnp.zeros((TAIL - 3, width), jnp.float32)
    for turn in range(parts):
        part = column ^ turn
        start = part * part_width + offset
        cols = pl.ds(pl.multiple_of(start, 128), width)
        tap_cols = pl.ds(pl.multiple_of(group * features + start, 128), width)
        spread = spread_heads(start // HEAD_WIDTH, heads, width).astype(jnp.bfloat16)
        w_wide = contract(w, spread, ((1,), (0,)))
        own_cols = pl.ds(pl.multiple_of(core * features + start, 128), width)
        own_x, other_x = inner[:, own_cols], other[:, own_cols]
        halo = before[0:3, offset : offset + width]
        for index in range(1, parts):
            at = before[3 * index : 3 * index + 3, offset : offset + width]
            halo = jnp.where(part == index, at, halo)
        halo = jnp.concatenate([blank, halo], axis=0)
        own_last, other_last = own_x[rows - TAIL :], other_x[rows - TAIL :]
        lead_own = jnp.where(first_own, halo, other_last.astype(jnp.float32))
        lead_other = jnp.where(first_own, own_last.astype(jnp.float32), halo)
        x_own = conv_rows(taps[:, tap_cols], lead_own, own_x) * w_wide[0:rows]
        x_other = conv_rows(taps[:, tap_cols], lead_other, other_x) * w_wide[rows:]
        mine = contract(b_here[:, 0:rows], x_own.astype(jnp.bfloat16), ((1,), (0,)))
        theirs = contract(b_here[:, rows:], x_other.astype(jnp.bfloat16), ((1,), (0,)))
        outs[turn][0:state] = (mine + theirs).astype(jnp.bfloat16)
        if outs[turn].shape[0] > state:
            log_width = part_width * LOG_LANES // HEAD_WIDTH
            at = pl.ds(pl.multiple_of(part * log_width, log_width), log_width)
            pieces = tail[:, 0:width].astype(jnp.float32)
            row = lax.broadcasted_iota(jnp.int32, pieces.shape, 0)
            pieces = jnp.where(row == TAIL - 1, logs[0:1, at], pieces)
            outs[turn][state : state + TAIL] = pieces.astype(jnp.bfloat16)
            outs[turn][state + TAIL :] = tail[:, width:]
    for out in handed:
        out[...] = tail[...]


def pick_kernel(count, place, after, *refs):
    held, (stays, goes), tails = refs[:count], refs[count : count + 2], refs[count + 2 :]
    turn = place[0] ^ place[1]
    rows, width = stays.shape[1:]
    for index in range(count):

        @pl.when(turn == index)
        def _():
            for step in range(0, count, 2):
                stays[step // 2] = held[index ^ step][0:rows]
                goes[step // 2] = held[index ^ (step + 1)][0:rows]
            for tail in tails:
                tail[:, 0:width] = held[index][rows - TAIL : rows]
                tail[:, width:] = held[index][rows:]


def merge_kernel(bit, chunk, place, own, came, given, after, *refs):
    count, rows, width = own.shape
    state = STATE_WIDTH
    first = (place[0] >> bit) & 1 == 0
    outs = refs if chunk else refs[:-1]
    factors = given if chunk else refs[-1]
    if chunk == 0:
        last = slice(rows - TAIL, rows)
        tiles = [ref[index, last] for index in range(count) for ref in (own, came)]
        wide, lanes = logs_of(tiles, factors.shape[1])
        row = lax.broadcasted_iota(jnp.int32, wide.shape, 0)
        other = jnp.where(row % 2 == 0, pltpu.roll(wide, 7, 0), pltpu.roll(wide, 1, 0))
        scaled = (row % 2 == 0) == first
        factors[...] = jnp.exp(jnp.where(scaled, other, 0.0))
    for index in range(count):
        cols = slice(chunk * width, (chunk + 1) * width)
        mine_by = factors[2 * index : 2 * index + 1, cols]
        theirs_by = factors[2 * index + 1 : 2 * index + 2, cols]
        joined = own[index, 0:state].astype(jnp.float32) * mine_by
        joined = joined + came[index, 0:state].astype(jnp.float32) * theirs_by
        if count == 1:
            outs[0][...] = joined.astype(jnp.bfloat16)
            continue
        outs[index][0, 0:state] = joined.astype(jnp.bfloat16)
        if rows > state:
            total = lanes[2 * index : 2 * index + 1] + lanes[2 * index + 1 : 2 * index + 2]
            total = jnp.broadcast_to(total, (8, total.shape[1]))
            high = total.astype(jnp.bfloat16).astype(jnp.float32)
            compact = log_lanes(high, total - high)
            compact = jnp.concatenate([compact, compact], axis=0)
            outs[index][0, state:] = compact.astype(jnp.bfloat16)


def prepare_kernel(
    slot, fetch, place, gate, step, decay, after,
    gate_out, factor_out, cum_out, turned_out, log_out, after_out, *rest,
):
    width = 2 * STATE_WIDTH
    copies = []
    if fetch:
        gate_in, sems = rest
        copies = [
            pltpu.make_async_copy(
                gate.at[slot, :, at : at + width], gate_in.at[:, at : at + width], sems.at[index]
            )
            for index, at in enumerate(range(0, gate.shape[2], width))
        ]
    for copy in copies:
        copy.start()
    after_out[...] = after[...]
    rows, features = gate_out.shape
    heads = step.shape[0]
    row = lax.broadcasted_iota(jnp.int32, (rows, rows), 0)
    col = lax.broadcasted_iota(jnp.int32, (rows, rows), 1)
    dt = softplus(step[:, slot])
    decay_row = jnp.broadcast_to(group_of(decay, place[3], heads), (8, heads))
    decay_col = jnp.transpose(decay_row)[:, 0:1]
    before = (row <= col).astype(jnp.float32)
    cum = contract(dt, before, ((1,), (0,)), HIGHEST) * (-LOG2E * jnp.exp(decay_col))
    log_dt = jnp.log(dt) * LOG2E
    cum_out[...] = cum - log_dt
    log_out[...] = log_dt
    turned = jnp.transpose(cum)
    turned_out[...] = turned
    decays = jnp.exp2(turned).astype(jnp.bfloat16)
    for index, at in enumerate(range(0, features, width)):
        cols = slice(at, at + width)
        if fetch:
            copies[index].wait()
        gate_here = gate_in[:, cols] if fetch else gate[slot, :, cols]
        silu_gate = half_silu(gate_here.astype(jnp.float32))
        gate_out[:, cols] = silu_gate.astype(jnp.bfloat16)
        spread = spread_heads(at // HEAD_WIDTH, heads, width).astype(jnp.bfloat16)
        decay_wide = contract(decays, spread, ((1,), (0,)))
        factor_out[:, cols] = (decay_wide * silu_gate).astype(jnp.bfloat16)


def completion_kernel(
    slot, place, inner, proj, tail, taps, taps_bc, gates, base_rows, cum_cols, log_dt, after,
    fixed_out, c_out, x_held, bc_in, sems,
):
    rows, features = fixed_out.shape
    heads = base_rows.shape[0]
    half = rows // 2
    own = place[3]
    state = STATE_WIDTH
    copies = [
        pltpu.make_async_copy(
            proj.at[slot, :, pl.ds(pl.multiple_of((own + skip) * state, state), state)],
            bc_in.at[index],
            sems.at[index],
        )
        for index, skip in enumerate((0, STATE_GROUPS))
    ]
    for copy in copies:
        copy.start()
    edges = tail[...].astype(jnp.float32)
    pair_width = edges.shape[1]
    blank = jnp.zeros((TAIL - 3, pair_width), jnp.float32)
    row = lax.broadcasted_iota(jnp.int32, (rows, rows), 0)
    col = lax.broadcasted_iota(jnp.int32, (rows, rows), 1)
    blocks = features // pair_width
    for block in range(blocks):
        at = block * pair_width
        cols = slice(at, at + pair_width)
        lead = jnp.concatenate([blank, edges[3 * block : 3 * block + 3]], axis=0)
        taps_here = taps[:, pl.ds(pl.multiple_of(own * features + at, pair_width), pair_width)]
        x_held[:, cols] = conv_rows(taps_here, lead, inner[slot, :, cols]).astype(jnp.bfloat16)
    for copy in copies:
        copy.wait()
    lead_bc = jnp.concatenate([blank, edges[3 * blocks : 3 * blocks + 3]], axis=0)
    bc = []
    for index, skip in enumerate((0, STATE_GROUPS)):
        taps_here = taps_bc[:, pl.ds(pl.multiple_of((own + skip) * state, state), state)]
        lead = lead_bc[:, index * state : (index + 1) * state]
        bc.append(conv_rows(taps_here, lead, bc_in[index]).astype(jnp.bfloat16))
    c_out[...] = bc[1]
    scores = contract(bc[1], bc[0], ((1,), (1,)))
    scores = jnp.where(row >= col, scores, 0.0)
    low, high_left, high_right = scores[0:half, 0:half], scores[half:, 0:half], scores[half:, half:]
    pair = 2 * HEAD_WIDTH
    lane = lax.broadcasted_iota(jnp.int32, (rows, pair), 1)
    for first in range(0, heads, 2):
        cols = slice(first * HEAD_WIDTH, first * HEAD_WIDTH + pair)
        x_pair = x_held[:, cols]
        zero = jnp.zeros_like(x_pair)
        left = jnp.where(lane < HEAD_WIDTH, x_pair, zero)
        right = jnp.where(lane < HEAD_WIDTH, zero, x_pair)
        lows, highs = [], []
        for h in (first, first + 1):
            cc = cum_cols[:, h : h + 1]
            rr, ll = base_rows[h : h + 1], log_dt[h : h + 1]
            grown = jnp.minimum(cc[0:half] - rr[:, 0:half], ll[:, 0:half])
            lows.append((low * jnp.exp2(grown)).astype(jnp.bfloat16))
            grown = jnp.minimum(cc[half:] - rr[:, 0:half], ll[:, 0:half])
            highs.append((high_left * jnp.exp2(grown)).astype(jnp.bfloat16))
            grown = jnp.minimum(cc[half:] - rr[:, half:], ll[:, half:])
            highs.append((high_right * jnp.exp2(grown)).astype(jnp.bfloat16))
        y_low = contract(
            jnp.concatenate(lows, axis=1),
            jnp.concatenate([left[0:half], right[0:half]], axis=0),
            ((1,), (0,)),
        )
        y_high = contract(
            jnp.concatenate(highs, axis=1), jnp.concatenate([left, right], axis=0), ((1,), (0,))
        )
        fixed_out[0:half, cols] = (y_low * gates[0:half, cols].astype(jnp.float32)).astype(jnp.bfloat16)
        fixed_out[half:, cols] = (y_high * gates[half:, cols].astype(jnp.float32)).astype(jnp.bfloat16)


def read_slot(parts, offset, column, slot, states, own_work, gated, slot_at):
    c_ref, fixed, factor = own_work[3 * slot : 3 * slot + 3]
    rows, features = fixed.shape
    part_width = features // parts
    width = states[0].shape[1]
    c = c_ref[...]
    total = jnp.zeros((rows, 128), jnp.float32)
    for step in range(parts):
        start = (column ^ step) * part_width + offset
        cols = pl.ds(pl.multiple_of(start, 128), width)
        read = contract(c, states[step][...], ((1,), (0,)))
        weight = factor[:, cols].astype(jnp.float32)
        value = fixed[:, cols].astype(jnp.float32) + read * weight
        gated[slot_at, step] = value
        square = value * value
        for lanes in range(0, width, 128):
            total = total + square[:, lanes : lanes + 128]
    return total


def read_kernel(parts, offset, slots, place, *refs):
    states, own_work, (gated, squares) = refs[:parts], refs[parts:-2], refs[-2:]
    for slot in range(slots):
        squares[slot] = read_slot(parts, offset, place[1], slot, states, own_work, gated, slot)


def finish_kernel(parts, offsets, slots, place, live, gain, *refs):
    chunks = len(offsets)
    inputs, (out, gated, held, sems) = refs[:-4], refs[-4:]
    earlier, inputs = inputs[: 2 * (chunks - 1)], inputs[2 * (chunks - 1) :]
    states, own_work = inputs[:parts], inputs[parts:]
    column = place[1]
    slots, rows, features = held.shape
    part_width = features // parts
    copies = []
    for slot in range(slots):
        total = read_slot(parts, offsets[-1], column, slot, states, own_work, gated, 0)
        for chunk in range(chunks - 1):
            total = total + earlier[2 * chunk + 1][slot]
        scale = lax.rsqrt(jnp.sum(total, axis=1, keepdims=True) / features + EPS)
        alive = lax.broadcasted_iota(jnp.int32, (rows, 1), 0) < live[slot]
        scale = jnp.where(alive, scale, 0.0)
        for step in range(parts):
            for chunk, offset in enumerate(offsets):
                last = chunk + 1 == chunks
                values = gated if last else earlier[2 * chunk]
                width = values.shape[-1]
                start = (column ^ step) * part_width + offset
                cols = pl.ds(pl.multiple_of(start, 128), width)
                gain_here = jnp.reshape(gain[cols], (1, width))
                value = values[0 if last else slot, step]
                held[slot, :, cols] = (value * scale * gain_here).astype(jnp.bfloat16)
            part = pl.ds(pl.multiple_of((column ^ step) * part_width, part_width), part_width)
            copies.append(
                pltpu.make_async_copy(
                    held.at[slot, :, part], out.at[slot, :, part], sems.at[slot * parts + step]
                )
            )
            copies[-1].start()
    for copy in copies:
        copy.wait()


LASTS = dict(
    pack=2, prompt_weights=2, prompt_state=3, pick=1, merge=1, prepare=0, completion=4, read=2, finish=2
)


def matched(
    prompt_inner,
    prompt_proj,
    prompt_step,
    completion_inner,
    completion_gate,
    completion_projections,
    sample_step,
    sample_length,
    decay_log,
    conv_inner,
    conv_proj,
    norm_gain,
):
    parts = lax.axis_size("comp")
    row, column = lax.axis_index("prompt"), lax.axis_index("comp")
    plane, core = row // 2, row % 2
    group = 2 * column + core
    rows = prompt_inner.shape[0]
    heads = sample_step.shape[0]
    features = heads * HEAD_WIDTH
    place = jnp.stack([plane, column, core, row]).astype(jnp.int32)
    bf16, f32 = jnp.bfloat16, jnp.float32

    def take(array, start, size, axis):
        return lax.dynamic_slice_in_dim(array, start, size, axis)

    planes = lax.axis_size("prompt") // 2
    pair_width = 2 * STATE_WIDTH
    edge = jax.ShapeDtypeStruct((TAIL, pair_width), bf16)
    held_inner = pltpu.with_memory_space_constraint(prompt_inner, pltpu.HBM)
    held_proj = pltpu.with_memory_space_constraint(prompt_proj, pltpu.HBM)
    held_step = pltpu.with_memory_space_constraint(prompt_step, pltpu.HBM)

    swap, edge_1, own_b = run_whole(
        pack_kernel,
        "pack",
        (place,),
        (
            jax.ShapeDtypeStruct((rows + TAIL, pair_width), bf16),
            edge,
            jax.ShapeDtypeStruct((rows, STATE_WIDTH), bf16),
        ),
        (held_inner, held_proj, held_step),
        spaces=[pltpu.HBM] * 3,
        scratch=[
            pltpu.VMEM((heads, rows), f32),
            pltpu.VMEM((TAIL, 2 * features), bf16),
            pltpu.VMEM((TAIL, pair_width), bf16),
            pltpu.VMEM((TAIL, pair_width), bf16),
            pltpu.SemaphoreType.DMA((6,)),
        ],
    )
    trade = lambda z, k, c: (z, 1 - k, c)
    other = routed(swap, trade)
    other_inner = routed(prompt_inner, trade)
    slots, positions = completion_inner.shape[:2]
    wide = jax.ShapeDtypeStruct((positions, features), bf16)
    prepared = {}
    held_gate = pltpu.with_memory_space_constraint(completion_gate, pltpu.HBM)

    def prepare(slot, after, fetch):
        every = jax.ShapeDtypeStruct((heads, positions), f32)
        turned = jax.ShapeDtypeStruct((positions, heads), f32)
        return run_whole(
            lambda *refs: prepare_kernel(slot, fetch, *refs),
            "prepare",
            (place,),
            (wide, wide, every, turned, every, edge),
            (held_gate if fetch else completion_gate, sample_step, decay_log, after),
            spaces=[pltpu.HBM if fetch else pltpu.VMEM] + [pltpu.VMEM] * 3,
            scratch=[
                pltpu.VMEM((positions, features), bf16),
                pltpu.SemaphoreType.DMA((features // pair_width,)),
            ]
            * fetch,
        )

    for slot in range(1, slots):
        *prepared[slot], edge_1 = prepare(slot, edge_1, True)
    edges = jnp.where(core == 0, other[rows:], edge_1)
    near = routed(edges, lambda z, k, c: (z + 1, k, c) if z + 1 < planes else None)
    far = routed(edges, lambda z, k, c: (c, k, c) if z + 1 == planes else None)
    weights, b_turned, logs, b_first = run_whole(
        prompt_weights_kernel,
        "prompt_weights",
        (place,),
        (
            jax.ShapeDtypeStruct((2 * rows, heads), f32),
            jax.ShapeDtypeStruct((STATE_WIDTH, 2 * rows), bf16),
            jax.ShapeDtypeStruct((8, heads * LOG_LANES), f32),
            jax.ShapeDtypeStruct((TAIL, STATE_WIDTH), bf16),
        ),
        (own_b, other, conv_proj, prompt_step, decay_log),
    )
    unit = features // parts // sum(CHUNKS)
    widths = [unit * size for size in CHUNKS]
    offsets = [sum(widths[:chunk]) for chunk in range(len(widths))]
    picks = []
    for chunk, width in enumerate(widths):
        with_tail = chunk == 0
        message = jax.ShapeDtypeStruct((STATE_WIDTH + TAIL * with_tail, width), bf16)
        spread = jax.ShapeDtypeStruct((STATE_WIDTH + 2 * TAIL * with_tail, width), bf16)
        sent = run_whole(
            lambda *refs, offset=offsets[chunk]: prompt_state_kernel(offset, parts, *refs),
            "prompt_state",
            (place,),
            (spread,) * parts + (edge,) * (chunk + 1 == len(widths)),
            (
                prompt_inner, other_inner, near, conv_inner, conv_proj, weights, b_turned, b_first,
                logs, far,
            ),
            scratch=[pltpu.VMEM((STATE_WIDTH, 2 * rows), bf16)],
        )
        if chunk + 1 == len(widths):
            *prepared[0], handed = prepare(0, sent[parts], False)
        held = [sent[0]] + [
            routed(sent[step], lambda z, k, c: (z, k, c ^ step)) for step in range(1, parts)
        ]
        two = jax.ShapeDtypeStruct((parts // 2,) + message.shape, bf16)
        picks.append(
            lambda after, held=held, two=two, with_tail=with_tail: run_whole(
                lambda *refs: pick_kernel(parts, *refs),
                "pick",
                (place,),
                (two, two) + (edge,) * with_tail,
                [after] + held,
                spaces=[pl.ANY] + [pltpu.VMEM] * parts,
            )
        )

    held_projections = pltpu.with_memory_space_constraint(completion_projections, pltpu.HBM)
    def completion(slot, after):
        gates, factor, *decays = prepared[slot]
        fixed, c = run_whole(
            lambda *refs: completion_kernel(slot, *refs),
            "completion",
            (place,),
            (wide, jax.ShapeDtypeStruct((positions, STATE_WIDTH), bf16)),
            (
                completion_inner, held_projections, tail, conv_inner, conv_proj, gates, *decays, after,
            ),
            spaces=[pltpu.VMEM, pltpu.HBM] + [pltpu.VMEM] * 7 + [pl.ANY],
            scratch=[
                pltpu.VMEM((positions, features), bf16),
                pltpu.VMEM((2, positions, STATE_WIDTH), bf16),
                pltpu.SemaphoreType.DMA((2,)),
            ],
        )
        return c, fixed, factor

    def merge(bit, chunk, own, came, shapes, given, after):
        table = jax.ShapeDtypeStruct((8, features // parts), f32)
        *outs, factors = run_whole(
            lambda *refs: merge_kernel(bit, chunk, *refs),
            "merge",
            (place,),
            shapes + (table,) * (chunk == 0),
            (own, came, given, after),
            spaces=[pltpu.VMEM] * 2 + [pltpu.VMEM if chunk else pl.ANY, pl.ANY],
        ) + ((given,) if chunk else ())
        return outs, factors

    def gather(state):
        return [state] + [
            routed(state, lambda z, k, c: (z, k, c ^ step)) for step in range(1, parts)
        ]

    work = list(range(slots))
    finished = []

    def do_work(after):
        if not work:
            return after
        finished.append(completion(work.pop(0), after))
        return finished[-1][0]

    stays, goes, go_shapes, merged, joined = [], [], [], [], []
    near_plane = lambda z, k, c: (z ^ 1, k, c)
    far_plane = lambda z, k, c: (z ^ 2, k, c)
    tail, after = None, handed
    for chunk in range(len(widths)):
        stay, go, *maybe = picks[chunk](after)
        tail = maybe[0] if maybe else tail
        stays.append(stay)
        goes.append(routed(go, near_plane))
        go_shapes.append(go.shape[1:])
        if chunk + 1 < len(widths):
            after = do_work(go)
    given = after = go
    for chunk in range(len(widths)):
        one = jax.ShapeDtypeStruct((1,) + go_shapes[chunk], bf16)
        (stay, go), given = merge(
            0, chunk, stays[chunk], goes[chunk], (one, one), given, after
        )
        merged.append((stay, routed(go, far_plane)))
        after = do_work(go)
    given = go
    for chunk, width in enumerate(widths):
        state = jax.ShapeDtypeStruct((STATE_WIDTH, width), bf16)
        (state,), given = merge(1, chunk, *merged[chunk], (state,), given, go)
        joined.append(gather(state))
    after = state
    while work:
        after = do_work(after)
    own_work = [array for three in finished for array in three]
    earlier = []
    for chunk, width in enumerate(widths[:-1]):
        earlier += run_whole(
            lambda *refs, offset=offsets[chunk]: read_kernel(parts, offset, slots, *refs),
            "read",
            (place,),
            (
                jax.ShapeDtypeStruct((slots, parts, positions, width), f32),
                jax.ShapeDtypeStruct((slots, positions, 128), f32),
            ),
            joined[chunk] + own_work,
        )
    return run_whole(
        lambda *refs: finish_kernel(parts, offsets, slots, *refs),
        "finish",
        (place, sample_length),
        jax.ShapeDtypeStruct((slots, positions, features), bf16),
        [norm_gain] + earlier + joined[-1] + own_work,
        out_spaces=pltpu.HBM,
        scratch=[
            pltpu.VMEM((1, parts, positions, widths[-1]), f32),
            pltpu.VMEM((slots, positions, features), bf16),
            pltpu.SemaphoreType.DMA((slots * parts,)),
        ],
    )


def run_whole(
    kernel, name, place, out_shape, operands, scratch=(), spaces=None, out_spaces=None, aliases=None
):
    vmem = pltpu.VMEM
    spaces = spaces or [vmem] * len(operands)
    out_spaces = out_spaces or jax.tree.map(lambda _: vmem, out_shape)
    return pl.pallas_call(
        kernel,
        out_shape=out_shape,
        in_specs=[pl.BlockSpec(memory_space=pltpu.SMEM)] * len(place)
        + [pl.BlockSpec(memory_space=space) for space in spaces],
        out_specs=jax.tree.map(lambda space: pl.BlockSpec(memory_space=space), out_spaces),
        scratch_shapes=scratch,
        input_output_aliases=aliases or {},
        compiler_params=pltpu.CompilerParams(vmem_limit_bytes=VMEM_BYTES),
        cost_estimate=pl.CostEstimate(
            flops=LASTS[name] * 10**9, transcendentals=0, bytes_accessed=LASTS[name] * 3 * 10**6
        ),
        name=name,
    )(*place, *operands)


def local(*arrays):
    columns, prompts = lax.axis_size("comp"), lax.axis_size("prompt")
    heads_col, heads_row = arrays[2].shape[0], arrays[6].shape[0]
    one_group = heads_row == STATE_HEADS // STATE_GROUPS and heads_col == 2 * heads_row
    if one_group and prompts == 2 * columns and columns & (columns - 1) == 0:
        return matched(*arrays)
    return any_shape(*arrays)


def solution(mesh):
    placed = (
        P("prompt", "comp"),
        P("prompt", None),
        P("comp", "prompt"),
        P("comp", None, "prompt"),
        P("comp", None, "prompt"),
        P("comp", None, None),
        P("prompt", "comp", None),
        P("comp"),
        P(),
        P(),
        P(),
        P("prompt"),
    )
    return jax.shard_map(
        local, mesh=mesh, in_specs=placed, out_specs=P("comp", None, "prompt"), check_vma=False
    )
```

```python
import jax
import jax.numpy as jnp
from jax import lax
from jax.experimental import pallas as pl
from jax.experimental.pallas import tpu as pltpu
from jax.sharding import PartitionSpec as P

STATE_HEADS = 256
HEAD_WIDTH = 64
STATE_WIDTH = 256
STATE_GROUPS = 8
CONV = 4
BLOCK = 128


EPS = 1e-05
HIGHEST = lax.Precision.HIGHEST


def from_behind(block, axis, distance):
    devices = range(lax.axis_size(axis))
    route = [(i - distance, i) for i in devices if i - distance in devices]
    return lax.ppermute(block, axis, route)


def carried_in(array, axis, combine, identity):
    peers, position = (lax.axis_size(axis), lax.axis_index(axis))
    everything = jax.tree.map(
        lambda part, kind: lax.all_gather(part.astype(kind), axis),
        array,
        (jnp.bfloat16, jnp.bfloat16),
    )
    start = jax.tree.map(
        lambda part, zero: jnp.broadcast_to(jnp.asarray(zero, part.dtype), part.shape),
        array,
        identity,
    )

    def hop(k, before):
        reached = k < position
        new = combine(
            before, jax.tree.map(lambda part, own: part[k].astype(own.dtype), everything, array)
        )
        return jax.tree.map(lambda a, b: jnp.where(reached, a, b), new, before)

    return lax.fori_loop(0, peers, hop, start)


def from_root(array, axis, root):
    mine = lax.axis_index(axis) == root
    return lax.psum(jnp.where(mine, array, jnp.zeros_like(array)), axis)


def from_partner(block, axis, stride):
    count = lax.axis_size(axis)
    route = []
    for low in range(count):
        high = low | 1 << stride
        if high != low and high < count:
            route += [(low, high), (high, low)]
    return lax.ppermute(block, axis, route)


def causal_conv(source, kernel, leading):
    padded = jnp.concatenate([leading, source], axis=0).astype(jnp.float32)
    kernel_wide = kernel.astype(jnp.float32)
    row_count = source.shape[0]
    summed = jnp.zeros(source.shape, jnp.float32)
    for offset in range(kernel.shape[0]):
        summed = summed + kernel_wide[offset] * padded[offset : offset + row_count]
    return jax.nn.silu(summed).astype(jnp.bfloat16)


def block_scan(state_in, inner_blk, b_blk, c_blk, step_blk, rate_vals):
    cumul = jnp.cumsum(-rate_vals[:, :, None] * step_blk, axis=2)
    scores = jnp.einsum("ign,jgn->gij", c_blk, b_blk, preferred_element_type=jnp.float32)
    spread_log = cumul[:, :, :, None] - cumul[:, :, None, :]
    length_q = step_blk.shape[2]
    causal = jnp.arange(length_q)[:, None] >= jnp.arange(length_q)[None, :]
    decay_mat = jnp.exp(jnp.where(causal, spread_log, -jnp.inf))
    mixer_w = (scores[:, None] * decay_mat * step_blk[:, :, None, :]).astype(jnp.bfloat16)
    intra_part = jnp.einsum(
        "gkij,jgkd->igkd", mixer_w, inner_blk, preferred_element_type=jnp.float32
    )
    readout = jnp.einsum("ign,gkdn->igkd", c_blk.astype(jnp.float32), state_in, precision=HIGHEST)
    inter_part = jnp.transpose(jnp.exp(cumul), (2, 0, 1))[..., None] * readout
    weights = jnp.exp(cumul[:, :, -1:] - cumul) * step_blk
    packed = (inner_blk.astype(jnp.float32) * jnp.transpose(weights, (2, 0, 1))[..., None]).astype(
        jnp.bfloat16
    )
    fresh_part = jnp.einsum("jgn,jgkd->gkdn", b_blk, packed, preferred_element_type=jnp.float32)
    return (
        intra_part + inter_part,
        jnp.exp(cumul[:, :, -1])[..., None, None] * state_in + fresh_part,
    )


def any_shape(
    prompt_inner,
    prompt_proj,
    prompt_step,
    completion_inner,
    completion_gate,
    completion_projections,
    sample_step,
    sample_length,
    decay_log,
    conv_inner,
    conv_proj,
    norm_gain,
):
    prompt_count = lax.axis_size("prompt")
    prompt_idx = lax.axis_index("prompt")
    column_idx = lax.axis_index("comp")
    heads_group = STATE_HEADS // STATE_GROUPS
    heads_col = prompt_step.shape[0]
    heads_row = sample_step.shape[0]
    state_feats = STATE_GROUPS * STATE_WIDTH
    lag_rows = CONV - 1
    rows_prompt = prompt_inner.shape[0]
    prev_inner, prev_proj = from_behind(
        (
            prompt_inner[rows_prompt - lag_rows :],
            prompt_proj[rows_prompt - lag_rows :, :state_feats],
        ),
        "prompt",
        1,
    )
    col_start = column_idx * heads_col
    conv_col = lax.dynamic_slice_in_dim(
        conv_inner, col_start * HEAD_WIDTH, heads_col * HEAD_WIDTH, 1
    )
    inner_conv = causal_conv(prompt_inner, conv_col, prev_inner)
    b_conv = causal_conv(prompt_proj[:, :state_feats], conv_proj[:, :state_feats], prev_proj)
    rate_col = jnp.exp(lax.dynamic_slice_in_dim(decay_log, col_start, heads_col, 0))
    step_col = jax.nn.softplus(prompt_step)
    cumul = jnp.cumsum(-rate_col[:, None] * step_col, axis=1)
    local_log = cumul[:, -1]
    weight_col = jnp.exp(local_log[:, None] - cumul) * step_col
    group_span = max(1, heads_col // heads_group)
    per_group = heads_col // group_span
    group_start = col_start // heads_group
    b_select = lax.dynamic_slice_in_dim(
        b_conv.reshape(rows_prompt, STATE_GROUPS, STATE_WIDTH), group_start, group_span, 1
    ).astype(jnp.float32)
    scaled = (
        inner_conv.astype(jnp.float32).reshape(rows_prompt, heads_col, HEAD_WIDTH)
        * jnp.transpose(weight_col)[:, :, None]
    )
    scaled = scaled.reshape(rows_prompt, group_span, per_group, HEAD_WIDTH)
    local_state = jnp.einsum("tgn,tghd->ghdn", b_select, scaled, precision=HIGHEST).reshape(
        heads_col, HEAD_WIDTH, STATE_WIDTH
    )
    own_inner = prompt_inner[rows_prompt - lag_rows :].astype(jnp.float32)
    own_proj = prompt_proj[rows_prompt - lag_rows :].astype(jnp.float32)
    last_index = prompt_count - 1
    head_start = prompt_idx * heads_row
    owner = head_start // heads_col
    head_offset = head_start - owner * heads_col

    def combine(earlier, later):
        return (earlier[0] + later[0], earlier[1] * jnp.exp(later[0])[:, None, None] + later[1])

    before = carried_in(
        (local_log, local_state),
        "prompt",
        combine,
        (jnp.zeros_like(local_log), jnp.zeros_like(local_state)),
    )
    through = combine(before, (local_log, local_state))[1]
    final_state, tail_inner, tail_proj = (
        from_root(through.astype(jnp.bfloat16), "prompt", last_index).astype(through.dtype),
        from_root(own_inner.astype(jnp.bfloat16), "prompt", last_index).astype(own_inner.dtype),
        from_root(own_proj.astype(jnp.bfloat16), "prompt", last_index).astype(own_proj.dtype),
    )
    moved_state, moved_inner = (
        from_root(final_state.astype(jnp.bfloat16), "comp", owner).astype(final_state.dtype),
        from_root(tail_inner.astype(jnp.bfloat16), "comp", owner).astype(tail_inner.dtype),
    )
    start_state = lax.dynamic_slice_in_dim(moved_state, head_offset, heads_row, 0)
    lead_inner = lax.dynamic_slice_in_dim(
        moved_inner, head_offset * HEAD_WIDTH, heads_row * HEAD_WIDTH, 1
    ).astype(jnp.bfloat16)
    group_row = head_start // heads_group
    b_start = group_row * STATE_WIDTH
    c_start = state_feats + group_row * STATE_WIDTH
    proj_select = jnp.concatenate(
        [
            lax.dynamic_slice_in_dim(completion_projections, b_start, STATE_WIDTH, 2),
            lax.dynamic_slice_in_dim(completion_projections, c_start, STATE_WIDTH, 2),
        ],
        axis=2,
    )
    kernel_select = jnp.concatenate(
        [
            lax.dynamic_slice_in_dim(conv_proj, b_start, STATE_WIDTH, 1),
            lax.dynamic_slice_in_dim(conv_proj, c_start, STATE_WIDTH, 1),
        ],
        axis=1,
    )
    lead_wide = tail_proj.astype(jnp.bfloat16)
    lead_select = jnp.concatenate(
        [
            lax.dynamic_slice_in_dim(lead_wide, b_start, STATE_WIDTH, 1),
            lax.dynamic_slice_in_dim(lead_wide, c_start, STATE_WIDTH, 1),
        ],
        axis=1,
    )
    conv_row = lax.dynamic_slice_in_dim(
        conv_inner, head_start * HEAD_WIDTH, heads_row * HEAD_WIDTH, 1
    )
    rate_row = jnp.exp(lax.dynamic_slice_in_dim(decay_log, head_start, heads_row, 0))
    step_row = jax.nn.softplus(sample_step)
    slot_count = completion_inner.shape[0]
    sample_len = completion_inner.shape[1]
    block_count = sample_len // BLOCK

    def advance(carry, block_in):
        block_out, carry_next = block_scan(
            carry, block_in[0], block_in[1], block_in[2], block_in[3], rate_row[None]
        )
        return (carry_next, block_out)

    gated_list = []
    square_list = []
    for slot in range(slot_count):
        slot_conv = causal_conv(completion_inner[slot], conv_row, lead_inner)
        proj_conv = causal_conv(proj_select[slot], kernel_select, lead_select)
        inner_blocks = slot_conv.reshape(block_count, BLOCK, 1, heads_row, HEAD_WIDTH)
        b_blocks = proj_conv[:, :STATE_WIDTH].reshape(block_count, BLOCK, 1, STATE_WIDTH)
        c_blocks = proj_conv[:, STATE_WIDTH:].reshape(block_count, BLOCK, 1, STATE_WIDTH)
        step_blocks = jnp.transpose(
            step_row[:, slot].reshape(heads_row, block_count, BLOCK), (1, 0, 2)
        )[:, None]
        block_inputs = (inner_blocks, b_blocks, c_blocks, step_blocks)
        _, block_outs = lax.scan(advance, start_state[None], block_inputs)
        ssm_out = block_outs.reshape(sample_len, heads_row * HEAD_WIDTH)
        gated = ssm_out * jax.nn.silu(completion_gate[slot].astype(jnp.float32))
        gated_list.append(gated)
        square_list.append(jnp.sum(gated * gated, axis=1))
    square_all = jnp.stack(square_list)
    partner_bits = (prompt_count // STATE_GROUPS).bit_length() - 1
    for bit_number in range(partner_bits):
        square_all = square_all + from_partner(square_all, "prompt", bit_number)
    scale_all = lax.rsqrt(square_all / (heads_group * HEAD_WIDTH) + EPS)
    gated_all = jnp.stack(gated_list)
    result = gated_all * scale_all[:, :, None] * norm_gain[None, None, :]
    live_rows = jnp.arange(sample_len)[None, :] < sample_length[:, None]
    return jnp.where(live_rows[:, :, None], result, 0.0).astype(jnp.bfloat16)


LOG2E = 1.4426950408889634
AXES = ("prompt", "comp")
CHUNKS = (1, 1)
LOG_LANES = 32
TAIL = 16
VMEM_BYTES = 16 * 1024 * 1024


def routed(block, route):
    columns = lax.axis_size("comp")
    pairs = []
    for row in range(lax.axis_size("prompt")):
        for column in range(columns):
            target = route(row // 2, row % 2, column)
            if target is not None:
                plane, core, to = target
                pairs.append((row * columns + column, (2 * plane + core) * columns + to))
    return lax.ppermute(block, AXES, pairs)


def half_silu(value):
    return 0.5 * value * (1.0 + jnp.tanh(0.5 * value))


def conv_rows(taps, lead, block):
    wide = taps.astype(jnp.float32)
    rows = block.astype(jnp.float32)
    edge = jnp.concatenate([lead.astype(jnp.float32)[TAIL - 8 :], rows[0:8]], axis=0)
    total = wide[CONV - 1 : CONV] * rows
    for back in range(1, CONV):
        shifted = pltpu.roll(rows, back, 0)
        shifted = jnp.concatenate([edge[8 - back : 16 - back], shifted[8:]], axis=0)
        total = total + wide[CONV - 1 - back : CONV - back] * shifted
    return half_silu(total)


def spread_heads(first, heads, width):
    row = lax.broadcasted_iota(jnp.int32, (heads, width), 0)
    col = lax.broadcasted_iota(jnp.int32, (heads, width), 1)
    return row == first + col // HEAD_WIDTH


def contract(lhs, rhs, dims, precision=None):
    return lax.dot_general(
        lhs, rhs, (dims, ((), ())), preferred_element_type=jnp.float32, precision=precision
    )


def in_three(value):
    high = value.astype(jnp.bfloat16)
    rest = value - high.astype(jnp.float32)
    mid = rest.astype(jnp.bfloat16)
    low = (rest - mid.astype(jnp.float32)).astype(jnp.bfloat16)
    return high, mid, low


def softplus(value):
    return jnp.maximum(value, 0.0) + jnp.log1p(jnp.exp(-jnp.abs(value)))


def group_of(decay, index, size):
    every = jnp.reshape(decay[...], (1, decay.shape[0]))
    count = decay.shape[0]
    return pltpu.roll(every, lax.rem(count - index * size, count), 1)[:, 0:size]


def pack_kernel(
    place, inner, proj, step, swap_out, edge_out, own_out, step_in, inner_in, b_in, c_in, sems
):
    heads, rows = step_in.shape
    features = heads * HEAD_WIDTH
    column, core = place[1], place[2]
    theirs = 1 - core
    pair = 2 * STATE_WIDTH

    def columns(first, size):
        return pl.ds(pl.multiple_of(first * size, size), size)

    last = slice(rows - TAIL, rows)
    copies = [
        (step.at[columns(theirs, heads)], step_in),
        (inner.at[last], inner_in),
        (proj.at[last, columns(column, pair)], b_in),
        (proj.at[last, columns(STATE_GROUPS // 2 + column, pair)], c_in),
        (proj.at[:, columns(2 * column + theirs, STATE_WIDTH)], swap_out.at[0:rows, 0:STATE_WIDTH]),
        (proj.at[:, columns(2 * column + core, STATE_WIDTH)], own_out),
    ]
    copies = [
        pltpu.make_async_copy(source, target, sems.at[index])
        for index, (source, target) in enumerate(copies)
    ]
    for copy in copies:
        copy.start()
    copies[0].wait()
    dt = jnp.transpose(softplus(step_in[...]))
    high = dt.astype(jnp.bfloat16)
    low = (dt - high.astype(jnp.float32)).astype(jnp.bfloat16)
    swap_out[0:rows, STATE_WIDTH:pair] = jnp.concatenate([high, low] * (STATE_WIDTH // heads // 2), axis=1)
    for copy in copies[1:4]:
        copy.wait()
    edges = []
    for to in range(2):
        group = slice(to * STATE_WIDTH, (to + 1) * STATE_WIDTH)
        inner_last = inner_in[:, to * features : (to + 1) * features].astype(jnp.float32)
        bc_last = jnp.concatenate([b_in[:, group], c_in[:, group]], axis=1)
        pieces = [inner_last[TAIL - 3 :, at : at + pair] for at in range(0, features, pair)]
        pieces.append(bc_last.astype(jnp.float32)[TAIL - 3 :])
        pieces.append(jnp.zeros((TAIL - 3 * len(pieces), pair), jnp.float32))
        edges.append(jnp.concatenate(pieces, axis=0))
    swap_out[rows:] = jnp.where(core == 0, edges[1], edges[0]).astype(jnp.bfloat16)
    edge_out[...] = edges[1].astype(jnp.bfloat16)
    for copy in copies[4:]:
        copy.wait()


def log_lanes(high, low):
    lane = lax.broadcasted_iota(jnp.int32, high.shape, 1)
    return jnp.where(lane % LOG_LANES < LOG_LANES // 2, high, low)


def logs_of(tiles, width):
    rows = [tile.astype(jnp.float32)[TAIL - 1 : TAIL] for tile in tiles]
    lanes = rows[0].shape[1]
    rows.append(jnp.zeros((8 - len(rows), lanes), jnp.float32))
    source = lax.broadcasted_iota(jnp.int32, (lanes, width + lanes), 0)
    target = lax.broadcasted_iota(jnp.int32, (lanes, width + lanes), 1)
    head = jnp.where(target < width, target >> 6, (target - width) >> 5)
    pick = (source >> 5 == head) & ((source & (LOG_LANES // 2 - 1)) == 0)
    rows = jnp.concatenate(rows, axis=0).astype(jnp.bfloat16)
    found = contract(rows, pick.astype(jnp.bfloat16), ((1,), (0,)))
    return found[:, 0:width], found[:, width:]


def prompt_weights_kernel(
    place, own, other, taps_b, step, decay, w_out, b_out, log_out, first_out
):
    rows = own.shape[0]
    heads = step.shape[0] // 2
    group = 2 * place[1] + place[2]
    own_b = own[...]
    other_b = other[0:rows, 0:STATE_WIDTH]
    other_dt = other[0:rows, STATE_WIDTH : STATE_WIDTH + 2 * heads]
    taps = taps_b[:, pl.ds(pl.multiple_of(group * STATE_WIDTH, STATE_WIDTH), STATE_WIDTH)]
    own_step = step[pl.ds(pl.multiple_of(place[2] * heads, heads), heads)]
    core = place[2]
    first_own = core == 0
    rate = jnp.exp(group_of(decay, 2 * place[1] + core, heads))
    dt_own = jnp.transpose(softplus(own_step))
    parts = other_dt.astype(jnp.float32)
    dt_other = parts[:, 0:heads] + parts[:, heads : 2 * heads]
    row = lax.broadcasted_iota(jnp.int32, (rows, rows), 0)
    col = lax.broadcasted_iota(jnp.int32, (rows, rows), 1)
    later = (col > row).astype(jnp.bfloat16)
    both = jnp.concatenate([dt_own, dt_other], axis=1)
    after = contract(later, jnp.concatenate(in_three(both), axis=1), ((1,), (0,)))
    size = 2 * heads
    after = after[:, 0:size] + after[:, size : 2 * size] + after[:, 2 * size :]
    sum_own = after[0:1, 0:heads] + dt_own[0:1]
    sum_other = after[0:1, heads:] + dt_other[0:1]
    after_own = after[:, 0:heads] + jnp.where(first_own, sum_other, 0.0)
    after_other = after[:, heads:] + jnp.where(first_own, 0.0, sum_own)
    w_out[0:rows] = jnp.exp(-rate * after_own) * dt_own
    w_out[rows:] = jnp.exp(-rate * after_other) * dt_other
    total = jnp.broadcast_to(-rate * (sum_own + sum_other), (8, heads))
    high = total.astype(jnp.bfloat16)
    low = (total - high.astype(jnp.float32)).astype(jnp.bfloat16)
    row = lax.broadcasted_iota(jnp.int32, (heads, heads * LOG_LANES), 0)
    lane = lax.broadcasted_iota(jnp.int32, (heads, heads * LOG_LANES), 1)
    spread = (row == lane // LOG_LANES).astype(jnp.bfloat16)
    log_out[...] = log_lanes(
        contract(high, spread, ((1,), (0,))), contract(low, spread, ((1,), (0,)))
    )
    own_last, other_last = own_b[rows - TAIL :], other_b[rows - TAIL :]
    first = jnp.where(first_own, own_b[0:TAIL].astype(jnp.float32), other_b[0:TAIL].astype(jnp.float32))
    first_out[...] = first.astype(jnp.bfloat16)
    blank = jnp.zeros((TAIL, STATE_WIDTH), jnp.float32)
    lead_own = jnp.where(first_own, blank, other_last.astype(jnp.float32))
    lead_other = jnp.where(first_own, own_last.astype(jnp.float32), blank)
    conv_own = conv_rows(taps, lead_own, own_b)
    b_out[:, 0:rows] = jnp.transpose(conv_own).astype(jnp.bfloat16)
    conv_other = conv_rows(taps, lead_other, other_b)
    b_out[:, rows:] = jnp.transpose(conv_other).astype(jnp.bfloat16)


def prompt_state_kernel(
    offset, parts, place, inner, other, near, taps, taps_b, weights, b_turned, b_first, logs, tail,
    *rest,
):
    outs, handed = rest[:parts], rest[parts]
    patch = offset == 0
    b_here = handed if patch else b_turned
    column, core = place[1], place[2]
    group = 2 * column + core
    first_own = core == 0
    rows = inner.shape[0]
    width = outs[0].shape[1]
    heads = weights.shape[1]
    features = heads * HEAD_WIDTH
    part_width = features // parts
    state = b_turned.shape[0]
    w = weights[...].astype(jnp.bfloat16)
    before = jnp.where(place[0] == 0, 0.0, near[...].astype(jnp.float32))
    if patch:
        blank = jnp.zeros((TAIL - 3, STATE_WIDTH), jnp.float32)
        lead_b = jnp.concatenate([blank, before[3 * parts : 3 * parts + 3, 0:STATE_WIDTH]], axis=0)
        taps_here = taps_b[:, pl.ds(pl.multiple_of(group * STATE_WIDTH, STATE_WIDTH), STATE_WIDTH)]
        fresh = conv_rows(taps_here, lead_b, b_first[...])
        fresh = jnp.transpose(jnp.concatenate([fresh, jnp.zeros((128 - TAIL, state), jnp.float32)], axis=0))
        lane = lax.broadcasted_iota(jnp.int32, fresh.shape, 1)
        for index, first in enumerate((core == 0, core == 1)):
            at = index * rows
            old = b_turned[:, at : at + 128].astype(jnp.float32)
            patched = jnp.where(lane < jnp.where(first, CONV - 1, 0), fresh, old)
            b_here[:, at : at + 128] = patched.astype(jnp.bfloat16)
            b_here[:, at + 128 : at + rows] = b_turned[:, at + 128 : at + rows]
    blank = jnp.zeros((TAIL - 3, width), jnp.float32)
    for turn in range(parts):
        part = column ^ turn
        start = part * part_width + offset
        cols = pl.ds(pl.multiple_of(start, 128), width)
        tap_cols = pl.ds(pl.multiple_of(group * features + start, 128), width)
        spread = spread_heads(start // HEAD_WIDTH, heads, width).astype(jnp.bfloat16)
        w_wide = contract(w, spread, ((1,), (0,)))
        own_cols = pl.ds(pl.multiple_of(core * features + start, 128), width)
        own_x, other_x = inner[:, own_cols], other[:, own_cols]
        halo = before[0:3, offset : offset + width]
        for index in range(1, parts):
            at = before[3 * index : 3 * index + 3, offset : offset + width]
            halo = jnp.where(part == index, at, halo)
        halo = jnp.concatenate([blank, halo], axis=0)
        own_last, other_last = own_x[rows - TAIL :], other_x[rows - TAIL :]
        lead_own = jnp.where(first_own, halo, other_last.astype(jnp.float32))
        lead_other = jnp.where(first_own, own_last.astype(jnp.float32), halo)
        x_own = conv_rows(taps[:, tap_cols], lead_own, own_x) * w_wide[0:rows]
        x_other = conv_rows(taps[:, tap_cols], lead_other, other_x) * w_wide[rows:]
        mine = contract(b_here[:, 0:rows], x_own.astype(jnp.bfloat16), ((1,), (0,)))
        theirs = contract(b_here[:, rows:], x_other.astype(jnp.bfloat16), ((1,), (0,)))
        outs[turn][0:state] = (mine + theirs).astype(jnp.bfloat16)
        if outs[turn].shape[0] > state:
            log_width = part_width * LOG_LANES // HEAD_WIDTH
            at = pl.ds(pl.multiple_of(part * log_width, log_width), log_width)
            pieces = tail[:, 0:width].astype(jnp.float32)
            row = lax.broadcasted_iota(jnp.int32, pieces.shape, 0)
            pieces = jnp.where(row == TAIL - 1, logs[0:1, at], pieces)
            outs[turn][state : state + TAIL] = pieces.astype(jnp.bfloat16)
            outs[turn][state + TAIL :] = tail[:, width:]
    if not patch:
        handed[...] = tail[...]


def pick_kernel(count, place, after, *refs):
    held, (stays, goes), tails = refs[:count], refs[count : count + 2], refs[count + 2 :]
    turn = place[0] ^ place[1]
    rows, width = stays.shape[1:]
    for index in range(count):

        @pl.when(turn == index)
        def _():
            for step in range(0, count, 2):
                stays[step // 2] = held[index ^ step][0:rows]
                goes[step // 2] = held[index ^ (step + 1)][0:rows]
            for tail in tails:
                tail[:, 0:width] = held[index][rows - TAIL : rows]
                tail[:, width:] = held[index][rows:]


def merge_kernel(bit, chunk, place, own, came, given, after, *refs):
    count, rows, width = own.shape
    state = STATE_WIDTH
    first = (place[0] >> bit) & 1 == 0
    outs = refs if chunk else refs[:-1]
    factors = given if chunk else refs[-1]
    if chunk == 0:
        last = slice(rows - TAIL, rows)
        tiles = [ref[index, last] for index in range(count) for ref in (own, came)]
        wide, lanes = logs_of(tiles, factors.shape[1])
        row = lax.broadcasted_iota(jnp.int32, wide.shape, 0)
        other = jnp.where(row % 2 == 0, pltpu.roll(wide, 7, 0), pltpu.roll(wide, 1, 0))
        scaled = (row % 2 == 0) == first
        factors[...] = jnp.exp(jnp.where(scaled, other, 0.0))
    for index in range(count):
        cols = slice(chunk * width, (chunk + 1) * width)
        mine_by = factors[2 * index : 2 * index + 1, cols]
        theirs_by = factors[2 * index + 1 : 2 * index + 2, cols]
        joined = own[index, 0:state].astype(jnp.float32) * mine_by
        joined = joined + came[index, 0:state].astype(jnp.float32) * theirs_by
        if count == 1:
            outs[0][...] = joined.astype(jnp.bfloat16)
            continue
        outs[index][0, 0:state] = joined.astype(jnp.bfloat16)
        if rows > state:
            total = lanes[2 * index : 2 * index + 1] + lanes[2 * index + 1 : 2 * index + 2]
            total = jnp.broadcast_to(total, (8, total.shape[1]))
            high = total.astype(jnp.bfloat16).astype(jnp.float32)
            compact = log_lanes(high, total - high)
            compact = jnp.concatenate([compact, compact], axis=0)
            outs[index][0, state:] = compact.astype(jnp.bfloat16)


def prepare_kernel(
    slot, fetch, place, gate, step, decay, after,
    gate_out, factor_out, cum_out, turned_out, log_out, after_out, *rest,
):
    rows, features = gate_out.shape
    size = rows // 4
    copies = []
    if fetch:
        gate_in, sems = rest
        copies = [
            pltpu.make_async_copy(
                gate.at[slot, at : at + size], gate_in.at[at : at + size], sems.at[index]
            )
            for index, at in enumerate(range(0, rows, size))
        ]
    for copy in copies:
        copy.start()
    after_out[...] = after[...]
    heads = step.shape[0]
    row = lax.broadcasted_iota(jnp.int32, (rows, rows), 0)
    col = lax.broadcasted_iota(jnp.int32, (rows, rows), 1)
    dt = softplus(step[:, slot])
    decay_row = jnp.broadcast_to(group_of(decay, place[3], heads), (8, heads))
    decay_col = jnp.transpose(decay_row)[:, 0:1]
    before = (row <= col).astype(jnp.bfloat16)
    cum = contract(jnp.concatenate(in_three(dt), axis=0), before, ((1,), (0,)))
    cum = cum[0:heads] + cum[heads : 2 * heads] + cum[2 * heads :]
    cum = cum * (-LOG2E * jnp.exp(decay_col))
    log_dt = jnp.log(dt) * LOG2E
    cum_out[...] = cum - log_dt
    log_out[...] = log_dt
    turned = jnp.transpose(cum)
    turned_out[...] = turned
    decays = jnp.exp2(turned).astype(jnp.bfloat16)
    width = 2 * STATE_WIDTH
    for index, top in enumerate(range(0, rows, size)):
        if fetch:
            copies[index].wait()
        here = slice(top, top + size)
        for at in range(0, features, width):
            cols = slice(at, at + width)
            gate_here = gate_in[here, cols] if fetch else gate[slot, here, cols]
            silu_gate = half_silu(gate_here.astype(jnp.float32))
            gate_out[here, cols] = silu_gate.astype(jnp.bfloat16)
            spread = spread_heads(at // HEAD_WIDTH, heads, width).astype(jnp.bfloat16)
            decay_wide = contract(decays[here], spread, ((1,), (0,)))
            factor_out[here, cols] = (decay_wide * silu_gate).astype(jnp.bfloat16)


def completion_kernel(
    slot, place, inner, proj, tail, taps, taps_bc, gates, base_rows, cum_cols, log_dt, after,
    fixed_out, c_out, x_held, bc_in, sems,
):
    rows, features = fixed_out.shape
    heads = base_rows.shape[0]
    half = rows // 2
    own = place[3]
    state = STATE_WIDTH
    copies = [
        pltpu.make_async_copy(
            proj.at[slot, :, pl.ds(pl.multiple_of((own + skip) * state, state), state)],
            bc_in.at[index],
            sems.at[index],
        )
        for index, skip in enumerate((0, STATE_GROUPS))
    ]
    for copy in copies:
        copy.start()
    edges = tail[...].astype(jnp.float32)
    pair_width = edges.shape[1]
    blank = jnp.zeros((TAIL - 3, pair_width), jnp.float32)
    row = lax.broadcasted_iota(jnp.int32, (rows, rows), 0)
    col = lax.broadcasted_iota(jnp.int32, (rows, rows), 1)
    blocks = features // pair_width
    for block in range(blocks):
        at = block * pair_width
        cols = slice(at, at + pair_width)
        lead = jnp.concatenate([blank, edges[3 * block : 3 * block + 3]], axis=0)
        taps_here = taps[:, pl.ds(pl.multiple_of(own * features + at, pair_width), pair_width)]
        x_held[:, cols] = conv_rows(taps_here, lead, inner[slot, :, cols]).astype(jnp.bfloat16)
    for copy in copies:
        copy.wait()
    lead_bc = jnp.concatenate([blank, edges[3 * blocks : 3 * blocks + 3]], axis=0)
    bc = []
    for index, skip in enumerate((0, STATE_GROUPS)):
        taps_here = taps_bc[:, pl.ds(pl.multiple_of((own + skip) * state, state), state)]
        lead = lead_bc[:, index * state : (index + 1) * state]
        bc.append(conv_rows(taps_here, lead, bc_in[index]).astype(jnp.bfloat16))
    c_out[...] = bc[1]
    scores = contract(bc[1], bc[0], ((1,), (1,)))
    scores = jnp.where(row >= col, scores, 0.0)
    low, high_left, high_right = scores[0:half, 0:half], scores[half:, 0:half], scores[half:, half:]
    pair = 2 * HEAD_WIDTH
    lane = lax.broadcasted_iota(jnp.int32, (rows, pair), 1)
    for first in range(0, heads, 2):
        cols = slice(first * HEAD_WIDTH, first * HEAD_WIDTH + pair)
        x_pair = x_held[:, cols]
        zero = jnp.zeros_like(x_pair)
        left = jnp.where(lane < HEAD_WIDTH, x_pair, zero)
        right = jnp.where(lane < HEAD_WIDTH, zero, x_pair)
        lows, highs = [], []
        for h in (first, first + 1):
            cc = cum_cols[:, h : h + 1]
            rr, ll = base_rows[h : h + 1], log_dt[h : h + 1]
            grown = jnp.minimum(cc[0:half] - rr[:, 0:half], ll[:, 0:half])
            lows.append((low * jnp.exp2(grown)).astype(jnp.bfloat16))
            grown = jnp.minimum(cc[half:] - rr[:, 0:half], ll[:, 0:half])
            highs.append((high_left * jnp.exp2(grown)).astype(jnp.bfloat16))
            grown = jnp.minimum(cc[half:] - rr[:, half:], ll[:, half:])
            highs.append((high_right * jnp.exp2(grown)).astype(jnp.bfloat16))
        y_low = contract(
            jnp.concatenate(lows, axis=1),
            jnp.concatenate([left[0:half], right[0:half]], axis=0),
            ((1,), (0,)),
        )
        y_high = contract(
            jnp.concatenate(highs, axis=1), jnp.concatenate([left, right], axis=0), ((1,), (0,))
        )
        fixed_out[0:half, cols] = (y_low * gates[0:half, cols].astype(jnp.float32)).astype(jnp.bfloat16)
        fixed_out[half:, cols] = (y_high * gates[half:, cols].astype(jnp.float32)).astype(jnp.bfloat16)


def read_slot(parts, steps, offset, column, slot, states, own_work, gated, slot_at):
    c_ref, fixed, factor = own_work[3 * slot : 3 * slot + 3]
    rows, features = fixed.shape
    part_width = features // parts
    width = states[0].shape[1]
    c = c_ref[...]
    total = jnp.zeros((rows, 128), jnp.float32)
    for index, step in enumerate(steps):
        start = (column ^ step) * part_width + offset
        cols = pl.ds(pl.multiple_of(start, 128), width)
        read = contract(c, states[index][...], ((1,), (0,)))
        weight = factor[:, cols].astype(jnp.float32)
        value = fixed[:, cols].astype(jnp.float32) + read * weight
        gated[slot_at, index] = value
        square = value * value
        for lanes in range(0, width, 128):
            total = total + square[:, lanes : lanes + 128]
    return total


def read_kernel(parts, steps, offset, slots, place, after, *refs):
    states, own_work, (gated, squares) = refs[: len(steps)], refs[len(steps) : -2], refs[-2:]
    for slot in range(slots):
        squares[slot] = read_slot(
            parts, steps, offset, place[1], slot, states, own_work, gated, slot
        )


def finish_kernel(parts, groups, slots, place, live, gain, *refs):
    inputs, (out, gated, held, sems) = refs[:-4], refs[-4:]
    count = 2 * (len(groups) - 1)
    earlier, inputs = inputs[:count], inputs[count:]
    offset, steps = groups[-1]
    states, own_work = inputs[: len(steps)], inputs[len(steps) :]
    column = place[1]
    slots, rows, features = held.shape
    part_width = features // parts
    copies = []
    for slot in range(slots):
        total = read_slot(parts, steps, offset, column, slot, states, own_work, gated, 0)
        for group in range(len(groups) - 1):
            total = total + earlier[2 * group + 1][slot]
        scale = lax.rsqrt(jnp.sum(total, axis=1, keepdims=True) / features + EPS)
        alive = lax.broadcasted_iota(jnp.int32, (rows, 1), 0) < live[slot]
        scale = jnp.where(alive, scale, 0.0)
        size = rows // parts
        for block in range(parts):
            here = slice(block * size, (block + 1) * size)
            for group, (offset_here, steps_here) in enumerate(groups):
                last = group + 1 == len(groups)
                values = gated if last else earlier[2 * group]
                width = values.shape[-1]
                for index, step in enumerate(steps_here):
                    start = (column ^ step) * part_width + offset_here
                    cols = pl.ds(pl.multiple_of(start, 128), width)
                    gain_here = jnp.reshape(gain[cols], (1, width))
                    value = values[0 if last else slot, index, here]
                    held[slot, here, cols] = (value * scale[here] * gain_here).astype(jnp.bfloat16)
            copies.append(
                pltpu.make_async_copy(
                    held.at[slot, here], out.at[slot, here], sems.at[slot * parts + block]
                )
            )
            copies[-1].start()
    for copy in copies:
        copy.wait()


LASTS = dict(
    pack=2, prompt_weights=2, prompt_state=3, pick=1, merge=1, prepare=0, completion=4, read=2, finish=2
)


def matched(
    prompt_inner,
    prompt_proj,
    prompt_step,
    completion_inner,
    completion_gate,
    completion_projections,
    sample_step,
    sample_length,
    decay_log,
    conv_inner,
    conv_proj,
    norm_gain,
):
    parts = lax.axis_size("comp")
    row, column = lax.axis_index("prompt"), lax.axis_index("comp")
    plane, core = row // 2, row % 2
    group = 2 * column + core
    rows = prompt_inner.shape[0]
    heads = sample_step.shape[0]
    features = heads * HEAD_WIDTH
    place = jnp.stack([plane, column, core, row]).astype(jnp.int32)
    bf16, f32 = jnp.bfloat16, jnp.float32

    def take(array, start, size, axis):
        return lax.dynamic_slice_in_dim(array, start, size, axis)

    planes = lax.axis_size("prompt") // 2
    pair_width = 2 * STATE_WIDTH
    edge = jax.ShapeDtypeStruct((TAIL, pair_width), bf16)
    held_inner = pltpu.with_memory_space_constraint(prompt_inner, pltpu.HBM)
    held_proj = pltpu.with_memory_space_constraint(prompt_proj, pltpu.HBM)
    held_step = pltpu.with_memory_space_constraint(prompt_step, pltpu.HBM)

    swap, edge_1, own_b = run_whole(
        pack_kernel,
        "pack",
        (place,),
        (
            jax.ShapeDtypeStruct((rows + TAIL, pair_width), bf16),
            edge,
            jax.ShapeDtypeStruct((rows, STATE_WIDTH), bf16),
        ),
        (held_inner, held_proj, held_step),
        spaces=[pltpu.HBM] * 3,
        scratch=[
            pltpu.VMEM((heads, rows), f32),
            pltpu.VMEM((TAIL, 2 * features), bf16),
            pltpu.VMEM((TAIL, pair_width), bf16),
            pltpu.VMEM((TAIL, pair_width), bf16),
            pltpu.SemaphoreType.DMA((6,)),
        ],
    )
    trade = lambda z, k, c: (z, 1 - k, c)
    other = routed(swap, trade)
    other_inner = routed(prompt_inner, trade)
    slots, positions = completion_inner.shape[:2]
    wide = jax.ShapeDtypeStruct((positions, features), bf16)
    prepared = {}
    held_gate = pltpu.with_memory_space_constraint(completion_gate, pltpu.HBM)

    def prepare(slot, after, fetch):
        every = jax.ShapeDtypeStruct((heads, positions), f32)
        turned = jax.ShapeDtypeStruct((positions, heads), f32)
        return run_whole(
            lambda *refs: prepare_kernel(slot, fetch, *refs),
            "prepare",
            (place,),
            (wide, wide, every, turned, every, edge),
            (held_gate if fetch else completion_gate, sample_step, decay_log, after),
            spaces=[pltpu.HBM if fetch else pltpu.VMEM] + [pltpu.VMEM] * 3,
            scratch=[
                pltpu.VMEM((positions, features), bf16),
                pltpu.SemaphoreType.DMA((4,)),
            ]
            * fetch,
        )

    for slot in range(1, slots):
        *prepared[slot], edge_1 = prepare(slot, edge_1, True)
    edges = jnp.where(core == 0, other[rows:], edge_1)
    near = routed(edges, lambda z, k, c: (z + 1, k, c) if z + 1 < planes else None)
    far = routed(edges, lambda z, k, c: (c, k, c) if z + 1 == planes else None)
    weights, b_turned, logs, b_first = run_whole(
        prompt_weights_kernel,
        "prompt_weights",
        (place,),
        (
            jax.ShapeDtypeStruct((2 * rows, heads), f32),
            jax.ShapeDtypeStruct((STATE_WIDTH, 2 * rows), bf16),
            jax.ShapeDtypeStruct((8, heads * LOG_LANES), f32),
            jax.ShapeDtypeStruct((TAIL, STATE_WIDTH), bf16),
        ),
        (own_b, other, conv_proj, prompt_step, decay_log),
    )
    unit = features // parts // sum(CHUNKS)
    widths = [unit * size for size in CHUNKS]
    offsets = [sum(widths[:chunk]) for chunk in range(len(widths))]
    picks = []
    for chunk, width in enumerate(widths):
        with_tail = chunk == 0
        message = jax.ShapeDtypeStruct((STATE_WIDTH + TAIL * with_tail, width), bf16)
        spread = jax.ShapeDtypeStruct((STATE_WIDTH + 2 * TAIL * with_tail, width), bf16)
        sent = run_whole(
            lambda *refs, offset=offsets[chunk]: prompt_state_kernel(offset, parts, *refs),
            "prompt_state",
            (place,),
            (spread,) * parts
            + (edge if chunk else jax.ShapeDtypeStruct((STATE_WIDTH, 2 * rows), bf16),),
            (
                prompt_inner, other_inner, near, conv_inner, conv_proj, weights, b_turned, b_first,
                logs, far,
            ),
        )
        if chunk == 0:
            b_turned = sent[parts]
        else:
            *prepared[0], handed = prepare(0, sent[parts], False)
        held = [sent[0]] + [
            routed(sent[step], lambda z, k, c: (z, k, c ^ step)) for step in range(1, parts)
        ]
        two = jax.ShapeDtypeStruct((parts // 2,) + message.shape, bf16)
        picks.append(
            lambda after, held=held, two=two, with_tail=with_tail: run_whole(
                lambda *refs: pick_kernel(parts, *refs),
                "pick",
                (place,),
                (two, two) + (edge,) * with_tail,
                [after] + held,
                spaces=[pl.ANY] + [pltpu.VMEM] * parts,
            )
        )

    held_projections = pltpu.with_memory_space_constraint(completion_projections, pltpu.HBM)
    def completion(slot, after):
        gates, factor, *decays = prepared[slot]
        fixed, c = run_whole(
            lambda *refs: completion_kernel(slot, *refs),
            "completion",
            (place,),
            (wide, jax.ShapeDtypeStruct((positions, STATE_WIDTH), bf16)),
            (
                completion_inner, held_projections, tail, conv_inner, conv_proj, gates, *decays, after,
            ),
            spaces=[pltpu.VMEM, pltpu.HBM] + [pltpu.VMEM] * 7 + [pl.ANY],
            scratch=[
                pltpu.VMEM((positions, features), bf16),
                pltpu.VMEM((2, positions, STATE_WIDTH), bf16),
                pltpu.SemaphoreType.DMA((2,)),
            ],
        )
        return c, fixed, factor

    def merge(bit, chunk, own, came, shapes, given, after):
        table = jax.ShapeDtypeStruct((8, features // parts), f32)
        *outs, factors = run_whole(
            lambda *refs: merge_kernel(bit, chunk, *refs),
            "merge",
            (place,),
            shapes + (table,) * (chunk == 0),
            (own, came, given, after),
            spaces=[pltpu.VMEM] * 2 + [pltpu.VMEM if chunk else pl.ANY, pl.ANY],
        ) + ((given,) if chunk else ())
        return outs, factors

    def gather(state):
        return [state] + [
            routed(state, lambda z, k, c: (z, k, c ^ step)) for step in range(1, parts)
        ]

    work = list(range(slots))
    finished = []

    def do_work(after):
        if not work:
            return after
        finished.append(completion(work.pop(0), after))
        return finished[-1][0]

    stays, goes, go_shapes, merged, joined = [], [], [], [], []
    near_plane = lambda z, k, c: (z ^ 1, k, c)
    far_plane = lambda z, k, c: (z ^ 2, k, c)
    tail, after = None, handed
    for chunk in range(len(widths)):
        stay, go, *maybe = picks[chunk](after)
        tail = maybe[0] if maybe else tail
        stays.append(stay)
        goes.append(routed(go, near_plane))
        go_shapes.append(go.shape[1:])
        if chunk + 1 < len(widths):
            after = do_work(go)
    given = after = go
    for chunk in range(len(widths)):
        one = jax.ShapeDtypeStruct((1,) + go_shapes[chunk], bf16)
        (stay, go), given = merge(
            0, chunk, stays[chunk], goes[chunk], (one, one), given, after
        )
        merged.append((stay, routed(go, far_plane)))
        after = do_work(go)
    given = go
    for chunk, width in enumerate(widths):
        state = jax.ShapeDtypeStruct((STATE_WIDTH, width), bf16)
        (state,), given = merge(1, chunk, *merged[chunk], (state,), given, go)
        joined.append(gather(state))
    after = state
    while work:
        after = do_work(after)
    own_work = [array for three in finished for array in three]
    every = tuple(range(parts))
    groups = [(chunk, every) for chunk in range(len(widths) - 1)]
    groups.append((len(widths) - 1, every))
    earlier = []
    for chunk, steps in groups[:-1]:
        earlier += run_whole(
            lambda *refs, steps=steps, offset=offsets[chunk]: read_kernel(
                parts, steps, offset, slots, *refs
            ),
            "read",
            (place,),
            (
                jax.ShapeDtypeStruct((slots, len(steps), positions, widths[chunk]), f32),
                jax.ShapeDtypeStruct((slots, positions, 128), f32),
            ),
            [earlier[-1] if earlier else joined[chunk][0]]
            + [joined[chunk][step] for step in steps]
            + own_work,
            spaces=[pl.ANY] + [pltpu.VMEM] * (len(steps) + len(own_work)),
        )
    chunk, steps = groups[-1]
    groups = [(offsets[chunk], steps) for chunk, steps in groups]
    return run_whole(
        lambda *refs: finish_kernel(parts, groups, slots, *refs),
        "finish",
        (place, sample_length),
        jax.ShapeDtypeStruct((slots, positions, features), bf16),
        [norm_gain] + earlier + [joined[chunk][step] for step in steps] + own_work,
        out_spaces=pltpu.HBM,
        scratch=[
            pltpu.VMEM((1, len(steps), positions, widths[-1]), f32),
            pltpu.VMEM((slots, positions, features), bf16),
            pltpu.SemaphoreType.DMA((slots * parts,)),
        ],
    )


def run_whole(
    kernel, name, place, out_shape, operands, scratch=(), spaces=None, out_spaces=None, aliases=None
):
    vmem = pltpu.VMEM
    spaces = spaces or [vmem] * len(operands)
    out_spaces = out_spaces or jax.tree.map(lambda _: vmem, out_shape)
    return pl.pallas_call(
        kernel,
        out_shape=out_shape,
        in_specs=[pl.BlockSpec(memory_space=pltpu.SMEM)] * len(place)
        + [pl.BlockSpec(memory_space=space) for space in spaces],
        out_specs=jax.tree.map(lambda space: pl.BlockSpec(memory_space=space), out_spaces),
        scratch_shapes=scratch,
        input_output_aliases=aliases or {},
        compiler_params=pltpu.CompilerParams(vmem_limit_bytes=VMEM_BYTES),
        cost_estimate=pl.CostEstimate(
            flops=LASTS[name] * 10**9, transcendentals=0, bytes_accessed=LASTS[name] * 3 * 10**6
        ),
        name=name,
    )(*place, *operands)


def local(*arrays):
    columns, prompts = lax.axis_size("comp"), lax.axis_size("prompt")
    heads_col, heads_row = arrays[2].shape[0], arrays[6].shape[0]
    one_group = heads_row == STATE_HEADS // STATE_GROUPS and heads_col == 2 * heads_row
    if one_group and prompts == 2 * columns and columns & (columns - 1) == 0:
        return matched(*arrays)
    return any_shape(*arrays)


def solution(mesh):
    placed = (
        P("prompt", "comp"),
        P("prompt", None),
        P("comp", "prompt"),
        P("comp", None, "prompt"),
        P("comp", None, "prompt"),
        P("comp", None, None),
        P("prompt", "comp", None),
        P("comp"),
        P(),
        P(),
        P(),
        P("prompt"),
    )
    return jax.shard_map(
        local, mesh=mesh, in_specs=placed, out_specs=P("comp", None, "prompt"), check_vma=False
    )
```

```python
import jax
import jax.numpy as jnp
from jax import lax
from jax.experimental import pallas as pl
from jax.experimental.pallas import tpu as pltpu
from jax.sharding import PartitionSpec as P

STATE_HEADS = 256
HEAD_WIDTH = 64
STATE_WIDTH = 256
STATE_GROUPS = 8
CONV = 4
BLOCK = 128


EPS = 1e-05
HIGHEST = lax.Precision.HIGHEST


def from_behind(block, axis, distance):
    devices = range(lax.axis_size(axis))
    route = [(i - distance, i) for i in devices if i - distance in devices]
    return lax.ppermute(block, axis, route)


def carried_in(array, axis, combine, identity):
    peers, position = (lax.axis_size(axis), lax.axis_index(axis))
    everything = jax.tree.map(
        lambda part, kind: lax.all_gather(part.astype(kind), axis),
        array,
        (jnp.bfloat16, jnp.bfloat16),
    )
    start = jax.tree.map(
        lambda part, zero: jnp.broadcast_to(jnp.asarray(zero, part.dtype), part.shape),
        array,
        identity,
    )

    def hop(k, before):
        reached = k < position
        new = combine(
            before, jax.tree.map(lambda part, own: part[k].astype(own.dtype), everything, array)
        )
        return jax.tree.map(lambda a, b: jnp.where(reached, a, b), new, before)

    return lax.fori_loop(0, peers, hop, start)


def from_root(array, axis, root):
    mine = lax.axis_index(axis) == root
    return lax.psum(jnp.where(mine, array, jnp.zeros_like(array)), axis)


def from_partner(block, axis, stride):
    count = lax.axis_size(axis)
    route = []
    for low in range(count):
        high = low | 1 << stride
        if high != low and high < count:
            route += [(low, high), (high, low)]
    return lax.ppermute(block, axis, route)


def causal_conv(source, kernel, leading):
    padded = jnp.concatenate([leading, source], axis=0).astype(jnp.float32)
    kernel_wide = kernel.astype(jnp.float32)
    row_count = source.shape[0]
    summed = jnp.zeros(source.shape, jnp.float32)
    for offset in range(kernel.shape[0]):
        summed = summed + kernel_wide[offset] * padded[offset : offset + row_count]
    return jax.nn.silu(summed).astype(jnp.bfloat16)


def block_scan(state_in, inner_blk, b_blk, c_blk, step_blk, rate_vals):
    cumul = jnp.cumsum(-rate_vals[:, :, None] * step_blk, axis=2)
    scores = jnp.einsum("ign,jgn->gij", c_blk, b_blk, preferred_element_type=jnp.float32)
    spread_log = cumul[:, :, :, None] - cumul[:, :, None, :]
    length_q = step_blk.shape[2]
    causal = jnp.arange(length_q)[:, None] >= jnp.arange(length_q)[None, :]
    decay_mat = jnp.exp(jnp.where(causal, spread_log, -jnp.inf))
    mixer_w = (scores[:, None] * decay_mat * step_blk[:, :, None, :]).astype(jnp.bfloat16)
    intra_part = jnp.einsum(
        "gkij,jgkd->igkd", mixer_w, inner_blk, preferred_element_type=jnp.float32
    )
    readout = jnp.einsum("ign,gkdn->igkd", c_blk.astype(jnp.float32), state_in, precision=HIGHEST)
    inter_part = jnp.transpose(jnp.exp(cumul), (2, 0, 1))[..., None] * readout
    weights = jnp.exp(cumul[:, :, -1:] - cumul) * step_blk
    packed = (inner_blk.astype(jnp.float32) * jnp.transpose(weights, (2, 0, 1))[..., None]).astype(
        jnp.bfloat16
    )
    fresh_part = jnp.einsum("jgn,jgkd->gkdn", b_blk, packed, preferred_element_type=jnp.float32)
    return (
        intra_part + inter_part,
        jnp.exp(cumul[:, :, -1])[..., None, None] * state_in + fresh_part,
    )


def any_shape(
    prompt_inner,
    prompt_proj,
    prompt_step,
    completion_inner,
    completion_gate,
    completion_projections,
    sample_step,
    sample_length,
    decay_log,
    conv_inner,
    conv_proj,
    norm_gain,
):
    prompt_count = lax.axis_size("prompt")
    prompt_idx = lax.axis_index("prompt")
    column_idx = lax.axis_index("comp")
    heads_group = STATE_HEADS // STATE_GROUPS
    heads_col = prompt_step.shape[0]
    heads_row = sample_step.shape[0]
    state_feats = STATE_GROUPS * STATE_WIDTH
    lag_rows = CONV - 1
    rows_prompt = prompt_inner.shape[0]
    prev_inner, prev_proj = from_behind(
        (
            prompt_inner[rows_prompt - lag_rows :],
            prompt_proj[rows_prompt - lag_rows :, :state_feats],
        ),
        "prompt",
        1,
    )
    col_start = column_idx * heads_col
    conv_col = lax.dynamic_slice_in_dim(
        conv_inner, col_start * HEAD_WIDTH, heads_col * HEAD_WIDTH, 1
    )
    inner_conv = causal_conv(prompt_inner, conv_col, prev_inner)
    b_conv = causal_conv(prompt_proj[:, :state_feats], conv_proj[:, :state_feats], prev_proj)
    rate_col = jnp.exp(lax.dynamic_slice_in_dim(decay_log, col_start, heads_col, 0))
    step_col = jax.nn.softplus(prompt_step)
    cumul = jnp.cumsum(-rate_col[:, None] * step_col, axis=1)
    local_log = cumul[:, -1]
    weight_col = jnp.exp(local_log[:, None] - cumul) * step_col
    group_span = max(1, heads_col // heads_group)
    per_group = heads_col // group_span
    group_start = col_start // heads_group
    b_select = lax.dynamic_slice_in_dim(
        b_conv.reshape(rows_prompt, STATE_GROUPS, STATE_WIDTH), group_start, group_span, 1
    ).astype(jnp.float32)
    scaled = (
        inner_conv.astype(jnp.float32).reshape(rows_prompt, heads_col, HEAD_WIDTH)
        * jnp.transpose(weight_col)[:, :, None]
    )
    scaled = scaled.reshape(rows_prompt, group_span, per_group, HEAD_WIDTH)
    local_state = jnp.einsum("tgn,tghd->ghdn", b_select, scaled, precision=HIGHEST).reshape(
        heads_col, HEAD_WIDTH, STATE_WIDTH
    )
    own_inner = prompt_inner[rows_prompt - lag_rows :].astype(jnp.float32)
    own_proj = prompt_proj[rows_prompt - lag_rows :].astype(jnp.float32)
    last_index = prompt_count - 1
    head_start = prompt_idx * heads_row
    owner = head_start // heads_col
    head_offset = head_start - owner * heads_col

    def combine(earlier, later):
        return (earlier[0] + later[0], earlier[1] * jnp.exp(later[0])[:, None, None] + later[1])

    before = carried_in(
        (local_log, local_state),
        "prompt",
        combine,
        (jnp.zeros_like(local_log), jnp.zeros_like(local_state)),
    )
    through = combine(before, (local_log, local_state))[1]
    final_state, tail_inner, tail_proj = (
        from_root(through.astype(jnp.bfloat16), "prompt", last_index).astype(through.dtype),
        from_root(own_inner.astype(jnp.bfloat16), "prompt", last_index).astype(own_inner.dtype),
        from_root(own_proj.astype(jnp.bfloat16), "prompt", last_index).astype(own_proj.dtype),
    )
    moved_state, moved_inner = (
        from_root(final_state.astype(jnp.bfloat16), "comp", owner).astype(final_state.dtype),
        from_root(tail_inner.astype(jnp.bfloat16), "comp", owner).astype(tail_inner.dtype),
    )
    start_state = lax.dynamic_slice_in_dim(moved_state, head_offset, heads_row, 0)
    lead_inner = lax.dynamic_slice_in_dim(
        moved_inner, head_offset * HEAD_WIDTH, heads_row * HEAD_WIDTH, 1
    ).astype(jnp.bfloat16)
    group_row = head_start // heads_group
    b_start = group_row * STATE_WIDTH
    c_start = state_feats + group_row * STATE_WIDTH
    proj_select = jnp.concatenate(
        [
            lax.dynamic_slice_in_dim(completion_projections, b_start, STATE_WIDTH, 2),
            lax.dynamic_slice_in_dim(completion_projections, c_start, STATE_WIDTH, 2),
        ],
        axis=2,
    )
    kernel_select = jnp.concatenate(
        [
            lax.dynamic_slice_in_dim(conv_proj, b_start, STATE_WIDTH, 1),
            lax.dynamic_slice_in_dim(conv_proj, c_start, STATE_WIDTH, 1),
        ],
        axis=1,
    )
    lead_wide = tail_proj.astype(jnp.bfloat16)
    lead_select = jnp.concatenate(
        [
            lax.dynamic_slice_in_dim(lead_wide, b_start, STATE_WIDTH, 1),
            lax.dynamic_slice_in_dim(lead_wide, c_start, STATE_WIDTH, 1),
        ],
        axis=1,
    )
    conv_row = lax.dynamic_slice_in_dim(
        conv_inner, head_start * HEAD_WIDTH, heads_row * HEAD_WIDTH, 1
    )
    rate_row = jnp.exp(lax.dynamic_slice_in_dim(decay_log, head_start, heads_row, 0))
    step_row = jax.nn.softplus(sample_step)
    slot_count = completion_inner.shape[0]
    sample_len = completion_inner.shape[1]
    block_count = sample_len // BLOCK

    def advance(carry, block_in):
        block_out, carry_next = block_scan(
            carry, block_in[0], block_in[1], block_in[2], block_in[3], rate_row[None]
        )
        return (carry_next, block_out)

    gated_list = []
    square_list = []
    for slot in range(slot_count):
        slot_conv = causal_conv(completion_inner[slot], conv_row, lead_inner)
        proj_conv = causal_conv(proj_select[slot], kernel_select, lead_select)
        inner_blocks = slot_conv.reshape(block_count, BLOCK, 1, heads_row, HEAD_WIDTH)
        b_blocks = proj_conv[:, :STATE_WIDTH].reshape(block_count, BLOCK, 1, STATE_WIDTH)
        c_blocks = proj_conv[:, STATE_WIDTH:].reshape(block_count, BLOCK, 1, STATE_WIDTH)
        step_blocks = jnp.transpose(
            step_row[:, slot].reshape(heads_row, block_count, BLOCK), (1, 0, 2)
        )[:, None]
        block_inputs = (inner_blocks, b_blocks, c_blocks, step_blocks)
        _, block_outs = lax.scan(advance, start_state[None], block_inputs)
        ssm_out = block_outs.reshape(sample_len, heads_row * HEAD_WIDTH)
        gated = ssm_out * jax.nn.silu(completion_gate[slot].astype(jnp.float32))
        gated_list.append(gated)
        square_list.append(jnp.sum(gated * gated, axis=1))
    square_all = jnp.stack(square_list)
    partner_bits = (prompt_count // STATE_GROUPS).bit_length() - 1
    for bit_number in range(partner_bits):
        square_all = square_all + from_partner(square_all, "prompt", bit_number)
    scale_all = lax.rsqrt(square_all / (heads_group * HEAD_WIDTH) + EPS)
    gated_all = jnp.stack(gated_list)
    result = gated_all * scale_all[:, :, None] * norm_gain[None, None, :]
    live_rows = jnp.arange(sample_len)[None, :] < sample_length[:, None]
    return jnp.where(live_rows[:, :, None], result, 0.0).astype(jnp.bfloat16)


LOG2E = 1.4426950408889634
AXES = ("prompt", "comp")
CHUNKS = (1, 1)
LOG_LANES = 32
TAIL = 16
VMEM_BYTES = 16 * 1024 * 1024


def routed(block, route):
    columns = lax.axis_size("comp")
    pairs = []
    for row in range(lax.axis_size("prompt")):
        for column in range(columns):
            target = route(row // 2, row % 2, column)
            if target is not None:
                plane, core, to = target
                pairs.append((row * columns + column, (2 * plane + core) * columns + to))
    return lax.ppermute(block, AXES, pairs)


def silu_of_twice(half):
    return half + half * jnp.tanh(half)


def conv_rows(taps, lead, block):
    wide = 0.5 * taps.astype(jnp.float32)
    rows = block.astype(jnp.float32)
    edge = jnp.concatenate([lead.astype(jnp.float32)[TAIL - 8 :], rows[0:8]], axis=0)
    total = wide[CONV - 1 : CONV] * rows
    for back in range(1, CONV):
        shifted = pltpu.roll(rows, back, 0)
        shifted = jnp.concatenate([edge[8 - back : 16 - back], shifted[8:]], axis=0)
        total = total + wide[CONV - 1 - back : CONV - back] * shifted
    return silu_of_twice(total)


def spread_heads(first, heads, width):
    row = lax.broadcasted_iota(jnp.int32, (heads, width), 0)
    col = lax.broadcasted_iota(jnp.int32, (heads, width), 1)
    return row == first + col // HEAD_WIDTH


def contract(lhs, rhs, dims, precision=None):
    return lax.dot_general(
        lhs, rhs, (dims, ((), ())), preferred_element_type=jnp.float32, precision=precision
    )


def in_three(value):
    high = value.astype(jnp.bfloat16)
    rest = value - high.astype(jnp.float32)
    mid = rest.astype(jnp.bfloat16)
    low = (rest - mid.astype(jnp.float32)).astype(jnp.bfloat16)
    return high, mid, low


def softplus(value):
    return jnp.maximum(value, 0.0) + jnp.log1p(jnp.exp(-jnp.abs(value)))


def group_of(decay, index, size):
    every = jnp.reshape(decay[...], (1, decay.shape[0]))
    count = decay.shape[0]
    return pltpu.roll(every, lax.rem(count - index * size, count), 1)[:, 0:size]


def pack_kernel(
    place, inner, proj, step, swap_out, edge_out, own_out, step_in, inner_in, b_in, c_in, sems
):
    heads, rows = step_in.shape
    features = heads * HEAD_WIDTH
    column, core = place[1], place[2]
    theirs = 1 - core
    pair = 2 * STATE_WIDTH

    def columns(first, size):
        return pl.ds(pl.multiple_of(first * size, size), size)

    last = slice(rows - TAIL, rows)
    copies = [
        (step.at[columns(theirs, heads)], step_in),
        (inner.at[last], inner_in),
        (proj.at[last, columns(column, pair)], b_in),
        (proj.at[last, columns(STATE_GROUPS // 2 + column, pair)], c_in),
        (proj.at[:, columns(2 * column + theirs, STATE_WIDTH)], swap_out.at[0:rows, 0:STATE_WIDTH]),
        (proj.at[:, columns(2 * column + core, STATE_WIDTH)], own_out),
    ]
    copies = [
        pltpu.make_async_copy(source, target, sems.at[index])
        for index, (source, target) in enumerate(copies)
    ]
    for copy in copies:
        copy.start()
    copies[0].wait()
    dt = jnp.transpose(softplus(step_in[...]))
    high = dt.astype(jnp.bfloat16)
    low = (dt - high.astype(jnp.float32)).astype(jnp.bfloat16)
    swap_out[0:rows, STATE_WIDTH:pair] = jnp.concatenate([high, low] * (STATE_WIDTH // heads // 2), axis=1)
    for copy in copies[1:4]:
        copy.wait()
    edges = []
    for to in range(2):
        group = slice(to * STATE_WIDTH, (to + 1) * STATE_WIDTH)
        inner_last = inner_in[:, to * features : (to + 1) * features].astype(jnp.float32)
        bc_last = jnp.concatenate([b_in[:, group], c_in[:, group]], axis=1)
        pieces = [inner_last[TAIL - 3 :, at : at + pair] for at in range(0, features, pair)]
        pieces.append(bc_last.astype(jnp.float32)[TAIL - 3 :])
        pieces.append(jnp.zeros((TAIL - 3 * len(pieces), pair), jnp.float32))
        edges.append(jnp.concatenate(pieces, axis=0))
    swap_out[rows:] = jnp.where(core == 0, edges[1], edges[0]).astype(jnp.bfloat16)
    edge_out[...] = edges[1].astype(jnp.bfloat16)
    for copy in copies[4:]:
        copy.wait()


def log_lanes(high, low):
    lane = lax.broadcasted_iota(jnp.int32, high.shape, 1)
    return jnp.where(lane % LOG_LANES < LOG_LANES // 2, high, low)


def logs_of(tiles, width):
    rows = [tile.astype(jnp.float32)[TAIL - 1 : TAIL] for tile in tiles]
    lanes = rows[0].shape[1]
    rows.append(jnp.zeros((8 - len(rows), lanes), jnp.float32))
    source = lax.broadcasted_iota(jnp.int32, (lanes, width + lanes), 0)
    target = lax.broadcasted_iota(jnp.int32, (lanes, width + lanes), 1)
    head = jnp.where(target < width, target >> 6, (target - width) >> 5)
    pick = (source >> 5 == head) & ((source & (LOG_LANES // 2 - 1)) == 0)
    rows = jnp.concatenate(rows, axis=0).astype(jnp.bfloat16)
    found = contract(rows, pick.astype(jnp.bfloat16), ((1,), (0,)))
    return found[:, 0:width], found[:, width:]


def prompt_weights_kernel(
    place, own, other, taps_b, step, decay, w_out, b_out, log_out, first_out
):
    rows = own.shape[0]
    heads = step.shape[0] // 2
    group = 2 * place[1] + place[2]
    own_b = own[...]
    other_b = other[0:rows, 0:STATE_WIDTH]
    other_dt = other[0:rows, STATE_WIDTH : STATE_WIDTH + 2 * heads]
    taps = taps_b[:, pl.ds(pl.multiple_of(group * STATE_WIDTH, STATE_WIDTH), STATE_WIDTH)]
    own_step = step[pl.ds(pl.multiple_of(place[2] * heads, heads), heads)]
    core = place[2]
    first_own = core == 0
    rate = jnp.exp(group_of(decay, 2 * place[1] + core, heads))
    dt_own = jnp.transpose(softplus(own_step))
    parts = other_dt.astype(jnp.float32)
    dt_other = parts[:, 0:heads] + parts[:, heads : 2 * heads]
    row = lax.broadcasted_iota(jnp.int32, (rows, rows), 0)
    col = lax.broadcasted_iota(jnp.int32, (rows, rows), 1)
    later = (col > row).astype(jnp.bfloat16)
    both = jnp.concatenate([dt_own, dt_other], axis=1)
    after = contract(later, jnp.concatenate(in_three(both), axis=1), ((1,), (0,)))
    size = 2 * heads
    after = after[:, 0:size] + after[:, size : 2 * size] + after[:, 2 * size :]
    sum_own = after[0:1, 0:heads] + dt_own[0:1]
    sum_other = after[0:1, heads:] + dt_other[0:1]
    after_own = after[:, 0:heads] + jnp.where(first_own, sum_other, 0.0)
    after_other = after[:, heads:] + jnp.where(first_own, 0.0, sum_own)
    w_out[0:rows] = jnp.exp(-rate * after_own) * dt_own
    w_out[rows:] = jnp.exp(-rate * after_other) * dt_other
    total = jnp.broadcast_to(-rate * (sum_own + sum_other), (8, heads))
    high = total.astype(jnp.bfloat16)
    low = (total - high.astype(jnp.float32)).astype(jnp.bfloat16)
    row = lax.broadcasted_iota(jnp.int32, (heads, heads * LOG_LANES), 0)
    lane = lax.broadcasted_iota(jnp.int32, (heads, heads * LOG_LANES), 1)
    spread = (row == lane // LOG_LANES).astype(jnp.bfloat16)
    log_out[...] = log_lanes(
        contract(high, spread, ((1,), (0,))), contract(low, spread, ((1,), (0,)))
    )
    own_last, other_last = own_b[rows - TAIL :], other_b[rows - TAIL :]
    first = jnp.where(first_own, own_b[0:TAIL].astype(jnp.float32), other_b[0:TAIL].astype(jnp.float32))
    first_out[...] = first.astype(jnp.bfloat16)
    blank = jnp.zeros((TAIL, STATE_WIDTH), jnp.float32)
    lead_own = jnp.where(first_own, blank, other_last.astype(jnp.float32))
    lead_other = jnp.where(first_own, own_last.astype(jnp.float32), blank)
    conv_own = conv_rows(taps, lead_own, own_b)
    b_out[:, 0:rows] = jnp.transpose(conv_own).astype(jnp.bfloat16)
    conv_other = conv_rows(taps, lead_other, other_b)
    b_out[:, rows:] = jnp.transpose(conv_other).astype(jnp.bfloat16)


def prompt_state_kernel(
    offset, parts, place, inner, other, near, taps, taps_b, weights, b_turned, b_first, logs, tail,
    *rest,
):
    outs, handed = rest[:parts], rest[parts]
    patch = offset == 0
    b_here = handed if patch else b_turned
    column, core = place[1], place[2]
    group = 2 * column + core
    first_own = core == 0
    rows = inner.shape[0]
    width = outs[0].shape[1]
    heads = weights.shape[1]
    features = heads * HEAD_WIDTH
    part_width = features // parts
    state = b_turned.shape[0]
    w = weights[...].astype(jnp.bfloat16)
    before = jnp.where(place[0] == 0, 0.0, near[...].astype(jnp.float32))
    if patch:
        blank = jnp.zeros((TAIL - 3, STATE_WIDTH), jnp.float32)
        lead_b = jnp.concatenate([blank, before[3 * parts : 3 * parts + 3, 0:STATE_WIDTH]], axis=0)
        taps_here = taps_b[:, pl.ds(pl.multiple_of(group * STATE_WIDTH, STATE_WIDTH), STATE_WIDTH)]
        fresh = conv_rows(taps_here, lead_b, b_first[...])
        fresh = jnp.transpose(jnp.concatenate([fresh, jnp.zeros((128 - TAIL, state), jnp.float32)], axis=0))
        lane = lax.broadcasted_iota(jnp.int32, fresh.shape, 1)
        for index, first in enumerate((core == 0, core == 1)):
            at = index * rows
            old = b_turned[:, at : at + 128].astype(jnp.float32)
            patched = jnp.where(lane < jnp.where(first, CONV - 1, 0), fresh, old)
            b_here[:, at : at + 128] = patched.astype(jnp.bfloat16)
            b_here[:, at + 128 : at + rows] = b_turned[:, at + 128 : at + rows]
    blank = jnp.zeros((TAIL - 3, width), jnp.float32)
    for turn in range(parts):
        part = column ^ turn
        start = part * part_width + offset
        cols = pl.ds(pl.multiple_of(start, 128), width)
        tap_cols = pl.ds(pl.multiple_of(group * features + start, 128), width)
        spread = spread_heads(start // HEAD_WIDTH, heads, width).astype(jnp.bfloat16)
        w_wide = contract(w, spread, ((1,), (0,)))
        own_cols = pl.ds(pl.multiple_of(core * features + start, 128), width)
        own_x, other_x = inner[:, own_cols], other[:, own_cols]
        halo = before[0:3, offset : offset + width]
        for index in range(1, parts):
            at = before[3 * index : 3 * index + 3, offset : offset + width]
            halo = jnp.where(part == index, at, halo)
        halo = jnp.concatenate([blank, halo], axis=0)
        own_last, other_last = own_x[rows - TAIL :], other_x[rows - TAIL :]
        lead_own = jnp.where(first_own, halo, other_last.astype(jnp.float32))
        lead_other = jnp.where(first_own, own_last.astype(jnp.float32), halo)
        x_own = conv_rows(taps[:, tap_cols], lead_own, own_x) * w_wide[0:rows]
        x_other = conv_rows(taps[:, tap_cols], lead_other, other_x) * w_wide[rows:]
        mine = contract(b_here[:, 0:rows], x_own.astype(jnp.bfloat16), ((1,), (0,)))
        theirs = contract(b_here[:, rows:], x_other.astype(jnp.bfloat16), ((1,), (0,)))
        outs[turn][0:state] = (mine + theirs).astype(jnp.bfloat16)
        if outs[turn].shape[0] > state:
            log_width = part_width * LOG_LANES // HEAD_WIDTH
            at = pl.ds(pl.multiple_of(part * log_width, log_width), log_width)
            pieces = tail[:, 0:width].astype(jnp.float32)
            row = lax.broadcasted_iota(jnp.int32, pieces.shape, 0)
            pieces = jnp.where(row == TAIL - 1, logs[0:1, at], pieces)
            outs[turn][state : state + TAIL] = pieces.astype(jnp.bfloat16)
            outs[turn][state + TAIL :] = tail[:, width:]
    if not patch:
        handed[...] = tail[...]


def pick_kernel(count, place, after, *refs):
    held, (stays, goes), tails = refs[:count], refs[count : count + 2], refs[count + 2 :]
    turn = place[0] ^ place[1]
    rows, width = stays.shape[1:]
    for index in range(count):

        @pl.when(turn == index)
        def _():
            for step in range(0, count, 2):
                stays[step // 2] = held[index ^ step][0:rows]
                goes[step // 2] = held[index ^ (step + 1)][0:rows]
            for tail in tails:
                tail[:, 0:width] = held[index][rows - TAIL : rows]
                tail[:, width:] = held[index][rows:]


def merge_kernel(bit, chunk, place, own, came, given, after, *refs):
    count, rows, width = own.shape
    state = STATE_WIDTH
    first = (place[0] >> bit) & 1 == 0
    outs = refs if chunk else refs[:-1]
    factors = given if chunk else refs[-1]
    if chunk == 0:
        last = slice(rows - TAIL, rows)
        tiles = [ref[index, last] for index in range(count) for ref in (own, came)]
        wide, lanes = logs_of(tiles, factors.shape[1])
        row = lax.broadcasted_iota(jnp.int32, wide.shape, 0)
        other = jnp.where(row % 2 == 0, pltpu.roll(wide, 7, 0), pltpu.roll(wide, 1, 0))
        scaled = (row % 2 == 0) == first
        factors[...] = jnp.exp(jnp.where(scaled, other, 0.0))
    for index in range(count):
        cols = slice(chunk * width, (chunk + 1) * width)
        mine_by = factors[2 * index : 2 * index + 1, cols]
        theirs_by = factors[2 * index + 1 : 2 * index + 2, cols]
        joined = own[index, 0:state].astype(jnp.float32) * mine_by
        joined = joined + came[index, 0:state].astype(jnp.float32) * theirs_by
        if count == 1:
            outs[0][...] = joined.astype(jnp.bfloat16)
            continue
        outs[index][0, 0:state] = joined.astype(jnp.bfloat16)
        if rows > state:
            total = lanes[2 * index : 2 * index + 1] + lanes[2 * index + 1 : 2 * index + 2]
            total = jnp.broadcast_to(total, (8, total.shape[1]))
            high = total.astype(jnp.bfloat16).astype(jnp.float32)
            compact = log_lanes(high, total - high)
            compact = jnp.concatenate([compact, compact], axis=0)
            outs[index][0, state:] = compact.astype(jnp.bfloat16)


def prepare_kernel(
    slot, fetch, place, gate, step, decay, after,
    gate_out, factor_out, cum_out, turned_out, log_out, after_out, *rest,
):
    rows, features = gate_out.shape
    size = rows // 4
    copies = []
    if fetch:
        gate_in, sems = rest
        copies = [
            pltpu.make_async_copy(
                gate.at[slot, at : at + size], gate_in.at[at : at + size], sems.at[index]
            )
            for index, at in enumerate(range(0, rows, size))
        ]
    for copy in copies:
        copy.start()
    after_out[...] = after[...]
    heads = step.shape[0]
    row = lax.broadcasted_iota(jnp.int32, (rows, rows), 0)
    col = lax.broadcasted_iota(jnp.int32, (rows, rows), 1)
    dt = softplus(step[:, slot])
    decay_row = jnp.broadcast_to(group_of(decay, place[3], heads), (8, heads))
    decay_col = jnp.transpose(decay_row)[:, 0:1]
    before = (row <= col).astype(jnp.bfloat16)
    cum = contract(jnp.concatenate(in_three(dt), axis=0), before, ((1,), (0,)))
    cum = cum[0:heads] + cum[heads : 2 * heads] + cum[2 * heads :]
    cum = cum * (-LOG2E * jnp.exp(decay_col))
    log_dt = jnp.log(dt) * LOG2E
    cum_out[...] = cum - log_dt
    log_out[...] = log_dt
    turned = jnp.transpose(cum)
    turned_out[...] = turned
    decays = jnp.exp2(turned).astype(jnp.bfloat16)
    width = 2 * STATE_WIDTH
    for index, top in enumerate(range(0, rows, size)):
        if fetch:
            copies[index].wait()
        here = slice(top, top + size)
        for at in range(0, features, width):
            cols = slice(at, at + width)
            gate_here = gate_in[here, cols] if fetch else gate[slot, here, cols]
            silu_gate = silu_of_twice(0.5 * gate_here.astype(jnp.float32))
            gate_out[here, cols] = silu_gate.astype(jnp.bfloat16)
            spread = spread_heads(at // HEAD_WIDTH, heads, width).astype(jnp.bfloat16)
            decay_wide = contract(decays[here], spread, ((1,), (0,)))
            factor_out[here, cols] = (decay_wide * silu_gate).astype(jnp.bfloat16)


def completion_kernel(
    slot, place, inner, proj, tail, taps, taps_bc, gates, base_rows, cum_cols, log_dt, after,
    fixed_out, c_out, x_held, bc_in, sems,
):
    rows, features = fixed_out.shape
    heads = base_rows.shape[0]
    half = rows // 2
    own = place[3]
    state = STATE_WIDTH
    copies = [
        pltpu.make_async_copy(
            proj.at[slot, :, pl.ds(pl.multiple_of((own + skip) * state, state), state)],
            bc_in.at[index],
            sems.at[index],
        )
        for index, skip in enumerate((0, STATE_GROUPS))
    ]
    for copy in copies:
        copy.start()
    edges = tail[...].astype(jnp.float32)
    pair_width = edges.shape[1]
    blank = jnp.zeros((TAIL - 3, pair_width), jnp.float32)
    row = lax.broadcasted_iota(jnp.int32, (rows, rows), 0)
    col = lax.broadcasted_iota(jnp.int32, (rows, rows), 1)
    blocks = features // pair_width
    for block in range(blocks):
        at = block * pair_width
        cols = slice(at, at + pair_width)
        lead = jnp.concatenate([blank, edges[3 * block : 3 * block + 3]], axis=0)
        taps_here = taps[:, pl.ds(pl.multiple_of(own * features + at, pair_width), pair_width)]
        x_held[:, cols] = conv_rows(taps_here, lead, inner[slot, :, cols]).astype(jnp.bfloat16)
    for copy in copies:
        copy.wait()
    lead_bc = jnp.concatenate([blank, edges[3 * blocks : 3 * blocks + 3]], axis=0)
    bc = []
    for index, skip in enumerate((0, STATE_GROUPS)):
        taps_here = taps_bc[:, pl.ds(pl.multiple_of((own + skip) * state, state), state)]
        lead = lead_bc[:, index * state : (index + 1) * state]
        bc.append(conv_rows(taps_here, lead, bc_in[index]).astype(jnp.bfloat16))
    c_out[...] = bc[1]
    scores = contract(bc[1], bc[0], ((1,), (1,)))
    scores = jnp.where(row >= col, scores, 0.0)
    low, high_left, high_right = scores[0:half, 0:half], scores[half:, 0:half], scores[half:, half:]
    pair = 2 * HEAD_WIDTH
    lane = lax.broadcasted_iota(jnp.int32, (rows, pair), 1)
    for first in range(0, heads, 2):
        cols = slice(first * HEAD_WIDTH, first * HEAD_WIDTH + pair)
        x_pair = x_held[:, cols]
        zero = jnp.zeros_like(x_pair)
        left = jnp.where(lane < HEAD_WIDTH, x_pair, zero)
        right = jnp.where(lane < HEAD_WIDTH, zero, x_pair)
        lows, highs = [], []
        for h in (first, first + 1):
            cc = cum_cols[:, h : h + 1]
            rr, ll = base_rows[h : h + 1], log_dt[h : h + 1]
            grown = jnp.minimum(cc[0:half] - rr[:, 0:half], ll[:, 0:half])
            lows.append((low * jnp.exp2(grown)).astype(jnp.bfloat16))
            grown = jnp.minimum(cc[half:] - rr[:, 0:half], ll[:, 0:half])
            highs.append((high_left * jnp.exp2(grown)).astype(jnp.bfloat16))
            grown = jnp.minimum(cc[half:] - rr[:, half:], ll[:, half:])
            highs.append((high_right * jnp.exp2(grown)).astype(jnp.bfloat16))
        y_low = contract(
            jnp.concatenate(lows, axis=1),
            jnp.concatenate([left[0:half], right[0:half]], axis=0),
            ((1,), (0,)),
        )
        y_high = contract(
            jnp.concatenate(highs, axis=1), jnp.concatenate([left, right], axis=0), ((1,), (0,))
        )
        fixed_out[0:half, cols] = (y_low * gates[0:half, cols].astype(jnp.float32)).astype(jnp.bfloat16)
        fixed_out[half:, cols] = (y_high * gates[half:, cols].astype(jnp.float32)).astype(jnp.bfloat16)


def read_slot(parts, steps, offset, column, slot, states, own_work, gated, slot_at):
    c_ref, fixed, factor = own_work[3 * slot : 3 * slot + 3]
    rows, features = fixed.shape
    part_width = features // parts
    width = states[0].shape[1]
    c = c_ref[...]
    total = jnp.zeros((rows, 128), jnp.float32)
    for index, step in enumerate(steps):
        start = (column ^ step) * part_width + offset
        cols = pl.ds(pl.multiple_of(start, 128), width)
        read = contract(c, states[index][...], ((1,), (0,)))
        weight = factor[:, cols].astype(jnp.float32)
        value = fixed[:, cols].astype(jnp.float32) + read * weight
        gated[slot_at, index] = value
        square = value * value
        for lanes in range(0, width, 128):
            total = total + square[:, lanes : lanes + 128]
    return total


def read_kernel(parts, steps, offset, slots, place, after, *refs):
    states, own_work, (gated, squares) = refs[: len(steps)], refs[len(steps) : -2], refs[-2:]
    for slot in range(slots):
        squares[slot] = read_slot(
            parts, steps, offset, place[1], slot, states, own_work, gated, slot
        )


def finish_kernel(parts, groups, slots, place, live, gain, *refs):
    inputs, (out, gated, held, sems) = refs[:-4], refs[-4:]
    count = 2 * (len(groups) - 1)
    earlier, inputs = inputs[:count], inputs[count:]
    offset, steps = groups[-1]
    states, own_work = inputs[: len(steps)], inputs[len(steps) :]
    column = place[1]
    slots, rows, features = held.shape
    part_width = features // parts
    copies = []
    for slot in range(slots):
        total = read_slot(parts, steps, offset, column, slot, states, own_work, gated, 0)
        for group in range(len(groups) - 1):
            total = total + earlier[2 * group + 1][slot]
        scale = lax.rsqrt(jnp.sum(total, axis=1, keepdims=True) / features + EPS)
        alive = lax.broadcasted_iota(jnp.int32, (rows, 1), 0) < live[slot]
        scale = jnp.where(alive, scale, 0.0)
        size = rows // parts
        for block in range(parts):
            here = slice(block * size, (block + 1) * size)
            for group, (offset_here, steps_here) in enumerate(groups):
                last = group + 1 == len(groups)
                values = gated if last else earlier[2 * group]
                width = values.shape[-1]
                for index, step in enumerate(steps_here):
                    start = (column ^ step) * part_width + offset_here
                    cols = pl.ds(pl.multiple_of(start, 128), width)
                    gain_here = jnp.reshape(gain[cols], (1, width))
                    value = values[0 if last else slot, index, here]
                    held[slot, here, cols] = (value * scale[here] * gain_here).astype(jnp.bfloat16)
            copies.append(
                pltpu.make_async_copy(
                    held.at[slot, here], out.at[slot, here], sems.at[slot * parts + block]
                )
            )
            copies[-1].start()
    for copy in copies:
        copy.wait()


LASTS = dict(
    pack=2, prompt_weights=2, prompt_state=3, pick=1, merge=1, prepare=0, completion=4, read=2, finish=2
)


def matched(
    prompt_inner,
    prompt_proj,
    prompt_step,
    completion_inner,
    completion_gate,
    completion_projections,
    sample_step,
    sample_length,
    decay_log,
    conv_inner,
    conv_proj,
    norm_gain,
):
    parts = lax.axis_size("comp")
    row, column = lax.axis_index("prompt"), lax.axis_index("comp")
    plane, core = row // 2, row % 2
    group = 2 * column + core
    rows = prompt_inner.shape[0]
    heads = sample_step.shape[0]
    features = heads * HEAD_WIDTH
    place = jnp.stack([plane, column, core, row]).astype(jnp.int32)
    bf16, f32 = jnp.bfloat16, jnp.float32

    def take(array, start, size, axis):
        return lax.dynamic_slice_in_dim(array, start, size, axis)

    planes = lax.axis_size("prompt") // 2
    pair_width = 2 * STATE_WIDTH
    edge = jax.ShapeDtypeStruct((TAIL, pair_width), bf16)
    held_inner = pltpu.with_memory_space_constraint(prompt_inner, pltpu.HBM)
    held_proj = pltpu.with_memory_space_constraint(prompt_proj, pltpu.HBM)
    held_step = pltpu.with_memory_space_constraint(prompt_step, pltpu.HBM)

    swap, edge_1, own_b = run_whole(
        pack_kernel,
        "pack",
        (place,),
        (
            jax.ShapeDtypeStruct((rows + TAIL, pair_width), bf16),
            edge,
            jax.ShapeDtypeStruct((rows, STATE_WIDTH), bf16),
        ),
        (held_inner, held_proj, held_step),
        spaces=[pltpu.HBM] * 3,
        scratch=[
            pltpu.VMEM((heads, rows), f32),
            pltpu.VMEM((TAIL, 2 * features), bf16),
            pltpu.VMEM((TAIL, pair_width), bf16),
            pltpu.VMEM((TAIL, pair_width), bf16),
            pltpu.SemaphoreType.DMA((6,)),
        ],
    )
    trade = lambda z, k, c: (z, 1 - k, c)
    other = routed(swap, trade)
    other_inner = routed(prompt_inner, trade)
    slots, positions = completion_inner.shape[:2]
    wide = jax.ShapeDtypeStruct((positions, features), bf16)
    prepared = {}
    held_gate = pltpu.with_memory_space_constraint(completion_gate, pltpu.HBM)

    def prepare(slot, after, fetch):
        every = jax.ShapeDtypeStruct((heads, positions), f32)
        turned = jax.ShapeDtypeStruct((positions, heads), f32)
        return run_whole(
            lambda *refs: prepare_kernel(slot, fetch, *refs),
            "prepare",
            (place,),
            (wide, wide, every, turned, every, edge),
            (held_gate if fetch else completion_gate, sample_step, decay_log, after),
            spaces=[pltpu.HBM if fetch else pltpu.VMEM] + [pltpu.VMEM] * 3,
            scratch=[
                pltpu.VMEM((positions, features), bf16),
                pltpu.SemaphoreType.DMA((4,)),
            ]
            * fetch,
        )

    for slot in range(1, slots):
        *prepared[slot], edge_1 = prepare(slot, edge_1, True)
    edges = jnp.where(core == 0, other[rows:], edge_1)
    near = routed(edges, lambda z, k, c: (z + 1, k, c) if z + 1 < planes else None)
    far = routed(edges, lambda z, k, c: (c, k, c) if z + 1 == planes else None)
    weights, b_turned, logs, b_first = run_whole(
        prompt_weights_kernel,
        "prompt_weights",
        (place,),
        (
            jax.ShapeDtypeStruct((2 * rows, heads), f32),
            jax.ShapeDtypeStruct((STATE_WIDTH, 2 * rows), bf16),
            jax.ShapeDtypeStruct((8, heads * LOG_LANES), f32),
            jax.ShapeDtypeStruct((TAIL, STATE_WIDTH), bf16),
        ),
        (own_b, other, conv_proj, prompt_step, decay_log),
    )
    unit = features // parts // sum(CHUNKS)
    widths = [unit * size for size in CHUNKS]
    offsets = [sum(widths[:chunk]) for chunk in range(len(widths))]
    picks = []
    for chunk, width in enumerate(widths):
        with_tail = chunk == 0
        message = jax.ShapeDtypeStruct((STATE_WIDTH + TAIL * with_tail, width), bf16)
        spread = jax.ShapeDtypeStruct((STATE_WIDTH + 2 * TAIL * with_tail, width), bf16)
        sent = run_whole(
            lambda *refs, offset=offsets[chunk]: prompt_state_kernel(offset, parts, *refs),
            "prompt_state",
            (place,),
            (spread,) * parts
            + (edge if chunk else jax.ShapeDtypeStruct((STATE_WIDTH, 2 * rows), bf16),),
            (
                prompt_inner, other_inner, near, conv_inner, conv_proj, weights, b_turned, b_first,
                logs, far,
            ),
        )
        if chunk == 0:
            b_turned = sent[parts]
        else:
            *prepared[0], handed = prepare(0, sent[parts], False)
        held = [sent[0]] + [
            routed(sent[step], lambda z, k, c: (z, k, c ^ step)) for step in range(1, parts)
        ]
        two = jax.ShapeDtypeStruct((parts // 2,) + message.shape, bf16)
        picks.append(
            lambda after, held=held, two=two, with_tail=with_tail: run_whole(
                lambda *refs: pick_kernel(parts, *refs),
                "pick",
                (place,),
                (two, two) + (edge,) * with_tail,
                [after] + held,
                spaces=[pl.ANY] + [pltpu.VMEM] * parts,
            )
        )

    held_projections = pltpu.with_memory_space_constraint(completion_projections, pltpu.HBM)
    def completion(slot, after):
        gates, factor, *decays = prepared[slot]
        fixed, c = run_whole(
            lambda *refs: completion_kernel(slot, *refs),
            "completion",
            (place,),
            (wide, jax.ShapeDtypeStruct((positions, STATE_WIDTH), bf16)),
            (
                completion_inner, held_projections, tail, conv_inner, conv_proj, gates, *decays, after,
            ),
            spaces=[pltpu.VMEM, pltpu.HBM] + [pltpu.VMEM] * 7 + [pl.ANY],
            scratch=[
                pltpu.VMEM((positions, features), bf16),
                pltpu.VMEM((2, positions, STATE_WIDTH), bf16),
                pltpu.SemaphoreType.DMA((2,)),
            ],
        )
        return c, fixed, factor

    def merge(bit, chunk, own, came, shapes, given, after):
        table = jax.ShapeDtypeStruct((8, features // parts), f32)
        *outs, factors = run_whole(
            lambda *refs: merge_kernel(bit, chunk, *refs),
            "merge",
            (place,),
            shapes + (table,) * (chunk == 0),
            (own, came, given, after),
            spaces=[pltpu.VMEM] * 2 + [pltpu.VMEM if chunk else pl.ANY, pl.ANY],
        ) + ((given,) if chunk else ())
        return outs, factors

    def gather(state):
        return [state] + [
            routed(state, lambda z, k, c: (z, k, c ^ step)) for step in range(1, parts)
        ]

    work = list(range(slots))
    finished = []

    def do_work(after):
        if not work:
            return after
        finished.append(completion(work.pop(0), after))
        return finished[-1][0]

    stays, goes, go_shapes, merged, joined = [], [], [], [], []
    near_plane = lambda z, k, c: (z ^ 1, k, c)
    far_plane = lambda z, k, c: (z ^ 2, k, c)
    tail, after = None, handed
    for chunk in range(len(widths)):
        stay, go, *maybe = picks[chunk](after)
        tail = maybe[0] if maybe else tail
        stays.append(stay)
        goes.append(routed(go, near_plane))
        go_shapes.append(go.shape[1:])
        if chunk + 1 < len(widths):
            after = do_work(go)
    given = after = go
    for chunk in range(len(widths)):
        one = jax.ShapeDtypeStruct((1,) + go_shapes[chunk], bf16)
        (stay, go), given = merge(
            0, chunk, stays[chunk], goes[chunk], (one, one), given, after
        )
        merged.append((stay, routed(go, far_plane)))
        after = do_work(go)
    given = go
    for chunk, width in enumerate(widths):
        state = jax.ShapeDtypeStruct((STATE_WIDTH, width), bf16)
        (state,), given = merge(1, chunk, *merged[chunk], (state,), given, go)
        joined.append(gather(state))
    after = state
    while work:
        after = do_work(after)
    own_work = [array for three in finished for array in three]
    every = tuple(range(parts))
    groups = [(chunk, every) for chunk in range(len(widths) - 1)]
    groups.append((len(widths) - 1, every))
    earlier = []
    for chunk, steps in groups[:-1]:
        earlier += run_whole(
            lambda *refs, steps=steps, offset=offsets[chunk]: read_kernel(
                parts, steps, offset, slots, *refs
            ),
            "read",
            (place,),
            (
                jax.ShapeDtypeStruct((slots, len(steps), positions, widths[chunk]), f32),
                jax.ShapeDtypeStruct((slots, positions, 128), f32),
            ),
            [earlier[-1] if earlier else joined[chunk][0]]
            + [joined[chunk][step] for step in steps]
            + own_work,
            spaces=[pl.ANY] + [pltpu.VMEM] * (len(steps) + len(own_work)),
        )
    chunk, steps = groups[-1]
    groups = [(offsets[chunk], steps) for chunk, steps in groups]
    return run_whole(
        lambda *refs: finish_kernel(parts, groups, slots, *refs),
        "finish",
        (place, sample_length),
        jax.ShapeDtypeStruct((slots, positions, features), bf16),
        [norm_gain] + earlier + [joined[chunk][step] for step in steps] + own_work,
        out_spaces=pltpu.HBM,
        scratch=[
            pltpu.VMEM((1, len(steps), positions, widths[-1]), f32),
            pltpu.VMEM((slots, positions, features), bf16),
            pltpu.SemaphoreType.DMA((slots * parts,)),
        ],
    )


def run_whole(
    kernel, name, place, out_shape, operands, scratch=(), spaces=None, out_spaces=None, aliases=None
):
    vmem = pltpu.VMEM
    spaces = spaces or [vmem] * len(operands)
    out_spaces = out_spaces or jax.tree.map(lambda _: vmem, out_shape)
    return pl.pallas_call(
        kernel,
        out_shape=out_shape,
        in_specs=[pl.BlockSpec(memory_space=pltpu.SMEM)] * len(place)
        + [pl.BlockSpec(memory_space=space) for space in spaces],
        out_specs=jax.tree.map(lambda space: pl.BlockSpec(memory_space=space), out_spaces),
        scratch_shapes=scratch,
        input_output_aliases=aliases or {},
        compiler_params=pltpu.CompilerParams(vmem_limit_bytes=VMEM_BYTES),
        cost_estimate=pl.CostEstimate(
            flops=LASTS[name] * 10**9, transcendentals=0, bytes_accessed=LASTS[name] * 3 * 10**6
        ),
        name=name,
    )(*place, *operands)


def local(*arrays):
    columns, prompts = lax.axis_size("comp"), lax.axis_size("prompt")
    heads_col, heads_row = arrays[2].shape[0], arrays[6].shape[0]
    one_group = heads_row == STATE_HEADS // STATE_GROUPS and heads_col == 2 * heads_row
    if one_group and prompts == 2 * columns and columns & (columns - 1) == 0:
        return matched(*arrays)
    return any_shape(*arrays)


def solution(mesh):
    placed = (
        P("prompt", "comp"),
        P("prompt", None),
        P("comp", "prompt"),
        P("comp", None, "prompt"),
        P("comp", None, "prompt"),
        P("comp", None, None),
        P("prompt", "comp", None),
        P("comp"),
        P(),
        P(),
        P(),
        P("prompt"),
    )
    return jax.shard_map(
        local, mesh=mesh, in_specs=placed, out_specs=P("comp", None, "prompt"), check_vma=False
    )
```

```python
import jax
import jax.numpy as jnp
from jax import lax
from jax.experimental import pallas as pl
from jax.experimental.pallas import tpu as pltpu
from jax.sharding import PartitionSpec as P

STATE_HEADS = 256
HEAD_WIDTH = 64
STATE_WIDTH = 256
STATE_GROUPS = 8
CONV = 4
BLOCK = 128


EPS = 1e-05
HIGHEST = lax.Precision.HIGHEST


def from_behind(block, axis, distance):
    devices = range(lax.axis_size(axis))
    route = [(i - distance, i) for i in devices if i - distance in devices]
    return lax.ppermute(block, axis, route)


def carried_in(array, axis, combine, identity):
    peers, position = (lax.axis_size(axis), lax.axis_index(axis))
    everything = jax.tree.map(
        lambda part, kind: lax.all_gather(part.astype(kind), axis),
        array,
        (jnp.bfloat16, jnp.bfloat16),
    )
    start = jax.tree.map(
        lambda part, zero: jnp.broadcast_to(jnp.asarray(zero, part.dtype), part.shape),
        array,
        identity,
    )

    def hop(k, before):
        reached = k < position
        new = combine(
            before, jax.tree.map(lambda part, own: part[k].astype(own.dtype), everything, array)
        )
        return jax.tree.map(lambda a, b: jnp.where(reached, a, b), new, before)

    return lax.fori_loop(0, peers, hop, start)


def from_root(array, axis, root):
    mine = lax.axis_index(axis) == root
    return lax.psum(jnp.where(mine, array, jnp.zeros_like(array)), axis)


def from_partner(block, axis, stride):
    count = lax.axis_size(axis)
    route = []
    for low in range(count):
        high = low | 1 << stride
        if high != low and high < count:
            route += [(low, high), (high, low)]
    return lax.ppermute(block, axis, route)


def causal_conv(source, kernel, leading):
    padded = jnp.concatenate([leading, source], axis=0).astype(jnp.float32)
    kernel_wide = kernel.astype(jnp.float32)
    row_count = source.shape[0]
    summed = jnp.zeros(source.shape, jnp.float32)
    for offset in range(kernel.shape[0]):
        summed = summed + kernel_wide[offset] * padded[offset : offset + row_count]
    return jax.nn.silu(summed).astype(jnp.bfloat16)


def block_scan(state_in, inner_blk, b_blk, c_blk, step_blk, rate_vals):
    cumul = jnp.cumsum(-rate_vals[:, :, None] * step_blk, axis=2)
    scores = jnp.einsum("ign,jgn->gij", c_blk, b_blk, preferred_element_type=jnp.float32)
    spread_log = cumul[:, :, :, None] - cumul[:, :, None, :]
    length_q = step_blk.shape[2]
    causal = jnp.arange(length_q)[:, None] >= jnp.arange(length_q)[None, :]
    decay_mat = jnp.exp(jnp.where(causal, spread_log, -jnp.inf))
    mixer_w = (scores[:, None] * decay_mat * step_blk[:, :, None, :]).astype(jnp.bfloat16)
    intra_part = jnp.einsum(
        "gkij,jgkd->igkd", mixer_w, inner_blk, preferred_element_type=jnp.float32
    )
    readout = jnp.einsum("ign,gkdn->igkd", c_blk.astype(jnp.float32), state_in, precision=HIGHEST)
    inter_part = jnp.transpose(jnp.exp(cumul), (2, 0, 1))[..., None] * readout
    weights = jnp.exp(cumul[:, :, -1:] - cumul) * step_blk
    packed = (inner_blk.astype(jnp.float32) * jnp.transpose(weights, (2, 0, 1))[..., None]).astype(
        jnp.bfloat16
    )
    fresh_part = jnp.einsum("jgn,jgkd->gkdn", b_blk, packed, preferred_element_type=jnp.float32)
    return (
        intra_part + inter_part,
        jnp.exp(cumul[:, :, -1])[..., None, None] * state_in + fresh_part,
    )


def any_shape(
    prompt_inner,
    prompt_proj,
    prompt_step,
    completion_inner,
    completion_gate,
    completion_projections,
    sample_step,
    sample_length,
    decay_log,
    conv_inner,
    conv_proj,
    norm_gain,
):
    prompt_count = lax.axis_size("prompt")
    prompt_idx = lax.axis_index("prompt")
    column_idx = lax.axis_index("comp")
    heads_group = STATE_HEADS // STATE_GROUPS
    heads_col = prompt_step.shape[0]
    heads_row = sample_step.shape[0]
    state_feats = STATE_GROUPS * STATE_WIDTH
    lag_rows = CONV - 1
    rows_prompt = prompt_inner.shape[0]
    prev_inner, prev_proj = from_behind(
        (
            prompt_inner[rows_prompt - lag_rows :],
            prompt_proj[rows_prompt - lag_rows :, :state_feats],
        ),
        "prompt",
        1,
    )
    col_start = column_idx * heads_col
    conv_col = lax.dynamic_slice_in_dim(
        conv_inner, col_start * HEAD_WIDTH, heads_col * HEAD_WIDTH, 1
    )
    inner_conv = causal_conv(prompt_inner, conv_col, prev_inner)
    b_conv = causal_conv(prompt_proj[:, :state_feats], conv_proj[:, :state_feats], prev_proj)
    rate_col = jnp.exp(lax.dynamic_slice_in_dim(decay_log, col_start, heads_col, 0))
    step_col = jax.nn.softplus(prompt_step)
    cumul = jnp.cumsum(-rate_col[:, None] * step_col, axis=1)
    local_log = cumul[:, -1]
    weight_col = jnp.exp(local_log[:, None] - cumul) * step_col
    group_span = max(1, heads_col // heads_group)
    per_group = heads_col // group_span
    group_start = col_start // heads_group
    b_select = lax.dynamic_slice_in_dim(
        b_conv.reshape(rows_prompt, STATE_GROUPS, STATE_WIDTH), group_start, group_span, 1
    ).astype(jnp.float32)
    scaled = (
        inner_conv.astype(jnp.float32).reshape(rows_prompt, heads_col, HEAD_WIDTH)
        * jnp.transpose(weight_col)[:, :, None]
    )
    scaled = scaled.reshape(rows_prompt, group_span, per_group, HEAD_WIDTH)
    local_state = jnp.einsum("tgn,tghd->ghdn", b_select, scaled, precision=HIGHEST).reshape(
        heads_col, HEAD_WIDTH, STATE_WIDTH
    )
    own_inner = prompt_inner[rows_prompt - lag_rows :].astype(jnp.float32)
    own_proj = prompt_proj[rows_prompt - lag_rows :].astype(jnp.float32)
    last_index = prompt_count - 1
    head_start = prompt_idx * heads_row
    owner = head_start // heads_col
    head_offset = head_start - owner * heads_col

    def combine(earlier, later):
        return (earlier[0] + later[0], earlier[1] * jnp.exp(later[0])[:, None, None] + later[1])

    before = carried_in(
        (local_log, local_state),
        "prompt",
        combine,
        (jnp.zeros_like(local_log), jnp.zeros_like(local_state)),
    )
    through = combine(before, (local_log, local_state))[1]
    final_state, tail_inner, tail_proj = (
        from_root(through.astype(jnp.bfloat16), "prompt", last_index).astype(through.dtype),
        from_root(own_inner.astype(jnp.bfloat16), "prompt", last_index).astype(own_inner.dtype),
        from_root(own_proj.astype(jnp.bfloat16), "prompt", last_index).astype(own_proj.dtype),
    )
    moved_state, moved_inner = (
        from_root(final_state.astype(jnp.bfloat16), "comp", owner).astype(final_state.dtype),
        from_root(tail_inner.astype(jnp.bfloat16), "comp", owner).astype(tail_inner.dtype),
    )
    start_state = lax.dynamic_slice_in_dim(moved_state, head_offset, heads_row, 0)
    lead_inner = lax.dynamic_slice_in_dim(
        moved_inner, head_offset * HEAD_WIDTH, heads_row * HEAD_WIDTH, 1
    ).astype(jnp.bfloat16)
    group_row = head_start // heads_group
    b_start = group_row * STATE_WIDTH
    c_start = state_feats + group_row * STATE_WIDTH
    proj_select = jnp.concatenate(
        [
            lax.dynamic_slice_in_dim(completion_projections, b_start, STATE_WIDTH, 2),
            lax.dynamic_slice_in_dim(completion_projections, c_start, STATE_WIDTH, 2),
        ],
        axis=2,
    )
    kernel_select = jnp.concatenate(
        [
            lax.dynamic_slice_in_dim(conv_proj, b_start, STATE_WIDTH, 1),
            lax.dynamic_slice_in_dim(conv_proj, c_start, STATE_WIDTH, 1),
        ],
        axis=1,
    )
    lead_wide = tail_proj.astype(jnp.bfloat16)
    lead_select = jnp.concatenate(
        [
            lax.dynamic_slice_in_dim(lead_wide, b_start, STATE_WIDTH, 1),
            lax.dynamic_slice_in_dim(lead_wide, c_start, STATE_WIDTH, 1),
        ],
        axis=1,
    )
    conv_row = lax.dynamic_slice_in_dim(
        conv_inner, head_start * HEAD_WIDTH, heads_row * HEAD_WIDTH, 1
    )
    rate_row = jnp.exp(lax.dynamic_slice_in_dim(decay_log, head_start, heads_row, 0))
    step_row = jax.nn.softplus(sample_step)
    slot_count = completion_inner.shape[0]
    sample_len = completion_inner.shape[1]
    block_count = sample_len // BLOCK

    def advance(carry, block_in):
        block_out, carry_next = block_scan(
            carry, block_in[0], block_in[1], block_in[2], block_in[3], rate_row[None]
        )
        return (carry_next, block_out)

    gated_list = []
    square_list = []
    for slot in range(slot_count):
        slot_conv = causal_conv(completion_inner[slot], conv_row, lead_inner)
        proj_conv = causal_conv(proj_select[slot], kernel_select, lead_select)
        inner_blocks = slot_conv.reshape(block_count, BLOCK, 1, heads_row, HEAD_WIDTH)
        b_blocks = proj_conv[:, :STATE_WIDTH].reshape(block_count, BLOCK, 1, STATE_WIDTH)
        c_blocks = proj_conv[:, STATE_WIDTH:].reshape(block_count, BLOCK, 1, STATE_WIDTH)
        step_blocks = jnp.transpose(
            step_row[:, slot].reshape(heads_row, block_count, BLOCK), (1, 0, 2)
        )[:, None]
        block_inputs = (inner_blocks, b_blocks, c_blocks, step_blocks)
        _, block_outs = lax.scan(advance, start_state[None], block_inputs)
        ssm_out = block_outs.reshape(sample_len, heads_row * HEAD_WIDTH)
        gated = ssm_out * jax.nn.silu(completion_gate[slot].astype(jnp.float32))
        gated_list.append(gated)
        square_list.append(jnp.sum(gated * gated, axis=1))
    square_all = jnp.stack(square_list)
    partner_bits = (prompt_count // STATE_GROUPS).bit_length() - 1
    for bit_number in range(partner_bits):
        square_all = square_all + from_partner(square_all, "prompt", bit_number)
    scale_all = lax.rsqrt(square_all / (heads_group * HEAD_WIDTH) + EPS)
    gated_all = jnp.stack(gated_list)
    result = gated_all * scale_all[:, :, None] * norm_gain[None, None, :]
    live_rows = jnp.arange(sample_len)[None, :] < sample_length[:, None]
    return jnp.where(live_rows[:, :, None], result, 0.0).astype(jnp.bfloat16)


LOG2E = 1.4426950408889634
AXES = ("prompt", "comp")
CHUNKS = (1, 1)
LOG_LANES = 32
TAIL = 16
VMEM_BYTES = 16 * 1024 * 1024


def routed(block, route):
    columns = lax.axis_size("comp")
    pairs = []
    for row in range(lax.axis_size("prompt")):
        for column in range(columns):
            target = route(row // 2, row % 2, column)
            if target is not None:
                plane, core, to = target
                pairs.append((row * columns + column, (2 * plane + core) * columns + to))
    return lax.ppermute(block, AXES, pairs)


def silu_of_twice(half):
    return half + half * jnp.tanh(half)


def conv_rows(taps, lead, block):
    wide = 0.5 * taps.astype(jnp.float32)
    rows = block.astype(jnp.float32)
    edge = jnp.concatenate([lead.astype(jnp.float32)[TAIL - 8 :], rows[0:8]], axis=0)
    total = wide[CONV - 1 : CONV] * rows
    for back in range(1, CONV):
        shifted = pltpu.roll(rows, back, 0)
        shifted = jnp.concatenate([edge[8 - back : 16 - back], shifted[8:]], axis=0)
        total = total + wide[CONV - 1 - back : CONV - back] * shifted
    return silu_of_twice(total)


def spread_heads(first, heads, width):
    row = lax.broadcasted_iota(jnp.int32, (heads, width), 0)
    col = lax.broadcasted_iota(jnp.int32, (heads, width), 1)
    return row == first + col // HEAD_WIDTH


def contract(lhs, rhs, dims, precision=None):
    return lax.dot_general(
        lhs, rhs, (dims, ((), ())), preferred_element_type=jnp.float32, precision=precision
    )


def in_three(value):
    high = value.astype(jnp.bfloat16)
    rest = value - high.astype(jnp.float32)
    mid = rest.astype(jnp.bfloat16)
    low = (rest - mid.astype(jnp.float32)).astype(jnp.bfloat16)
    return high, mid, low


def softplus(value):
    return jnp.maximum(value, 0.0) + jnp.log1p(jnp.exp(-jnp.abs(value)))


def group_of(decay, index, size):
    every = jnp.reshape(decay[...], (1, decay.shape[0]))
    count = decay.shape[0]
    return pltpu.roll(every, lax.rem(count - index * size, count), 1)[:, 0:size]


def pack_kernel(
    place, inner, proj, step, swap_out, edge_out, own_out, step_in, inner_in, b_in, c_in, sems
):
    heads, rows = step_in.shape
    features = heads * HEAD_WIDTH
    column, core = place[1], place[2]
    theirs = 1 - core
    pair = 2 * STATE_WIDTH

    def columns(first, size):
        return pl.ds(pl.multiple_of(first * size, size), size)

    last = slice(rows - TAIL, rows)
    copies = [
        (step.at[columns(theirs, heads)], step_in),
        (inner.at[last], inner_in),
        (proj.at[last, columns(column, pair)], b_in),
        (proj.at[last, columns(STATE_GROUPS // 2 + column, pair)], c_in),
        (proj.at[:, columns(2 * column + theirs, STATE_WIDTH)], swap_out.at[0:rows, 0:STATE_WIDTH]),
        (proj.at[:, columns(2 * column + core, STATE_WIDTH)], own_out),
    ]
    copies = [
        pltpu.make_async_copy(source, target, sems.at[index])
        for index, (source, target) in enumerate(copies)
    ]
    for copy in copies:
        copy.start()
    copies[0].wait()
    dt = jnp.transpose(softplus(step_in[...]))
    high = dt.astype(jnp.bfloat16)
    low = (dt - high.astype(jnp.float32)).astype(jnp.bfloat16)
    swap_out[0:rows, STATE_WIDTH:pair] = jnp.concatenate([high, low] * (STATE_WIDTH // heads // 2), axis=1)
    for copy in copies[1:4]:
        copy.wait()
    edges = []
    for to in range(2):
        group = slice(to * STATE_WIDTH, (to + 1) * STATE_WIDTH)
        inner_last = inner_in[:, to * features : (to + 1) * features].astype(jnp.float32)
        bc_last = jnp.concatenate([b_in[:, group], c_in[:, group]], axis=1)
        pieces = [inner_last[TAIL - 3 :, at : at + pair] for at in range(0, features, pair)]
        pieces.append(bc_last.astype(jnp.float32)[TAIL - 3 :])
        pieces.append(jnp.zeros((TAIL - 3 * len(pieces), pair), jnp.float32))
        edges.append(jnp.concatenate(pieces, axis=0))
    swap_out[rows:] = jnp.where(core == 0, edges[1], edges[0]).astype(jnp.bfloat16)
    edge_out[...] = edges[1].astype(jnp.bfloat16)
    for copy in copies[4:]:
        copy.wait()


def log_lanes(high, low):
    lane = lax.broadcasted_iota(jnp.int32, high.shape, 1)
    return jnp.where(lane % LOG_LANES < LOG_LANES // 2, high, low)


def logs_of(tiles, width):
    rows = [tile.astype(jnp.float32)[TAIL - 1 : TAIL] for tile in tiles]
    lanes = rows[0].shape[1]
    rows.append(jnp.zeros((8 - len(rows), lanes), jnp.float32))
    source = lax.broadcasted_iota(jnp.int32, (lanes, width + lanes), 0)
    target = lax.broadcasted_iota(jnp.int32, (lanes, width + lanes), 1)
    head = jnp.where(target < width, target >> 6, (target - width) >> 5)
    pick = (source >> 5 == head) & ((source & (LOG_LANES // 2 - 1)) == 0)
    rows = jnp.concatenate(rows, axis=0).astype(jnp.bfloat16)
    found = contract(rows, pick.astype(jnp.bfloat16), ((1,), (0,)))
    return found[:, 0:width], found[:, width:]


def prompt_weights_kernel(
    place, own, other, taps_b, step, decay, w_out, b_out, log_out, first_out
):
    rows = own.shape[0]
    heads = step.shape[0] // 2
    group = 2 * place[1] + place[2]
    own_b = own[...]
    other_b = other[0:rows, 0:STATE_WIDTH]
    other_dt = other[0:rows, STATE_WIDTH : STATE_WIDTH + 2 * heads]
    taps = taps_b[:, pl.ds(pl.multiple_of(group * STATE_WIDTH, STATE_WIDTH), STATE_WIDTH)]
    own_step = step[pl.ds(pl.multiple_of(place[2] * heads, heads), heads)]
    core = place[2]
    first_own = core == 0
    rate = jnp.exp(group_of(decay, 2 * place[1] + core, heads))
    dt_own = jnp.transpose(softplus(own_step))
    parts = other_dt.astype(jnp.float32)
    dt_other = parts[:, 0:heads] + parts[:, heads : 2 * heads]
    row = lax.broadcasted_iota(jnp.int32, (rows, rows), 0)
    col = lax.broadcasted_iota(jnp.int32, (rows, rows), 1)
    later = (col > row).astype(jnp.bfloat16)
    both = jnp.concatenate([dt_own, dt_other], axis=1)
    after = contract(later, jnp.concatenate(in_three(both), axis=1), ((1,), (0,)))
    size = 2 * heads
    after = after[:, 0:size] + after[:, size : 2 * size] + after[:, 2 * size :]
    sum_own = after[0:1, 0:heads] + dt_own[0:1]
    sum_other = after[0:1, heads:] + dt_other[0:1]
    after_own = after[:, 0:heads] + jnp.where(first_own, sum_other, 0.0)
    after_other = after[:, heads:] + jnp.where(first_own, 0.0, sum_own)
    w_out[0:rows] = jnp.exp(-rate * after_own) * dt_own
    w_out[rows:] = jnp.exp(-rate * after_other) * dt_other
    total = jnp.broadcast_to(-rate * (sum_own + sum_other), (8, heads))
    high = total.astype(jnp.bfloat16)
    low = (total - high.astype(jnp.float32)).astype(jnp.bfloat16)
    row = lax.broadcasted_iota(jnp.int32, (heads, heads * LOG_LANES), 0)
    lane = lax.broadcasted_iota(jnp.int32, (heads, heads * LOG_LANES), 1)
    spread = (row == lane // LOG_LANES).astype(jnp.bfloat16)
    log_out[...] = log_lanes(
        contract(high, spread, ((1,), (0,))), contract(low, spread, ((1,), (0,)))
    )
    own_last, other_last = own_b[rows - TAIL :], other_b[rows - TAIL :]
    first = jnp.where(first_own, own_b[0:TAIL].astype(jnp.float32), other_b[0:TAIL].astype(jnp.float32))
    first_out[...] = first.astype(jnp.bfloat16)
    blank = jnp.zeros((TAIL, STATE_WIDTH), jnp.float32)
    lead_own = jnp.where(first_own, blank, other_last.astype(jnp.float32))
    lead_other = jnp.where(first_own, own_last.astype(jnp.float32), blank)
    conv_own = conv_rows(taps, lead_own, own_b)
    b_out[:, 0:rows] = jnp.transpose(conv_own).astype(jnp.bfloat16)
    conv_other = conv_rows(taps, lead_other, other_b)
    b_out[:, rows:] = jnp.transpose(conv_other).astype(jnp.bfloat16)


def prompt_state_kernel(
    offset, parts, place, inner, other, near, taps, taps_b, weights, b_turned, b_first, logs, tail,
    *rest,
):
    outs, handed = rest[:parts], rest[parts]
    patch = offset == 0
    b_here = handed if patch else b_turned
    column, core = place[1], place[2]
    group = 2 * column + core
    first_own = core == 0
    rows = inner.shape[0]
    width = outs[0].shape[1]
    heads = weights.shape[1]
    features = heads * HEAD_WIDTH
    part_width = features // parts
    state = b_turned.shape[0]
    w = weights[...].astype(jnp.bfloat16)
    before = jnp.where(place[0] == 0, 0.0, near[...].astype(jnp.float32))
    if patch:
        blank = jnp.zeros((TAIL - 3, STATE_WIDTH), jnp.float32)
        lead_b = jnp.concatenate([blank, before[3 * parts : 3 * parts + 3, 0:STATE_WIDTH]], axis=0)
        taps_here = taps_b[:, pl.ds(pl.multiple_of(group * STATE_WIDTH, STATE_WIDTH), STATE_WIDTH)]
        fresh = conv_rows(taps_here, lead_b, b_first[...])
        fresh = jnp.transpose(jnp.concatenate([fresh, jnp.zeros((128 - TAIL, state), jnp.float32)], axis=0))
        lane = lax.broadcasted_iota(jnp.int32, fresh.shape, 1)
        for index, first in enumerate((core == 0, core == 1)):
            at = index * rows
            old = b_turned[:, at : at + 128].astype(jnp.float32)
            patched = jnp.where(lane < jnp.where(first, CONV - 1, 0), fresh, old)
            b_here[:, at : at + 128] = patched.astype(jnp.bfloat16)
            b_here[:, at + 128 : at + rows] = b_turned[:, at + 128 : at + rows]
    blank = jnp.zeros((TAIL - 3, width), jnp.float32)
    for turn in range(parts):
        part = column ^ turn
        start = part * part_width + offset
        cols = pl.ds(pl.multiple_of(start, 128), width)
        tap_cols = pl.ds(pl.multiple_of(group * features + start, 128), width)
        spread = spread_heads(start // HEAD_WIDTH, heads, width).astype(jnp.bfloat16)
        w_wide = contract(w, spread, ((1,), (0,)))
        own_cols = pl.ds(pl.multiple_of(core * features + start, 128), width)
        own_x, other_x = inner[:, own_cols], other[:, own_cols]
        halo = before[0:3, offset : offset + width]
        for index in range(1, parts):
            at = before[3 * index : 3 * index + 3, offset : offset + width]
            halo = jnp.where(part == index, at, halo)
        halo = jnp.concatenate([blank, halo], axis=0)
        own_last, other_last = own_x[rows - TAIL :], other_x[rows - TAIL :]
        lead_own = jnp.where(first_own, halo, other_last.astype(jnp.float32))
        lead_other = jnp.where(first_own, own_last.astype(jnp.float32), halo)
        x_own = conv_rows(taps[:, tap_cols], lead_own, own_x) * w_wide[0:rows]
        x_other = conv_rows(taps[:, tap_cols], lead_other, other_x) * w_wide[rows:]
        mine = contract(b_here[:, 0:rows], x_own.astype(jnp.bfloat16), ((1,), (0,)))
        theirs = contract(b_here[:, rows:], x_other.astype(jnp.bfloat16), ((1,), (0,)))
        outs[turn][0:state] = (mine + theirs).astype(jnp.bfloat16)
        if outs[turn].shape[0] > state:
            log_width = part_width * LOG_LANES // HEAD_WIDTH
            at = pl.ds(pl.multiple_of(part * log_width, log_width), log_width)
            pieces = tail[:, 0:width].astype(jnp.float32)
            row = lax.broadcasted_iota(jnp.int32, pieces.shape, 0)
            pieces = jnp.where(row == TAIL - 1, logs[0:1, at], pieces)
            outs[turn][state : state + TAIL] = pieces.astype(jnp.bfloat16)
            outs[turn][state + TAIL :] = tail[:, width:]
    if not patch:
        handed[...] = tail[...]


def pick_kernel(count, place, after, *refs):
    held, (goes, *more) = refs[:count], refs[count:]
    stays, tails = more[:1], more[1:]
    turn = place[0] ^ place[1]
    rows, width = goes.shape[1:]
    for index in range(count):

        @pl.when(turn == index)
        def _():
            for step in range(0, count, 2):
                goes[step // 2] = held[index ^ (step + 1)][0:rows]
                for stay in stays:
                    stay[step // 2] = held[index ^ step][0:rows]
            for tail in tails:
                tail[:, 0:width] = held[index][rows - TAIL : rows]
                tail[:, width:] = held[index][rows:]


def merge_held_kernel(bit, chunk, place, *refs):
    count = lax.axis_size("comp")
    turn = place[0] ^ place[1]
    for index in range(count):

        @pl.when(turn == index)
        def _():
            own = [refs[index ^ step] for step in range(0, count, 2)]
            merge_kernel(bit, chunk, place, own, *refs[count:])


def merge_kernel(bit, chunk, place, own, came, given, after, *refs):
    count, rows, width = came.shape
    own = own if isinstance(own, list) else [own.at[index] for index in range(count)]
    state = STATE_WIDTH
    first = (place[0] >> bit) & 1 == 0
    outs = refs if chunk else refs[:-1]
    factors = given if chunk else refs[-1]
    if chunk == 0:
        last = slice(state, state + TAIL)
        tiles = [tile for at in range(count) for tile in (own[at][last], came[at, last])]
        wide, lanes = logs_of(tiles, factors.shape[1])
        row = lax.broadcasted_iota(jnp.int32, wide.shape, 0)
        other = jnp.where(row % 2 == 0, pltpu.roll(wide, 7, 0), pltpu.roll(wide, 1, 0))
        scaled = (row % 2 == 0) == first
        factors[...] = jnp.exp(jnp.where(scaled, other, 0.0))
    for index in range(count):
        cols = slice(chunk * width, (chunk + 1) * width)
        mine_by = factors[2 * index : 2 * index + 1, cols]
        theirs_by = factors[2 * index + 1 : 2 * index + 2, cols]
        joined = own[index][0:state].astype(jnp.float32) * mine_by
        joined = joined + came[index, 0:state].astype(jnp.float32) * theirs_by
        if count == 1:
            outs[0][...] = joined.astype(jnp.bfloat16)
            continue
        outs[index][0, 0:state] = joined.astype(jnp.bfloat16)
        if rows > state:
            total = lanes[2 * index : 2 * index + 1] + lanes[2 * index + 1 : 2 * index + 2]
            total = jnp.broadcast_to(total, (8, total.shape[1]))
            high = total.astype(jnp.bfloat16).astype(jnp.float32)
            compact = log_lanes(high, total - high)
            compact = jnp.concatenate([compact, compact], axis=0)
            outs[index][0, state:] = compact.astype(jnp.bfloat16)


def prepare_kernel(
    slot, fetch, place, gate, step, decay, after,
    gate_out, factor_out, cum_out, turned_out, log_out, after_out, *rest,
):
    rows, features = gate_out.shape
    size = rows // 4
    copies = []
    if fetch:
        gate_in, sems = rest
        copies = [
            pltpu.make_async_copy(
                gate.at[slot, at : at + size], gate_in.at[at : at + size], sems.at[index]
            )
            for index, at in enumerate(range(0, rows, size))
        ]
    for copy in copies:
        copy.start()
    after_out[...] = after[...]
    heads = step.shape[0]
    row = lax.broadcasted_iota(jnp.int32, (rows, rows), 0)
    col = lax.broadcasted_iota(jnp.int32, (rows, rows), 1)
    dt = softplus(step[:, slot])
    decay_row = jnp.broadcast_to(group_of(decay, place[3], heads), (8, heads))
    decay_col = jnp.transpose(decay_row)[:, 0:1]
    before = (row <= col).astype(jnp.bfloat16)
    cum = contract(jnp.concatenate(in_three(dt), axis=0), before, ((1,), (0,)))
    cum = cum[0:heads] + cum[heads : 2 * heads] + cum[2 * heads :]
    cum = cum * (-LOG2E * jnp.exp(decay_col))
    log_dt = jnp.log(dt) * LOG2E
    cum_out[...] = cum - log_dt
    log_out[...] = log_dt
    turned = jnp.transpose(cum)
    turned_out[...] = turned
    decays = jnp.exp2(turned).astype(jnp.bfloat16)
    width = 2 * STATE_WIDTH
    for index, top in enumerate(range(0, rows, size)):
        if fetch:
            copies[index].wait()
        here = slice(top, top + size)
        for at in range(0, features, width):
            cols = slice(at, at + width)
            gate_here = gate_in[here, cols] if fetch else gate[slot, here, cols]
            silu_gate = silu_of_twice(0.5 * gate_here.astype(jnp.float32))
            gate_out[here, cols] = silu_gate.astype(jnp.bfloat16)
            spread = spread_heads(at // HEAD_WIDTH, heads, width).astype(jnp.bfloat16)
            decay_wide = contract(decays[here], spread, ((1,), (0,)))
            factor_out[here, cols] = (decay_wide * silu_gate).astype(jnp.bfloat16)


def completion_kernel(
    slot, place, inner, proj, tail, taps, taps_bc, gates, base_rows, cum_cols, log_dt, after,
    fixed_out, c_out, x_held, bc_in, sems,
):
    rows, features = fixed_out.shape
    heads = base_rows.shape[0]
    half = rows // 2
    own = place[3]
    state = STATE_WIDTH
    copies = [
        pltpu.make_async_copy(
            proj.at[slot, :, pl.ds(pl.multiple_of((own + skip) * state, state), state)],
            bc_in.at[index],
            sems.at[index],
        )
        for index, skip in enumerate((0, STATE_GROUPS))
    ]
    for copy in copies:
        copy.start()
    edges = tail[...].astype(jnp.float32)
    pair_width = edges.shape[1]
    blank = jnp.zeros((TAIL - 3, pair_width), jnp.float32)
    row = lax.broadcasted_iota(jnp.int32, (rows, rows), 0)
    col = lax.broadcasted_iota(jnp.int32, (rows, rows), 1)
    blocks = features // pair_width
    for block in range(blocks):
        at = block * pair_width
        cols = slice(at, at + pair_width)
        lead = jnp.concatenate([blank, edges[3 * block : 3 * block + 3]], axis=0)
        taps_here = taps[:, pl.ds(pl.multiple_of(own * features + at, pair_width), pair_width)]
        x_held[:, cols] = conv_rows(taps_here, lead, inner[slot, :, cols]).astype(jnp.bfloat16)
    for copy in copies:
        copy.wait()
    lead_bc = jnp.concatenate([blank, edges[3 * blocks : 3 * blocks + 3]], axis=0)
    bc = []
    for index, skip in enumerate((0, STATE_GROUPS)):
        taps_here = taps_bc[:, pl.ds(pl.multiple_of((own + skip) * state, state), state)]
        lead = lead_bc[:, index * state : (index + 1) * state]
        bc.append(conv_rows(taps_here, lead, bc_in[index]).astype(jnp.bfloat16))
    c_out[...] = bc[1]
    scores = contract(bc[1], bc[0], ((1,), (1,)))
    scores = jnp.where(row >= col, scores, 0.0)
    low, high_left, high_right = scores[0:half, 0:half], scores[half:, 0:half], scores[half:, half:]
    pair = 2 * HEAD_WIDTH
    lane = lax.broadcasted_iota(jnp.int32, (rows, pair), 1)
    for first in range(0, heads, 2):
        cols = slice(first * HEAD_WIDTH, first * HEAD_WIDTH + pair)
        x_pair = x_held[:, cols]
        zero = jnp.zeros_like(x_pair)
        left = jnp.where(lane < HEAD_WIDTH, x_pair, zero)
        right = jnp.where(lane < HEAD_WIDTH, zero, x_pair)
        lows, highs = [], []
        for h in (first, first + 1):
            cc = cum_cols[:, h : h + 1]
            rr, ll = base_rows[h : h + 1], log_dt[h : h + 1]
            grown = jnp.minimum(cc[0:half] - rr[:, 0:half], ll[:, 0:half])
            lows.append((low * jnp.exp2(grown)).astype(jnp.bfloat16))
            grown = jnp.minimum(cc[half:] - rr[:, 0:half], ll[:, 0:half])
            highs.append((high_left * jnp.exp2(grown)).astype(jnp.bfloat16))
            grown = jnp.minimum(cc[half:] - rr[:, half:], ll[:, half:])
            highs.append((high_right * jnp.exp2(grown)).astype(jnp.bfloat16))
        y_low = contract(
            jnp.concatenate(lows, axis=1),
            jnp.concatenate([left[0:half], right[0:half]], axis=0),
            ((1,), (0,)),
        )
        y_high = contract(
            jnp.concatenate(highs, axis=1), jnp.concatenate([left, right], axis=0), ((1,), (0,))
        )
        fixed_out[0:half, cols] = (y_low * gates[0:half, cols].astype(jnp.float32)).astype(jnp.bfloat16)
        fixed_out[half:, cols] = (y_high * gates[half:, cols].astype(jnp.float32)).astype(jnp.bfloat16)


def read_slot(parts, steps, offset, column, slot, states, own_work, gated, slot_at):
    c_ref, fixed, factor = own_work[3 * slot : 3 * slot + 3]
    rows, features = fixed.shape
    part_width = features // parts
    width = states[0].shape[1]
    c = c_ref[...]
    total = jnp.zeros((rows, 128), jnp.float32)
    for index, step in enumerate(steps):
        start = (column ^ step) * part_width + offset
        cols = pl.ds(pl.multiple_of(start, 128), width)
        read = contract(c, states[index][...], ((1,), (0,)))
        weight = factor[:, cols].astype(jnp.float32)
        value = fixed[:, cols].astype(jnp.float32) + read * weight
        gated[slot_at, index] = value
        square = value * value
        for lanes in range(0, width, 128):
            total = total + square[:, lanes : lanes + 128]
    return total


def read_kernel(parts, steps, offset, slots, place, after, *refs):
    states, own_work, (gated, squares) = refs[: len(steps)], refs[len(steps) : -2], refs[-2:]
    for slot in range(slots):
        squares[slot] = read_slot(
            parts, steps, offset, place[1], slot, states, own_work, gated, slot
        )


def finish_kernel(parts, groups, slots, place, live, gain, *refs):
    inputs, (out, gated, held, sems) = refs[:-4], refs[-4:]
    count = 2 * (len(groups) - 1)
    earlier, inputs = inputs[:count], inputs[count:]
    offset, steps = groups[-1]
    states, own_work = inputs[: len(steps)], inputs[len(steps) :]
    column = place[1]
    slots, rows, features = held.shape
    part_width = features // parts
    copies = []
    for slot in range(slots):
        total = read_slot(parts, steps, offset, column, slot, states, own_work, gated, 0)
        for group in range(len(groups) - 1):
            total = total + earlier[2 * group + 1][slot]
        scale = lax.rsqrt(jnp.sum(total, axis=1, keepdims=True) / features + EPS)
        alive = lax.broadcasted_iota(jnp.int32, (rows, 1), 0) < live[slot]
        scale = jnp.where(alive, scale, 0.0)
        size = rows // parts
        for block in range(parts):
            here = slice(block * size, (block + 1) * size)
            for group, (offset_here, steps_here) in enumerate(groups):
                last = group + 1 == len(groups)
                values = gated if last else earlier[2 * group]
                width = values.shape[-1]
                for index, step in enumerate(steps_here):
                    start = (column ^ step) * part_width + offset_here
                    cols = pl.ds(pl.multiple_of(start, 128), width)
                    gain_here = jnp.reshape(gain[cols], (1, width))
                    value = values[0 if last else slot, index, here]
                    held[slot, here, cols] = (value * scale[here] * gain_here).astype(jnp.bfloat16)
            copies.append(
                pltpu.make_async_copy(
                    held.at[slot, here], out.at[slot, here], sems.at[slot * parts + block]
                )
            )
            copies[-1].start()
    for copy in copies:
        copy.wait()


LASTS = dict(
    pack=2, prompt_weights=2, prompt_state=3, pick=1, merge=1, prepare=0, completion=4, read=2, finish=2
)


def matched(
    prompt_inner,
    prompt_proj,
    prompt_step,
    completion_inner,
    completion_gate,
    completion_projections,
    sample_step,
    sample_length,
    decay_log,
    conv_inner,
    conv_proj,
    norm_gain,
):
    parts = lax.axis_size("comp")
    row, column = lax.axis_index("prompt"), lax.axis_index("comp")
    plane, core = row // 2, row % 2
    group = 2 * column + core
    rows = prompt_inner.shape[0]
    heads = sample_step.shape[0]
    features = heads * HEAD_WIDTH
    place = jnp.stack([plane, column, core, row]).astype(jnp.int32)
    bf16, f32 = jnp.bfloat16, jnp.float32

    def take(array, start, size, axis):
        return lax.dynamic_slice_in_dim(array, start, size, axis)

    planes = lax.axis_size("prompt") // 2
    pair_width = 2 * STATE_WIDTH
    edge = jax.ShapeDtypeStruct((TAIL, pair_width), bf16)
    held_inner = pltpu.with_memory_space_constraint(prompt_inner, pltpu.HBM)
    held_proj = pltpu.with_memory_space_constraint(prompt_proj, pltpu.HBM)
    held_step = pltpu.with_memory_space_constraint(prompt_step, pltpu.HBM)

    swap, edge_1, own_b = run_whole(
        pack_kernel,
        "pack",
        (place,),
        (
            jax.ShapeDtypeStruct((rows + TAIL, pair_width), bf16),
            edge,
            jax.ShapeDtypeStruct((rows, STATE_WIDTH), bf16),
        ),
        (held_inner, held_proj, held_step),
        spaces=[pltpu.HBM] * 3,
        scratch=[
            pltpu.VMEM((heads, rows), f32),
            pltpu.VMEM((TAIL, 2 * features), bf16),
            pltpu.VMEM((TAIL, pair_width), bf16),
            pltpu.VMEM((TAIL, pair_width), bf16),
            pltpu.SemaphoreType.DMA((6,)),
        ],
    )
    trade = lambda z, k, c: (z, 1 - k, c)
    other = routed(swap, trade)
    other_inner = routed(prompt_inner, trade)
    slots, positions = completion_inner.shape[:2]
    wide = jax.ShapeDtypeStruct((positions, features), bf16)
    prepared = {}
    held_gate = pltpu.with_memory_space_constraint(completion_gate, pltpu.HBM)

    def prepare(slot, after, fetch):
        every = jax.ShapeDtypeStruct((heads, positions), f32)
        turned = jax.ShapeDtypeStruct((positions, heads), f32)
        return run_whole(
            lambda *refs: prepare_kernel(slot, fetch, *refs),
            "prepare",
            (place,),
            (wide, wide, every, turned, every, edge),
            (held_gate if fetch else completion_gate, sample_step, decay_log, after),
            spaces=[pltpu.HBM if fetch else pltpu.VMEM] + [pltpu.VMEM] * 3,
            scratch=[
                pltpu.VMEM((positions, features), bf16),
                pltpu.SemaphoreType.DMA((4,)),
            ]
            * fetch,
        )

    for slot in range(1, slots):
        *prepared[slot], edge_1 = prepare(slot, edge_1, True)
    edges = jnp.where(core == 0, other[rows:], edge_1)
    near = routed(edges, lambda z, k, c: (z + 1, k, c) if z + 1 < planes else None)
    far = routed(edges, lambda z, k, c: (c, k, c) if z + 1 == planes else None)
    weights, b_turned, logs, b_first = run_whole(
        prompt_weights_kernel,
        "prompt_weights",
        (place,),
        (
            jax.ShapeDtypeStruct((2 * rows, heads), f32),
            jax.ShapeDtypeStruct((STATE_WIDTH, 2 * rows), bf16),
            jax.ShapeDtypeStruct((8, heads * LOG_LANES), f32),
            jax.ShapeDtypeStruct((TAIL, STATE_WIDTH), bf16),
        ),
        (own_b, other, conv_proj, prompt_step, decay_log),
    )
    unit = features // parts // sum(CHUNKS)
    widths = [unit * size for size in CHUNKS]
    offsets = [sum(widths[:chunk]) for chunk in range(len(widths))]
    picks, holds = [], []
    for chunk, width in enumerate(widths):
        with_tail = chunk == 0
        message = jax.ShapeDtypeStruct((STATE_WIDTH + TAIL * with_tail, width), bf16)
        spread = jax.ShapeDtypeStruct((STATE_WIDTH + 2 * TAIL * with_tail, width), bf16)
        sent = run_whole(
            lambda *refs, offset=offsets[chunk]: prompt_state_kernel(offset, parts, *refs),
            "prompt_state",
            (place,),
            (spread,) * parts
            + (edge if chunk else jax.ShapeDtypeStruct((STATE_WIDTH, 2 * rows), bf16),),
            (
                prompt_inner, other_inner, near, conv_inner, conv_proj, weights, b_turned, b_first,
                logs, far,
            ),
        )
        if chunk == 0:
            b_turned = sent[parts]
        else:
            *prepared[0], handed = prepare(0, sent[parts], False)
        held = [sent[0]] + [
            routed(sent[step], lambda z, k, c: (z, k, c ^ step)) for step in range(1, parts)
        ]
        two = jax.ShapeDtypeStruct((parts // 2,) + message.shape, bf16)
        holds.append(held)
        picks.append(
            lambda after, held=held, two=two, with_tail=with_tail: run_whole(
                lambda *refs: pick_kernel(parts, *refs),
                "pick",
                (place,),
                (two,) + (two, edge) * with_tail,
                [after] + held,
                spaces=[pl.ANY] + [pltpu.VMEM] * parts,
            )
        )

    held_projections = pltpu.with_memory_space_constraint(completion_projections, pltpu.HBM)
    def completion(slot, after):
        gates, factor, *decays = prepared[slot]
        fixed, c = run_whole(
            lambda *refs: completion_kernel(slot, *refs),
            "completion",
            (place,),
            (wide, jax.ShapeDtypeStruct((positions, STATE_WIDTH), bf16)),
            (
                completion_inner, held_projections, tail, conv_inner, conv_proj, gates, *decays, after,
            ),
            spaces=[pltpu.VMEM, pltpu.HBM] + [pltpu.VMEM] * 7 + [pl.ANY],
            scratch=[
                pltpu.VMEM((positions, features), bf16),
                pltpu.VMEM((2, positions, STATE_WIDTH), bf16),
                pltpu.SemaphoreType.DMA((2,)),
            ],
        )
        return c, fixed, factor

    def merge(bit, chunk, own, came, shapes, given, after):
        table = jax.ShapeDtypeStruct((8, features // parts), f32)
        *outs, factors = run_whole(
            lambda *refs: (merge_kernel if len(own) == 1 else merge_held_kernel)(bit, chunk, *refs),
            "merge",
            (place,),
            shapes + (table,) * (chunk == 0),
            (*own, came, given, after),
            spaces=[pltpu.VMEM] * (len(own) + 1) + [pltpu.VMEM if chunk else pl.ANY, pl.ANY],
        ) + ((given,) if chunk else ())
        return outs, factors

    def gather(state):
        return [state] + [
            routed(state, lambda z, k, c: (z, k, c ^ step)) for step in range(1, parts)
        ]

    work = list(range(slots))
    finished = []

    def do_work(after):
        if not work:
            return after
        finished.append(completion(work.pop(0), after))
        return finished[-1][0]

    stays, goes, go_shapes, merged, joined = [], [], [], [], []
    near_plane = lambda z, k, c: (z ^ 1, k, c)
    far_plane = lambda z, k, c: (z ^ 2, k, c)
    tail, after = None, handed
    for chunk in range(len(widths)):
        go, *maybe = picks[chunk](after)
        tail = maybe[1] if maybe else tail
        stays.append(maybe[:1] or holds[chunk])
        goes.append(routed(go, near_plane))
        go_shapes.append(go.shape[1:])
        if chunk + 1 < len(widths):
            after = do_work(go)
    given = after = go
    for chunk in range(len(widths)):
        one = jax.ShapeDtypeStruct((1,) + go_shapes[chunk], bf16)
        (stay, go), given = merge(
            0, chunk, stays[chunk], goes[chunk], (one, one), given, after
        )
        merged.append((stay, routed(go, far_plane)))
        after = do_work(go)
    given = go
    for chunk, width in enumerate(widths):
        state = jax.ShapeDtypeStruct((STATE_WIDTH, width), bf16)
        (state,), given = merge(1, chunk, [merged[chunk][0]], merged[chunk][1], (state,), given, go)
        joined.append(gather(state))
    after = state
    while work:
        after = do_work(after)
    own_work = [array for three in finished for array in three]
    every = tuple(range(parts))
    groups = [(chunk, every) for chunk in range(len(widths) - 1)]
    groups.append((len(widths) - 1, every))
    earlier = []
    for chunk, steps in groups[:-1]:
        earlier += run_whole(
            lambda *refs, steps=steps, offset=offsets[chunk]: read_kernel(
                parts, steps, offset, slots, *refs
            ),
            "read",
            (place,),
            (
                jax.ShapeDtypeStruct((slots, len(steps), positions, widths[chunk]), f32),
                jax.ShapeDtypeStruct((slots, positions, 128), f32),
            ),
            [earlier[-1] if earlier else joined[chunk][0]]
            + [joined[chunk][step] for step in steps]
            + own_work,
            spaces=[pl.ANY] + [pltpu.VMEM] * (len(steps) + len(own_work)),
        )
    chunk, steps = groups[-1]
    groups = [(offsets[chunk], steps) for chunk, steps in groups]
    return run_whole(
        lambda *refs: finish_kernel(parts, groups, slots, *refs),
        "finish",
        (place, sample_length),
        jax.ShapeDtypeStruct((slots, positions, features), bf16),
        [norm_gain] + earlier + [joined[chunk][step] for step in steps] + own_work,
        out_spaces=pltpu.HBM,
        scratch=[
            pltpu.VMEM((1, len(steps), positions, widths[-1]), f32),
            pltpu.VMEM((slots, positions, features), bf16),
            pltpu.SemaphoreType.DMA((slots * parts,)),
        ],
    )


def run_whole(
    kernel, name, place, out_shape, operands, scratch=(), spaces=None, out_spaces=None, aliases=None
):
    vmem = pltpu.VMEM
    spaces = spaces or [vmem] * len(operands)
    out_spaces = out_spaces or jax.tree.map(lambda _: vmem, out_shape)
    return pl.pallas_call(
        kernel,
        out_shape=out_shape,
        in_specs=[pl.BlockSpec(memory_space=pltpu.SMEM)] * len(place)
        + [pl.BlockSpec(memory_space=space) for space in spaces],
        out_specs=jax.tree.map(lambda space: pl.BlockSpec(memory_space=space), out_spaces),
        scratch_shapes=scratch,
        input_output_aliases=aliases or {},
        compiler_params=pltpu.CompilerParams(vmem_limit_bytes=VMEM_BYTES),
        cost_estimate=pl.CostEstimate(
            flops=LASTS[name] * 10**9, transcendentals=0, bytes_accessed=LASTS[name] * 3 * 10**6
        ),
        name=name,
    )(*place, *operands)


def local(*arrays):
    columns, prompts = lax.axis_size("comp"), lax.axis_size("prompt")
    heads_col, heads_row = arrays[2].shape[0], arrays[6].shape[0]
    one_group = heads_row == STATE_HEADS // STATE_GROUPS and heads_col == 2 * heads_row
    if one_group and prompts == 2 * columns and columns & (columns - 1) == 0:
        return matched(*arrays)
    return any_shape(*arrays)


def solution(mesh):
    placed = (
        P("prompt", "comp"),
        P("prompt", None),
        P("comp", "prompt"),
        P("comp", None, "prompt"),
        P("comp", None, "prompt"),
        P("comp", None, None),
        P("prompt", "comp", None),
        P("comp"),
        P(),
        P(),
        P(),
        P("prompt"),
    )
    return jax.shard_map(
        local, mesh=mesh, in_specs=placed, out_specs=P("comp", None, "prompt"), check_vma=False
    )
```
